32 devices in a mesh: dp: 2 (over x), tensor: 4 (over y, core), bucket: 4 (over z).
Axes of the slice: x: 2, y: 2, z: 4, core: 2. Of those that a mesh axis runs over, the one named last changes fastest.
Arguments:
- tokens: bfloat16 [8192, 2048], P(('dp', 'bucket')), may hold values from -6 to 6
- cotangent: bfloat16 [8192, 2048], P(('dp', 'bucket')), may hold values from -6 to 6
- lengths: int32 [8, 3], P(('dp', 'bucket')), may hold values from 1 to 768, 1024 in all within a row
- head_quarters: int32 [8192], P(('dp', 'bucket')), may hold values from 1 to 4
- buckets: int32 [8192, 1], P(('dp', 'bucket')), may hold values from 0 to 3, as said below
- ln1_gain: float32 [2048], replicated, may hold values from 0.5 to 1.5
- ln1_bias: float32 [2048], replicated, may hold values from -1.2 to 1.2
- w_qkv: bfloat16 [2048, 3, 2048], P(None, None, 'tensor'), may hold values from -0.125 to 0.125
- w_out: bfloat16 [2048, 2048], P('tensor'), may hold values from -0.5 to 0.5
- ln2_gain: float32 [2048], replicated, may hold values from 0.5 to 1.5
- ln2_bias: float32 [2048], replicated, may hold values from -1.2 to 1.2
- w_router: bfloat16 [2048, 4], replicated, may hold values from -0.09375 to 0.09375
- w_up: bfloat16 [2048, 4, 2048], P(None, 'bucket', 'tensor'), may hold values from -0.125 to 0.125
- w_down: bfloat16 [4, 2048, 2048], P('bucket', 'tensor'), may hold values from -0.25 to 0.25
Outputs:
- mixed: bfloat16 [8192, 2048], P(('dp', 'bucket'))
- tokens_grad: float32 [8192, 2048], P(('dp', 'bucket'))
- ln1_gain_grad: float32 [2048], P(('dp', 'bucket'))
- ln1_bias_grad: float32 [2048], P(('dp', 'bucket'))
- w_qkv_grad: float32 [2048, 3, 2048], P(('dp', 'bucket'), None, 'tensor')
- w_out_grad: float32 [2048, 2048], P('tensor', ('dp', 'bucket'))
- ln2_gain_grad: float32 [2048], P(('dp', 'bucket'))
- ln2_bias_grad: float32 [2048], P(('dp', 'bucket'))
- w_router_grad: float32 [2048, 4], P(('dp', 'bucket'))
- w_up_grad: float32 [2048, 4, 2048], P('dp', 'bucket', 'tensor')
- w_down_grad: float32 [4, 2048, 2048], P('bucket', 'tensor', 'dp')
The draws below stay inside these ranges and needn't reach their ends.
Inputs may be any that keep to these rules, and one draw needn't show every extreme that they name: `lengths`: each row sums to 1024. `buckets`: a token uses the hidden units of levels 0 to its level.
All inputs are finite; a program needn't handle non-finite values.
Results may differ from the reference program's by a relative error of at most 0.018.
Values may be sent and summed in bfloat16 or wider, within the bound.
A program may use at most 320 MiB of HBM per device.

```python
import math
import jax
import jax.numpy as jnp
import numpy as np
from jax import lax

D = 2048
HEADS = 16
HEAD_DIM = 128
FF = 8192
LEVELS = 4
TOK_DEV = 1024
SEQS_DEV = 3
SEQ_MOST = 768
GROUPS = 8
TOKENS = 8192
FFQ = 2048
N_TENSOR = 4


def draw_buckets(key, part):
    key = jax.random.fold_in(key, 11)
    first_key, second_key = jax.random.split(key)
    first = jax.random.randint(first_key, (TOKENS, 1), 0, LEVELS)
    second = jax.random.randint(second_key, (TOKENS, 1), 0, LEVELS)
    return jnp.maximum(first, second).astype(jnp.int32)


def set_ends(array, key, smallest, high):
    dims = array.shape
    place = [jax.random.randint(jax.random.fold_in(key, axis), (), 0, dims[axis]) for axis in range(len(dims))]
    array = array.at[tuple(place)].set(smallest)
    longest = dims.index(max(dims))
    place[longest] = (place[longest] + 1) % dims[longest]
    return array.at[tuple(place)].set(high)


def shard_levels(own_key, extent, pieces, least, largest):
    level, own = 1.0, jax.random.fold_in(own_key, 6)
    for dim, shards_of in pieces:
        steps = jnp.exp(jax.random.uniform(jax.random.fold_in(own, dim), (shards_of,), jnp.float32, least / len(pieces), largest / len(pieces)))
        level = level * jnp.repeat(steps, extent[dim] // shards_of).reshape([-1 if axis == dim else 1 for axis in range(len(extent))])
    return level


def length_profile(count, total, limit, skew):
    portions = [(1 << 20) // math.isqrt(rank ** skew) + 1 for rank in range(2, count + 1)]
    spare, given = total - limit - (count - 1), [1] * (count - 1)
    while spare > 0:
        free = [i for i in range(count - 1) if given[i] < limit]
        whole, left = sum([portions[i] for i in free]), spare
        for i in free:
            extra = min(limit - given[i], max(1, left * portions[i] // whole), spare)
            given[i] = given[i] + extra
            spare = spare - extra
    return np.array([limit] + given)


def ragged(key, number_of, total, reach, lean):
    if number_of == 2:
        one = jax.random.randint(key, (), max(1, total - reach), min(reach, total - 1) + 1)
        return jnp.stack([one, total - one])
    sizes = jnp.asarray(length_profile(number_of, total, reach, lean), jnp.int32)
    pairs = (number_of - 1) // 2
    giver, sink = sizes[1:1 + 2 * pairs:2], sizes[2:2 + 2 * pairs:2]
    slack = jnp.minimum(giver - 1, reach - sink)
    moved = jax.random.randint(jax.random.fold_in(key, 1), (pairs,), 0, 1 << 20) % (slack + 1)
    sizes = sizes.at[1:1 + 2 * pairs:2].set(giver - moved).at[2:2 + 2 * pairs:2].set(sink + moved)
    return sizes[jax.random.permutation(jax.random.fold_in(key, 2), number_of)]


def noise(own_key, shape, spread, reach, shards=(), kind=jnp.bfloat16):
    result = jax.random.normal(own_key, shape, jnp.float32) * spread
    if len(shards) > 0:
        result = shard_levels(own_key, shape, shards, -0.22, 0.18) * result
    return jnp.clip(result, min=-reach, max=reach).astype(kind)


def setup_inputs(seed: int = 0) -> dict:
    seeds = jax.random.split(jax.random.key(seed), 15)
    tokens = noise(seeds[0], (TOKENS, D), 1.0, 6.0, ((0, 8),))
    cotangent = noise(seeds[1], (TOKENS, D), 1.0, 6.0, ((0, 8),))
    lengths = jax.vmap(lambda own: ragged(own, SEQS_DEV, TOK_DEV, SEQ_MOST, 2))(jax.random.split(seeds[2], GROUPS)).reshape((GROUPS, SEQS_DEV)).astype(jnp.int32)
    head_quarters = set_ends(jax.random.randint(seeds[3], (TOKENS,), 1, LEVELS + 1), jax.random.fold_in(seeds[3], 1), 1, LEVELS).astype(jnp.int32)
    buckets = draw_buckets(jax.random.fold_in(seeds[14], 71), 0)
    ln1_gain = jnp.clip(1.0 + 0.1 * jax.random.normal(seeds[5], (D,), jnp.float32), 0.5, 1.5)
    ln1_bias = noise(seeds[6], (D,), 0.2, 1.2, (), jnp.float32)
    w_qkv = noise(seeds[7], (D, 3, D), D ** -0.5, 0.125, ((2, 4),))
    w_out = noise(seeds[8], (D, D), (D // 16) ** -0.5, 0.5, ((0, 4),))
    ln2_gain = jnp.clip(1.0 + 0.1 * jax.random.normal(seeds[9], (D,), jnp.float32), 0.5, 1.5)
    ln2_bias = noise(seeds[10], (D,), 0.2, 1.2, (), jnp.float32)
    w_router = noise(seeds[11], (D, LEVELS), (2 * D) ** -0.5, 0.09375)
    w_up = noise(seeds[12], (D, LEVELS, FFQ), D ** -0.5, 0.125, ((1, 4), (2, 4)))
    w_down = noise(seeds[13], (LEVELS, FFQ, D), (FF // 16) ** -0.5, 0.25, ((0, 4), (1, 4)))
    return {"tokens": tokens, "cotangent": cotangent, "lengths": lengths, "head_quarters": head_quarters, "buckets": buckets, "ln1_gain": ln1_gain, "ln1_bias": ln1_bias, "w_qkv": w_qkv, "w_out": w_out, "ln2_gain": ln2_gain, "ln2_bias": ln2_bias, "w_router": w_router, "w_up": w_up, "w_down": w_down}


EPS = 1e-05
HIGH = lax.Precision.HIGHEST
NEGATIVE = -1e+30

@jax.custom_vjp
def low(v):
    return lax.optimization_barrier(v.astype(jnp.bfloat16)).astype(jnp.float32)

@jax.custom_vjp
def low_back(v):
    return v

def low_keep(v):
    return (low(v), None)

def low_pass(kept, grad):
    return (grad,)

def back_keep(v):
    return (v, None)

def back_low(kept, grad):
    return (low(grad),)
low.defvjp(low_keep, low_pass)
low_back.defvjp(back_keep, back_low)

def product(left, right):
    return jnp.dot(left, right, precision=HIGH, preferred_element_type=jnp.float32)

def layer_norm(values, gain, shift):
    centred = values - lax.optimization_barrier(jnp.mean(values, -1, keepdims=True))
    return centred * lax.rsqrt(lax.optimization_barrier(jnp.mean(centred * centred, -1, keepdims=True)) + EPS) * gain + shift

def softmax(scores):
    row_max = lax.optimization_barrier(jnp.max(scores, -1, keepdims=True))
    expo = jnp.exp(scores - row_max)
    return expo / lax.optimization_barrier(jnp.sum(expo, -1, keepdims=True))

def layout(lengths_row, tok_rows):
    ends = jnp.cumsum(lengths_row).astype(jnp.int32)
    starts = ends - lengths_row
    tok_index = jnp.arange(tok_rows, dtype=jnp.int32)
    segments = lax.optimization_barrier(jnp.sum((tok_index[:, None] >= ends[None, :]).astype(jnp.int32), 1))
    chosen = segments[:, None] == jnp.arange(lengths_row.shape[0], dtype=jnp.int32)[None, :]
    positions = tok_index - lax.optimization_barrier(jnp.sum(jnp.where(chosen, starts[None, :], 0), 1)).astype(jnp.int32)
    return (positions, segments)

def tables(positions):
    half_dim = HEAD_DIM // 2
    freq = jnp.exp(jnp.arange(half_dim, dtype=jnp.float32) * (-math.log(10000.0) / half_dim))
    angle = positions.astype(jnp.float32)[:, None] * freq[None, :]
    return (jnp.cos(angle)[:, None, :], jnp.sin(angle)[:, None, :])

def rotate(values, cosine, sine):
    half_dim = values.shape[-1] // 2
    first_half, second_half = (values[..., :half_dim], values[..., half_dim:])
    return jnp.concatenate([first_half * cosine - second_half * sine, second_half * cosine + first_half * sine], -1)

def block_forward(inputs, params, positions, segments, head_keep, unit_keep, onehot):
    ln1_gain, ln1_bias, w_qkv, w_out, ln2_gain, ln2_bias, w_router, w_up, w_down = params
    tok_rows = inputs.shape[0]
    normed1 = low(layer_norm(inputs, ln1_gain, ln1_bias))
    projected = low_back(product(normed1, w_qkv.reshape(D, 3 * D))).reshape(tok_rows, 3, HEADS, HEAD_DIM)
    cosine, sine = tables(positions)
    queries = low_back(low(rotate(projected[:, 0], cosine, sine)))
    key_heads = low_back(low(rotate(projected[:, 1], cosine, sine)))
    value_heads = low(projected[:, 2])
    scores = low_back(jnp.einsum('qhd,khd->hqk', queries, key_heads, precision=HIGH) * HEAD_DIM ** (-0.5))
    tok_index = jnp.arange(tok_rows, dtype=jnp.int32)
    allowed = (segments[:, None] == segments[None, :]) & (tok_index[None, :] <= tok_index[:, None])
    scores = jnp.where(allowed[None], scores, NEGATIVE)
    weights = low(softmax(scores))
    heads_out = jnp.einsum('hqk,khd->qhd', weights, value_heads, precision=HIGH)
    heads_out = low_back(low(heads_out * head_keep[:, :, None])).reshape(tok_rows, D)
    attention = low_back(product(heads_out, w_out))
    middle = inputs + attention
    normed2 = low(layer_norm(middle, ln2_gain, ln2_bias))
    gate_tok = lax.optimization_barrier(jnp.sum(softmax(product(normed2, w_router)) * onehot, -1))
    up_act = low_back(product(low_back(normed2), w_up.reshape(D, FF)))
    hidden = low(jnp.square(jnp.maximum(up_act, 0.0)) * unit_keep)
    branch = low_back(low(product(hidden, w_down.reshape(FF, D))))
    return middle + gate_tok[:, None] * branch

def reference(tokens, cotangent, lengths, head_quarters, buckets, ln1_gain, ln1_bias, w_qkv, w_out, ln2_gain, ln2_bias, w_router, w_up, w_down):
    params = tuple((item.astype(jnp.float32) for item in (ln1_gain, ln1_bias, w_qkv, w_out, ln2_gain, ln2_bias, w_router, w_up, w_down)))
    groups = TOKENS // TOK_DEV
    inputs_all = tokens.astype(jnp.float32).reshape(groups, TOK_DEV, D)
    grads_all = cotangent.astype(jnp.float32).reshape(groups, TOK_DEV, D)
    quarters_all = head_quarters.reshape(groups, TOK_DEV)
    levels_all = buckets[:, 0].reshape(groups, TOK_DEV)

    def add_up(left, right):
        return left + right

    def one_group(totals, group_item):
        inputs, grad_out, lengths_row, quarters, levels = group_item
        positions, segments = layout(lengths_row, TOK_DEV)
        head_group = jnp.arange(HEADS, dtype=jnp.int32) * N_TENSOR // HEADS
        head_keep = (head_group[None, :] < quarters[:, None]).astype(jnp.float32)
        unit_keep = (jnp.arange(FF, dtype=jnp.int32)[None, :] // FFQ <= levels[:, None]).astype(jnp.float32)
        onehot = (jnp.arange(LEVELS, dtype=jnp.int32)[None, :] == levels[:, None]).astype(jnp.float32)

        def forward(values, weights):
            return block_forward(values, weights, positions, segments, head_keep, unit_keep, onehot)
        output, pullback = jax.vjp(forward, inputs, params)
        grad_inputs, grad_params = pullback(grad_out)
        totals = jax.tree.map(add_up, totals, grad_params)
        return (totals, (output.astype(jnp.bfloat16), grad_inputs))
    start = jax.tree.map(jnp.zeros_like, params)
    totals, (outputs, grad_inputs) = lax.scan(one_group, start, (inputs_all, grads_all, lengths, quarters_all, levels_all))
    return (outputs.reshape(TOKENS, D), grad_inputs.reshape(TOKENS, D), totals[0], totals[1], totals[2], totals[3], totals[4], totals[5], totals[6], totals[7], totals[8])
```

```python
import functools
import math

import jax
import jax.numpy as jnp
from jax import lax
from jax.experimental import pallas as pl
from jax.experimental.pallas import tpu as pltpu
from jax.sharding import PartitionSpec as P

HEAD_DIM = 128
QBLOCK = 256
EPS = 1e-05
HIGH = lax.Precision.HIGHEST
NEGATIVE = -1e30
F32 = jnp.float32
BF16 = jnp.bfloat16


def norm_parts(values):
    centred = values - jnp.mean(values, -1, keepdims=True)
    inverse = lax.rsqrt(jnp.mean(centred * centred, -1, keepdims=True) + EPS)
    return centred * inverse, inverse


def norm_backward(grad_in, normed, inverse, gain):
    scaled = grad_in * gain
    inner = (
        scaled
        - jnp.mean(scaled, -1, keepdims=True)
        - normed * jnp.mean(scaled * normed, -1, keepdims=True)
    )
    return inverse * inner, jnp.sum(grad_in * normed, 0), jnp.sum(grad_in, 0)


def softmax(scores):
    expo = jnp.exp(scores - jnp.max(scores, -1, keepdims=True))
    return expo / jnp.sum(expo, -1, keepdims=True)


def layout(lengths_row, tok_rows):
    ends = jnp.cumsum(lengths_row)
    starts = ends - lengths_row
    tok_index = jnp.arange(tok_rows, dtype=jnp.int32)
    segments = jnp.sum((tok_index[:, None] >= ends[None, :]).astype(jnp.int32), 1)
    chosen = segments[:, None] == jnp.arange(lengths_row.shape[0], dtype=jnp.int32)[None, :]
    first = jnp.sum(jnp.where(chosen, starts[None, :], 0), 1)
    return tok_index - first, first


def tables(positions):
    half_dim = HEAD_DIM // 2
    freq = jnp.exp(jnp.arange(half_dim, dtype=F32) * (-math.log(10000.0) / half_dim))
    angle = positions.astype(F32)[:, None] * freq[None, :]
    cosine, sine = jnp.cos(angle), jnp.sin(angle)
    return jnp.concatenate([cosine, cosine], -1), jnp.concatenate([-sine, sine], -1)


def dot(left, right, dims):
    return lax.dot_general(left, right, (dims, ((), ())), preferred_element_type=F32)


NN = ((1,), (0,))
NT = ((1,), (1,))
TN = ((0,), (0,))


def qkv_kernel(x_ref, gain_ref, bias_ref, w_ref, cos_ref, sin_ref, n_ref, q_ref, k_ref, v_ref):
    values = x_ref[...].astype(F32)
    normed, _ = norm_parts(values)
    low = (normed * gain_ref[...] + bias_ref[...]).astype(BF16)
    n_ref[...] = low
    cosine, sine = cos_ref[...], sin_ref[...]
    width = w_ref.shape[2]
    for part, out_ref in enumerate((q_ref, k_ref, v_ref)):
        projected = dot(low, w_ref[part], NN)
        if part == 2:
            out_ref[...] = projected.astype(BF16)
            continue
        for at in range(0, width, HEAD_DIM):
            head = projected[:, at : at + HEAD_DIM]
            turned = head * cosine + pltpu.roll(head, HEAD_DIM // 2, 1) * sine
            out_ref[:, at : at + HEAD_DIM] = turned.astype(BF16)


def qkv_call(tokens, gain, bias, w3, cosine, sine):
    rows, width = tokens.shape
    own = w3.shape[2]
    wide = pl.BlockSpec((QBLOCK, width), lambda i: (i, 0))
    row = pl.BlockSpec((1, width), lambda i: (0, 0))
    table = pl.BlockSpec((QBLOCK, HEAD_DIM), lambda i: (i, 0))
    out = pl.BlockSpec((QBLOCK, own), lambda i: (i, 0))
    return pl.pallas_call(
        qkv_kernel,
        grid=(rows // QBLOCK,),
        in_specs=[wide, row, row, pl.BlockSpec(w3.shape, lambda i: (0, 0, 0)), table, table],
        out_specs=[wide, out, out, out],
        out_shape=[jax.ShapeDtypeStruct((rows, width), BF16)]
        + [jax.ShapeDtypeStruct((rows, own), BF16)] * 3,
        compiler_params=pltpu.CompilerParams(vmem_limit_bytes=40 << 20),
        cost_estimate=pl.CostEstimate(
            flops=6 * rows * width * own, bytes_accessed=2 * (2 * rows * width + 3 * width * own + 3 * rows * own), transcendentals=0
        ),
        name="qkv",
    )(tokens, gain.reshape(1, -1), bias.reshape(1, -1), w3, cosine, sine)


def masked_scores(query, keys, first, block, length):
    scores = dot(query, keys, NT) * HEAD_DIM**-0.5
    key_at = lax.broadcasted_iota(jnp.int32, (QBLOCK, length), 1)
    row_at = lax.broadcasted_iota(jnp.int32, (QBLOCK, length), 0) + block * QBLOCK
    allowed = (key_at >= first) & (key_at <= row_at)
    return jnp.where(allowed, scores, NEGATIVE)


def attend_kernel(q_ref, k_ref, v_ref, first_ref, keep_ref, o_ref, log_ref):
    for block in range(pl.num_programs(1)):

        @pl.when(pl.program_id(1) == block)
        def _():
            length = (block + 1) * QBLOCK
            scores = masked_scores(q_ref[...], k_ref[:length], first_ref[...], block, length)
            most = jnp.max(scores, -1, keepdims=True)
            expo = jnp.exp(scores - most)
            total = jnp.sum(expo, -1, keepdims=True)
            weights = (expo * (1.0 / total)).astype(BF16)
            out = dot(weights, v_ref[:length], NN)
            o_ref[...] = (out * keep_ref[...]).astype(BF16)
            log_ref[0] = most + jnp.log(total)


def attend_call(queries, keys, values, first, keep):
    rows, own = queries.shape
    heads, blocks = own // HEAD_DIM, rows // QBLOCK
    part = pl.BlockSpec((QBLOCK, HEAD_DIM), lambda h, i: (i, h))
    whole = pl.BlockSpec((rows, HEAD_DIM), lambda h, i: (0, h))
    column = pl.BlockSpec((QBLOCK, 1), lambda h, i: (i, 0))
    return pl.pallas_call(
        attend_kernel,
        grid=(heads, blocks),
        in_specs=[part, whole, whole, column, column],
        out_specs=[part, pl.BlockSpec((1, QBLOCK, 1), lambda h, i: (h, i, 0))],
        out_shape=[
            jax.ShapeDtypeStruct((rows, own), BF16),
            jax.ShapeDtypeStruct((heads, rows, 1), F32),
        ],
        compiler_params=pltpu.CompilerParams(vmem_limit_bytes=40 << 20),
        cost_estimate=pl.CostEstimate(
            flops=4 * rows * rows * own, bytes_accessed=8 * rows * own, transcendentals=heads * rows * rows
        ),
        name="attend",
    )(queries, keys, values, first, keep)


def attend_back_kernel(
    q_ref, k_ref, v_ref, go_ref, first_ref, log_ref, cos_ref, sin_ref, g_ref, dk_ref, dv_ref
):
    head, step = pl.program_id(0), pl.program_id(1)
    blocks = pl.num_programs(1)
    own = q_ref.shape[1] * pl.num_programs(0)

    @pl.when(step == 0)
    def _():
        dk_ref[...] = jnp.zeros_like(dk_ref)
        dv_ref[...] = jnp.zeros_like(dv_ref)

    def place(part):
        return pl.ds(pl.multiple_of(part * own + head * HEAD_DIM, HEAD_DIM), HEAD_DIM)

    def turn_back(grad, rows):
        grad = grad.astype(BF16).astype(F32)
        back = grad * cos_ref[rows] - pltpu.roll(grad, HEAD_DIM // 2, 1) * sin_ref[rows]
        return back.astype(BF16)

    for block in range(blocks):

        @pl.when(step == block)
        def _():
            length = (block + 1) * QBLOCK
            rows = slice(block * QBLOCK, length)
            query, keys, grad = q_ref[...], k_ref[:length], go_ref[...]
            scores = masked_scores(query, keys, first_ref[...], block, length)
            probs = jnp.exp(scores - log_ref[0])
            grad_probs = dot(grad, v_ref[:length], NT)
            inner = jnp.sum(probs * grad_probs, -1, keepdims=True)
            grad_scores = (probs * (grad_probs - inner)).astype(BF16)
            dq = dot(grad_scores, keys, NN) * HEAD_DIM**-0.5
            g_ref[rows, place(0)] = turn_back(dq, rows)
            dk_ref[:length] += dot(grad_scores, query, TN)
            dv_ref[:length] += dot(probs.astype(BF16), grad, TN)

    @pl.when(step == blocks - 1)
    def _():
        g_ref[:, place(1)] = turn_back(dk_ref[...] * HEAD_DIM**-0.5, slice(None))
        g_ref[:, place(2)] = dv_ref[...].astype(BF16)


def attend_back_call(queries, keys, values, grads, first, logs, cosine, sine):
    rows, own = queries.shape
    heads, blocks = own // HEAD_DIM, rows // QBLOCK
    part = pl.BlockSpec((QBLOCK, HEAD_DIM), lambda h, i: (i, h))
    whole = pl.BlockSpec((rows, HEAD_DIM), lambda h, i: (0, h))
    column = pl.BlockSpec((QBLOCK, 1), lambda h, i: (i, 0))
    table = pl.BlockSpec((rows, HEAD_DIM), lambda h, i: (0, 0))
    return pl.pallas_call(
        attend_back_kernel,
        grid=(heads, blocks),
        in_specs=[
            part,
            whole,
            whole,
            part,
            column,
            pl.BlockSpec((1, QBLOCK, 1), lambda h, i: (h, i, 0)),
            table,
            table,
        ],
        out_specs=pl.BlockSpec((rows, 3 * own), lambda h, i: (0, 0)),
        out_shape=jax.ShapeDtypeStruct((rows, 3 * own), BF16),
        scratch_shapes=[pltpu.VMEM((rows, HEAD_DIM), F32)] * 2,
        compiler_params=pltpu.CompilerParams(vmem_limit_bytes=40 << 20),
        cost_estimate=pl.CostEstimate(
            flops=10 * rows * rows * own, bytes_accessed=14 * rows * own, transcendentals=heads * rows * rows
        ),
        name="attend_back",
    )(queries, keys, values, grads, first, logs, cosine, sine)


def qkv_back_kernel(g_ref, w_ref, o_ref):
    own = w_ref.shape[2]
    total = dot(g_ref[:, :own], w_ref[0], NT)
    total += dot(g_ref[:, own : 2 * own], w_ref[1], NT)
    total += dot(g_ref[:, 2 * own :], w_ref[2], NT)
    o_ref[...] = total.astype(BF16)


def qkv_back_call(grads, w3):
    rows = grads.shape[0]
    width, own = w3.shape[1], w3.shape[2]
    return pl.pallas_call(
        qkv_back_kernel,
        grid=(rows // QBLOCK,),
        in_specs=[
            pl.BlockSpec((QBLOCK, 3 * own), lambda i: (i, 0)),
            pl.BlockSpec(w3.shape, lambda i: (0, 0, 0)),
        ],
        out_specs=pl.BlockSpec((QBLOCK, width), lambda i: (i, 0)),
        out_shape=jax.ShapeDtypeStruct((rows, width), BF16),
        compiler_params=pltpu.CompilerParams(vmem_limit_bytes=40 << 20),
        cost_estimate=pl.CostEstimate(
            flops=6 * rows * width * own, bytes_accessed=2 * (rows * width + 3 * width * own + 3 * rows * own), transcendentals=0
        ),
        name="qkv_back",
    )(grads, w3)


def swap(values, axis, bit):
    pairs = [(i, i ^ bit) for i in range(lax.axis_size(axis))]
    return lax.ppermute(values, axis, pairs)


def local(
    tokens,
    cotangent,
    lengths,
    head_quarters,
    buckets,
    ln1_gain,
    ln1_bias,
    w_qkv,
    w_out,
    ln2_gain,
    ln2_bias,
    w_router,
    w_up,
    w_down,
):
    tok_rows, model_width = tokens.shape
    owners = lax.axis_size("bucket")
    splits = lax.axis_size("tensor")
    copies = lax.axis_size("dp")
    share = tok_rows // splits
    t, z, x = lax.axis_index("tensor"), lax.axis_index("bucket"), lax.axis_index("dp")
    up_own = w_up.reshape(model_width, -1)
    down_own = w_down.reshape(-1, model_width)
    hidden_width = up_own.shape[1]

    def fetch(weights):
        rows = weights.shape[0] // copies
        piece = swap(lax.dynamic_slice_in_dim(weights, x * rows, rows, 0), "bucket", 2)
        return lax.all_gather(piece, "dp", axis=0, tiled=True)

    up_other, down_other = fetch(up_own), fetch(down_own)
    levels = buckets[:, 0].astype(F32).reshape(-1, HEAD_DIM)
    near_levels = swap(levels, "bucket", 1)
    near_cotangent = swap(cotangent, "bucket", 1)

    def shard(values, bit):
        return lax.dynamic_slice_in_dim(values, (t ^ bit) * share, share, 0)

    ORDER = (0, 2, 1, 3)

    def arranged(values):
        return jnp.concatenate([shard(values, bit) for bit in ORDER], 0)

    inputs = tokens.astype(F32)
    positions, first = layout(lengths[0], tok_rows)
    first = first[:, None]
    keep = (t < head_quarters).astype(F32)[:, None]
    cosine, sine = tables(positions)
    w3 = jnp.transpose(w_qkv, (1, 0, 2))
    normed1, queries, keys, values = qkv_call(tokens, ln1_gain, ln1_bias, w3, cosine, sine)
    heads_low, logs = attend_call(queries, keys, values, first, keep)

    def gather_sum(away, kept):
        both = kept + swap(away.astype(BF16), "tensor", 1).astype(F32)
        half = both.shape[0] // 2
        return both[:half] + swap(both[half:].astype(BF16), "tensor", 2).astype(F32)

    def spread(piece):
        both = jnp.concatenate([piece, swap(piece, "tensor", 2)], 0)
        return jnp.concatenate([both, swap(both, "tensor", 1)], 0)

    def natural(piece, dtype):
        whole = jnp.zeros((tok_rows, model_width), dtype)
        for at, bit in enumerate(ORDER):
            part = lax.slice_in_dim(piece, at * share, (at + 1) * share).astype(dtype)
            whole = lax.dynamic_update_slice_in_dim(whole, part, (t ^ bit) * share, 0)
        return whole

    heads_kept = jnp.concatenate([shard(heads_low, 0), shard(heads_low, 2)], 0)
    heads_away = jnp.concatenate([shard(heads_low, 1), shard(heads_low, 3)], 0)
    attention = gather_sum(dot(heads_away, w_out, NN).astype(BF16), dot(heads_kept, w_out, NN))
    inputs_own = shard(tokens, 0).astype(F32)
    middle = inputs_own + attention
    hat2, inverse2 = norm_parts(middle)
    normed2 = (hat2 * ln2_gain + ln2_bias).astype(BF16)

    near = swap(normed2, "bucket", 1)
    n2 = jnp.concatenate([spread(normed2), spread(near)], 0)

    def gate_of(rows, tok_levels):
        probs = softmax(dot(rows, w_router, NN))
        onehot = (tok_levels[:, None] == jnp.arange(owners, dtype=F32)[None, :]).astype(F32)
        return jnp.sum(probs * onehot, -1), probs, onehot

    level_all = jnp.concatenate(
        [arranged(levels.reshape(-1)), arranged(near_levels.reshape(-1))], 0
    )
    gate_all, _, _ = gate_of(n2, level_all)
    grad_all = jnp.concatenate([arranged(cotangent), arranged(near_cotangent)], 0)
    grad_branch = (gate_all[:, None] * grad_all.astype(F32)).astype(BF16)
    kept_own = (level_all >= z.astype(F32))[:, None]
    kept_other = (level_all >= (z ^ 2).astype(F32))[:, None]

    def forward(up, kept):
        act = jnp.where(kept, jnp.maximum(dot(n2, up, NN), 0.0), 0.0)
        return act.astype(BF16), jnp.square(act).astype(BF16)

    act_own, hid_own = forward(up_own, kept_own)
    act_other, hid_other = forward(up_other, kept_other)
    parts = 2 * splits

    def scatter_sum(total):
        blocks = total.astype(BF16).reshape(2, 2, 2, share, model_width)
        kept, away = blocks[:, 0], blocks[:, 1]
        both = kept.astype(F32) + swap(away, "tensor", 1).astype(F32)
        one = both[:, 0] + swap(both[:, 1].astype(BF16), "tensor", 2).astype(F32)
        return one[0] + swap(one[1].astype(BF16), "bucket", 1).astype(F32)

    branch_sum = scatter_sum(dot(hid_own, down_own, NN) + dot(hid_other, down_other, NN))

    def backward(act, down):
        grad = dot(grad_branch, down, NT)
        return (grad * 2.0 * act.astype(F32)).astype(BF16)

    gu_own, gu_other = backward(act_own, down_own), backward(act_other, down_other)
    returned = scatter_sum(dot(gu_own, up_own, NT) + dot(gu_other, up_other, NT))

    def reduce_dp(grad, dim):
        return lax.psum_scatter(grad.astype(BF16), "dp", scatter_dimension=dim, tiled=True)

    def owner_sum(own, other):
        return own.astype(F32) + swap(other, "bucket", 2).astype(F32)

    grad_down = owner_sum(
        reduce_dp(dot(grad_branch, hid_own, TN), 0), reduce_dp(dot(grad_branch, hid_other, TN), 0)
    ).T
    grad_up = owner_sum(
        reduce_dp(dot(n2, gu_own, TN), 0), reduce_dp(dot(n2, gu_other, TN), 0)
    )

    branch = branch_sum.astype(BF16).astype(F32)
    level_own = shard(levels.reshape(-1), 0)
    gate, probs, onehot = gate_of(normed2, level_own)
    mixed_own = (middle + gate[:, None] * branch).astype(BF16)
    mixed = natural(spread(mixed_own), BF16)
    grad_output = shard(cotangent, 0).astype(F32)
    grad_gate = jnp.sum(grad_output * branch, -1)
    grad_logits = (grad_gate * gate)[:, None] * (onehot - probs)
    grad_router = dot(normed2.astype(F32), grad_logits, TN)
    grad_norm2 = returned.astype(BF16).astype(F32) + dot(grad_logits, w_router.astype(F32), NT)
    grad_in2, grad_ln2_gain, grad_ln2_bias = norm_backward(grad_norm2, hat2, inverse2, ln2_gain)
    grad_middle = grad_output + grad_in2
    grad_attention = natural(spread(grad_middle.astype(BF16)), BF16)

    def reduce_all(grad):
        return lax.psum_scatter(
            grad.astype(BF16), ("dp", "bucket"), scatter_dimension=0, tiled=True
        ).astype(F32)

    grad_w_out = reduce_all(dot(grad_attention, heads_low, TN)).T
    grad_heads = (dot(grad_attention, w_out, NT).astype(BF16).astype(F32) * keep).astype(BF16)
    grad_projected = attend_back_call(
        queries, keys, values, grad_heads, first, logs, cosine, sine
    )
    partial = qkv_back_call(grad_projected, w3)
    grad_w_qkv = reduce_all(dot(normed1, grad_projected, TN)).reshape(-1, 3, w3.shape[2])
    away = jnp.concatenate([shard(partial, 1), shard(partial, 3)], 0)
    kept = jnp.concatenate([shard(partial, 0), shard(partial, 2)], 0).astype(F32)
    grad_norm1 = gather_sum(away, kept)
    hat1, inverse1 = norm_parts(inputs_own)
    grad_in1, grad_ln1_gain, grad_ln1_bias = norm_backward(grad_norm1, hat1, inverse1, ln1_gain)
    tokens_grad = natural(spread((grad_middle + grad_in1).astype(BF16)), F32)

    def reduce_small(*grads):
        stacked = jnp.stack(grads, 0)
        total = lax.psum(stacked, ("dp", "tensor", "bucket"))
        width = model_width // (copies * owners)
        return lax.dynamic_slice_in_dim(total, (x * owners + z) * width, width, 1)

    small = reduce_small(grad_ln2_gain, grad_ln2_bias, *(grad_router[:, i] for i in range(owners)))
    last = reduce_small(grad_ln1_gain, grad_ln1_bias)
    return (
        mixed,
        tokens_grad,
        last[0],
        last[1],
        grad_w_qkv,
        grad_w_out,
        small[0],
        small[1],
        small[2:].T,
        grad_up.reshape(-1, 1, hidden_width),
        grad_down.reshape(1, hidden_width, -1),
    )


def solution(mesh):
    placed = (
        P(("dp", "bucket"), None),
        P(("dp", "bucket"), None),
        P(("dp", "bucket"), None),
        P(("dp", "bucket")),
        P(("dp", "bucket"), None),
        P(),
        P(),
        P(None, None, "tensor"),
        P("tensor", None),
        P(),
        P(),
        P(),
        P(None, "bucket", "tensor"),
        P("bucket", "tensor", None),
    )
    return jax.shard_map(
        local,
        mesh=mesh,
        in_specs=placed,
        out_specs=(
            P(("dp", "bucket"), None),
            P(("dp", "bucket"), None),
            P(("dp", "bucket")),
            P(("dp", "bucket")),
            P(("dp", "bucket"), None, "tensor"),
            P("tensor", ("dp", "bucket")),
            P(("dp", "bucket")),
            P(("dp", "bucket")),
            P(("dp", "bucket"), None),
            P("dp", "bucket", "tensor"),
            P("bucket", "tensor", "dp"),
        ),
        check_vma=False,
    )
```

```python
import functools
import math

import jax
import jax.numpy as jnp
from jax import lax
from jax.experimental import pallas as pl
from jax.experimental.pallas import tpu as pltpu
from jax.sharding import PartitionSpec as P

HEAD_DIM = 128
QBLOCK = 256
EPS = 1e-05
HIGH = lax.Precision.HIGHEST
NEGATIVE = -1e30
F32 = jnp.float32
BF16 = jnp.bfloat16


def norm_parts(values):
    centred = values - jnp.mean(values, -1, keepdims=True)
    inverse = lax.rsqrt(jnp.mean(centred * centred, -1, keepdims=True) + EPS)
    return centred * inverse, inverse


def norm_backward(grad_in, normed, inverse, gain):
    scaled = grad_in * gain
    inner = (
        scaled
        - jnp.mean(scaled, -1, keepdims=True)
        - normed * jnp.mean(scaled * normed, -1, keepdims=True)
    )
    return inverse * inner, jnp.sum(grad_in * normed, 0), jnp.sum(grad_in, 0)


def softmax(scores):
    expo = jnp.exp(scores - jnp.max(scores, -1, keepdims=True))
    return expo / jnp.sum(expo, -1, keepdims=True)


def layout(lengths_row, tok_rows):
    ends = jnp.cumsum(lengths_row)
    starts = ends - lengths_row
    tok_index = jnp.arange(tok_rows, dtype=jnp.int32)
    segments = jnp.sum((tok_index[:, None] >= ends[None, :]).astype(jnp.int32), 1)
    chosen = segments[:, None] == jnp.arange(lengths_row.shape[0], dtype=jnp.int32)[None, :]
    first = jnp.sum(jnp.where(chosen, starts[None, :], 0), 1)
    return tok_index - first, first


def tables(positions):
    half_dim = HEAD_DIM // 2
    freq = jnp.exp(jnp.arange(half_dim, dtype=F32) * (-math.log(10000.0) / half_dim))
    angle = positions.astype(F32)[:, None] * freq[None, :]
    cosine, sine = jnp.cos(angle), jnp.sin(angle)
    return jnp.concatenate([cosine, cosine], -1), jnp.concatenate([-sine, sine], -1)


def dot(left, right, dims):
    return lax.dot_general(left, right, (dims, ((), ())), preferred_element_type=F32)


NN = ((1,), (0,))
NT = ((1,), (1,))
TN = ((0,), (0,))


def masked_scores(query, keys, first, block, length):
    scores = dot(query, keys, NT) * HEAD_DIM**-0.5
    key_at = lax.broadcasted_iota(jnp.int32, (QBLOCK, length), 1)
    row_at = lax.broadcasted_iota(jnp.int32, (QBLOCK, length), 0) + block * QBLOCK
    allowed = (key_at >= first) & (key_at <= row_at)
    return jnp.where(allowed, scores, NEGATIVE)


def attend_back_kernel(
    q_ref, k_ref, v_ref, go_ref, first_ref, log_ref, cos_ref, sin_ref, g_ref, dk_ref, dv_ref
):
    head, step = pl.program_id(0), pl.program_id(1)
    blocks = pl.num_programs(1)
    own = q_ref.shape[1] * pl.num_programs(0)

    @pl.when(step == 0)
    def _():
        dk_ref[...] = jnp.zeros_like(dk_ref)
        dv_ref[...] = jnp.zeros_like(dv_ref)

    def place(part):
        return pl.ds(pl.multiple_of(part * own + head * HEAD_DIM, HEAD_DIM), HEAD_DIM)

    def turn_back(grad, rows):
        grad = grad.astype(BF16).astype(F32)
        back = grad * cos_ref[rows] - pltpu.roll(grad, HEAD_DIM // 2, 1) * sin_ref[rows]
        return back.astype(BF16)

    for block in range(blocks):

        @pl.when(step == block)
        def _():
            length = (block + 1) * QBLOCK
            rows = slice(block * QBLOCK, length)
            query, keys, grad = q_ref[...], k_ref[:length], go_ref[...]
            scores = masked_scores(query, keys, first_ref[...], block, length)
            probs = jnp.exp(scores - log_ref[0])
            grad_probs = dot(grad, v_ref[:length], NT)
            inner = jnp.sum(probs * grad_probs, -1, keepdims=True)
            grad_scores = (probs * (grad_probs - inner)).astype(BF16)
            dq = dot(grad_scores, keys, NN) * HEAD_DIM**-0.5
            g_ref[rows, place(0)] = turn_back(dq, rows)
            dk_ref[:length] += dot(grad_scores, query, TN)
            dv_ref[:length] += dot(probs.astype(BF16), grad, TN)

    @pl.when(step == blocks - 1)
    def _():
        g_ref[:, place(1)] = turn_back(dk_ref[...] * HEAD_DIM**-0.5, slice(None))
        g_ref[:, place(2)] = dv_ref[...].astype(BF16)


def attend_back_call(queries, keys, values, grads, first, logs, cosine, sine):
    rows, own = queries.shape
    heads, blocks = own // HEAD_DIM, rows // QBLOCK
    part = pl.BlockSpec((QBLOCK, HEAD_DIM), lambda h, i: (i, h))
    whole = pl.BlockSpec((rows, HEAD_DIM), lambda h, i: (0, h))
    column = pl.BlockSpec((QBLOCK, 1), lambda h, i: (i, 0))
    table = pl.BlockSpec((rows, HEAD_DIM), lambda h, i: (0, 0))
    return pl.pallas_call(
        attend_back_kernel,
        grid=(heads, blocks),
        in_specs=[
            part,
            whole,
            whole,
            part,
            column,
            pl.BlockSpec((1, QBLOCK, 1), lambda h, i: (h, i, 0)),
            table,
            table,
        ],
        out_specs=pl.BlockSpec((rows, 3 * own), lambda h, i: (0, 0)),
        out_shape=jax.ShapeDtypeStruct((rows, 3 * own), BF16),
        scratch_shapes=[pltpu.VMEM((rows, HEAD_DIM), F32)] * 2,
        compiler_params=pltpu.CompilerParams(vmem_limit_bytes=40 << 20),
        cost_estimate=pl.CostEstimate(
            flops=10 * rows * rows * own, bytes_accessed=14 * rows * own, transcendentals=heads * rows * rows
        ),
        name="attend_back",
    )(queries, keys, values, grads, first, logs, cosine, sine)


class Copies:
    def __init__(self, send_sems, recv_sems):
        self.send_sems, self.recv_sems, self.used = send_sems, recv_sems, 0

    def make(self, source, target, device):
        slot = self.used
        self.used += 1
        return pltpu.make_async_remote_copy(
            src_ref=source,
            dst_ref=target,
            send_sem=self.send_sems.at[slot],
            recv_sem=self.recv_sems.at[slot],
            device_id=device,
            device_id_type=pl.DeviceIdType.MESH,
        )

    def start(self, source, target, device):
        copy = self.make(source, target, device)
        copy.start()
        return copy


def meet(devices):
    barrier = pltpu.get_barrier_semaphore()
    for device in devices:
        pl.semaphore_signal(barrier, inc=1, device_id=device, device_id_type=pl.DeviceIdType.MESH)
    pl.semaphore_wait(barrier, len(devices))


def front_kernel(
    copies,
    tokens_ref,
    gain1_ref,
    bias1_ref,
    w_ref,
    cos_ref,
    sin_ref,
    first_ref,
    keep_ref,
    w_out_ref,
    gain2_ref,
    bias2_ref,
    up_ref,
    down_ref,
    cot_ref,
    n1_ref,
    q_ref,
    k_ref,
    v_ref,
    heads_ref,
    log_ref,
    middle_ref,
    n2_ref,
    up_other_ref,
    down_other_ref,
    near_cot_ref,
    away_ref,
    got_core_ref,
    pass_ref,
    got_y_ref,
    own_ref,
    send_sems,
    recv_sems,
    local_sem,
):
    t, z, x = lax.axis_index("tensor"), lax.axis_index("bucket"), lax.axis_index("dp")
    rows, own = q_ref.shape
    share = own_ref.shape[0]
    heads = own // HEAD_DIM
    core, y_side = {"tensor": t ^ 1}, {"tensor": t ^ 2}
    near, far = {"bucket": z ^ 1}, {"bucket": z ^ 2}
    twins = [{"dp": lax.rem(x + d, copies)} for d in range(1, copies)]
    meet([core, y_side, near, far] + twins)
    links = Copies(send_sems, recv_sems)

    def piece(ref, of):
        size = ref.shape[0] // copies
        return ref.at[pl.ds(pl.multiple_of(of * size, 16), size)]

    def shard(ref, index):
        return ref.at[pl.ds(pl.multiple_of(index * share, share), share)]

    up_piece = links.start(piece(up_ref, x), piece(up_other_ref, x), far)
    parity = lax.rem(t, 2)
    cots = [
        links.start(shard(cot_ref, parity + i), shard(near_cot_ref, parity + i), near)
        for i in (0, 2)
    ]
    down_piece = links.start(piece(down_ref, x), piece(down_other_ref, x), far)

    def project(i, carry):
        at = pl.ds(pl.multiple_of(i * QBLOCK, QBLOCK), QBLOCK)
        normed, _ = norm_parts(tokens_ref[at, :].astype(F32))
        low = (normed * gain1_ref[...] + bias1_ref[...]).astype(BF16)
        n1_ref[at, :] = low
        cosine, sine = cos_ref[at, :], sin_ref[at, :]
        for part, out_ref in enumerate((q_ref, k_ref, v_ref)):
            projected = dot(low, w_ref[part], NN)
            if part == 2:
                out_ref[at, :] = projected.astype(BF16)
                continue
            for lane in range(0, own, HEAD_DIM):
                head = projected[:, lane : lane + HEAD_DIM]
                turned = head * cosine + pltpu.roll(head, HEAD_DIM // 2, 1) * sine
                out_ref[at, lane : lane + HEAD_DIM] = turned.astype(BF16)
        return carry

    lax.fori_loop(0, rows // QBLOCK, project, 0)

    for head in range(heads):
        lanes = slice(head * HEAD_DIM, (head + 1) * HEAD_DIM)
        for block in range(rows // QBLOCK):
            length = (block + 1) * QBLOCK
            at = slice(block * QBLOCK, length)
            scores = masked_scores(
                q_ref[at, lanes], k_ref[:length, lanes], first_ref[at], block, length
            )
            most = jnp.max(scores, -1, keepdims=True)
            expo = jnp.exp(scores - most)
            total = jnp.sum(expo, -1, keepdims=True)
            weights = (expo * (1.0 / total)).astype(BF16)
            out = dot(weights, v_ref[:length, lanes], NN)
            heads_ref[at, lanes] = (out * keep_ref[at]).astype(BF16)
            log_ref[at, head : head + 1] = most + jnp.log(total)

    def attended(index):
        at = pl.ds(pl.multiple_of(index * share, share), share)
        return dot(heads_ref[at, :], w_out_ref[...], NN)

    away_ref[1] = attended(t ^ 3).astype(BF16)
    to_core1 = links.start(away_ref.at[1], got_core_ref.at[1], core)
    away_ref[0] = attended(t ^ 1).astype(BF16)
    to_core0 = links.start(away_ref.at[0], got_core_ref.at[0], core)
    passed = attended(t ^ 2)
    to_core1.wait_recv()
    pass_ref[...] = (passed + got_core_ref[1].astype(F32)).astype(BF16)
    to_y = links.start(pass_ref, got_y_ref, y_side)
    middle = attended(t)
    middle += tokens_ref[pl.ds(pl.multiple_of(t * share, share), share), :].astype(F32)
    to_core0.wait_recv()
    middle_ref[...] = middle + got_core_ref[0].astype(F32)

    onward = []

    def pass_on(copy, ref, devices):
        copy.wait_recv()
        onward.extend(links.start(ref, ref, device) for device in devices)

    for i, copy in zip((0, 2), cots):
        pass_on(copy, shard(near_cot_ref, parity + i), [core])
    pass_on(up_piece, piece(up_other_ref, x), twins)
    to_y.wait_recv()
    total = middle_ref[...] + got_y_ref[...].astype(F32)
    middle_ref[...] = total
    normed, _ = norm_parts(total)
    own_ref[...] = (normed * gain2_ref[...] + bias2_ref[...]).astype(BF16)
    keep_own = pltpu.make_async_copy(own_ref, n2_ref.at[0, t], local_sem)
    keep_own.start()
    to_near = links.start(own_ref, n2_ref.at[1, t], near)
    own_y = links.start(own_ref, n2_ref.at[0, t], y_side)
    own_core = links.start(own_ref, n2_ref.at[0, t], core)
    own_y.wait_recv()
    y_core = links.start(n2_ref.at[0, t ^ 2], n2_ref.at[0, t ^ 2], core)
    to_near.wait_recv()
    near_y = links.start(n2_ref.at[1, t], n2_ref.at[1, t], y_side)
    near_core = links.start(n2_ref.at[1, t], n2_ref.at[1, t], core)
    near_y.wait_recv()
    near_y_core = links.start(n2_ref.at[1, t ^ 2], n2_ref.at[1, t ^ 2], core)
    pass_on(down_piece, piece(down_other_ref, x), twins)
    keep_own.wait()
    for copy in (own_core, y_core, near_core, near_y_core, *onward):
        copy.wait_recv()
    for copy in (
        up_piece, *cots, down_piece, to_core1, to_core0, to_y,
        to_near, own_y, own_core, y_core, near_y, near_core, near_y_core, *onward,
    ):
        copy.wait_send()


def front_call(tokens, ln1, w3, tables_, first, keep, w_out, ln2, up, down, cotangent):
    rows, width = tokens.shape
    own = w3.shape[2]
    splits, copies = lax.axis_size("tensor"), lax.axis_size("dp")
    share = rows // splits
    inside = pl.BlockSpec(memory_space=pltpu.VMEM)
    outside = pl.BlockSpec(memory_space=pl.ANY)
    shape = jax.ShapeDtypeStruct
    total = 14 + 2 * copies
    return pl.pallas_call(
        functools.partial(front_kernel, copies),
        in_specs=[inside] * 11 + [outside] * 3,
        out_specs=[inside] * 7 + [outside] * 4,
        out_shape=[
            shape((rows, width), BF16),
            shape((rows, own), BF16),
            shape((rows, own), BF16),
            shape((rows, own), BF16),
            shape((rows, own), BF16),
            shape((rows, own // HEAD_DIM), F32),
            shape((share, width), F32),
            shape((2, splits, share, width), BF16),
            shape(up.shape, BF16),
            shape(down.shape, BF16),
            shape(cotangent.shape, BF16),
        ],
        scratch_shapes=[
            pltpu.VMEM((2, share, width), BF16),
            pltpu.VMEM((2, share, width), BF16),
            pltpu.VMEM((share, width), BF16),
            pltpu.VMEM((share, width), BF16),
            pltpu.VMEM((share, width), BF16),
            pltpu.SemaphoreType.DMA((total,)),
            pltpu.SemaphoreType.DMA((total,)),
            pltpu.SemaphoreType.DMA,
        ],
        compiler_params=pltpu.CompilerParams(
            vmem_limit_bytes=56 << 20, collective_id=0, has_side_effects=True
        ),
        cost_estimate=pl.CostEstimate(
            flops=8 * rows * width * own + 4 * rows * rows * own,
            bytes_accessed=60 << 20,
            transcendentals=rows * rows * own // HEAD_DIM,
        ),
        name="front",
    )(tokens, *ln1, w3, *tables_, first, keep, w_out, *ln2, up, down, cotangent)


def qkv_back_kernel(g_ref, w_ref, o_ref):
    own = w_ref.shape[2]
    total = dot(g_ref[:, :own], w_ref[0], NT)
    total += dot(g_ref[:, own : 2 * own], w_ref[1], NT)
    total += dot(g_ref[:, 2 * own :], w_ref[2], NT)
    o_ref[...] = total.astype(BF16)


def qkv_back_call(grads, w3):
    rows = grads.shape[0]
    width, own = w3.shape[1], w3.shape[2]
    return pl.pallas_call(
        qkv_back_kernel,
        grid=(rows // QBLOCK,),
        in_specs=[
            pl.BlockSpec((QBLOCK, 3 * own), lambda i: (i, 0)),
            pl.BlockSpec(w3.shape, lambda i: (0, 0, 0)),
        ],
        out_specs=pl.BlockSpec((QBLOCK, width), lambda i: (i, 0)),
        out_shape=jax.ShapeDtypeStruct((rows, width), BF16),
        compiler_params=pltpu.CompilerParams(vmem_limit_bytes=40 << 20),
        cost_estimate=pl.CostEstimate(
            flops=6 * rows * width * own, bytes_accessed=2 * (rows * width + 3 * width * own + 3 * rows * own), transcendentals=0
        ),
        name="qkv_back",
    )(grads, w3)


def swap(values, axis, bit):
    pairs = [(i, i ^ bit) for i in range(lax.axis_size(axis))]
    return lax.ppermute(values, axis, pairs)


def local(
    tokens,
    cotangent,
    lengths,
    head_quarters,
    buckets,
    ln1_gain,
    ln1_bias,
    w_qkv,
    w_out,
    ln2_gain,
    ln2_bias,
    w_router,
    w_up,
    w_down,
):
    tok_rows, model_width = tokens.shape
    owners = lax.axis_size("bucket")
    splits = lax.axis_size("tensor")
    copies = lax.axis_size("dp")
    share = tok_rows // splits
    t, z, x = lax.axis_index("tensor"), lax.axis_index("bucket"), lax.axis_index("dp")
    up_own = w_up.reshape(model_width, -1)
    down_own = w_down.reshape(-1, model_width)
    hidden_width = up_own.shape[1]

    levels = buckets[:, 0].astype(F32).reshape(-1, HEAD_DIM)
    near_levels = swap(levels, "bucket", 1)

    def shard(values, bit):
        return lax.dynamic_slice_in_dim(values, (t ^ bit) * share, share, 0)

    ORDER = (0, 2, 1, 3)

    positions, first = layout(lengths[0], tok_rows)
    first = first[:, None]
    keep = (t < head_quarters).astype(F32)[:, None]
    cosine, sine = tables(positions)
    w3 = jnp.transpose(w_qkv, (1, 0, 2))
    (
        normed1,
        queries,
        keys,
        values,
        heads_low,
        logs,
        middle,
        n2,
        up_other,
        down_other,
        near_cotangent,
    ) = front_call(
        tokens,
        (ln1_gain.reshape(1, -1), ln1_bias.reshape(1, -1)),
        w3,
        (cosine, sine),
        first,
        keep,
        w_out,
        (ln2_gain.reshape(1, -1), ln2_bias.reshape(1, -1)),
        up_own,
        down_own,
        cotangent,
    )
    logs = logs.T[:, :, None]
    normed2 = lax.dynamic_index_in_dim(n2[0], t, 0, False)
    n2 = n2.reshape(-1, model_width)

    def gather_sum(away, kept):
        both = kept + swap(away.astype(BF16), "tensor", 1).astype(F32)
        half = both.shape[0] // 2
        return both[:half] + swap(both[half:].astype(BF16), "tensor", 2).astype(F32)

    def spread(piece):
        both = jnp.concatenate([piece, swap(piece, "tensor", 2)], 0)
        return jnp.concatenate([both, swap(both, "tensor", 1)], 0)

    def natural(piece, dtype):
        whole = jnp.zeros((tok_rows, model_width), dtype)
        for at, bit in enumerate(ORDER):
            part = lax.slice_in_dim(piece, at * share, (at + 1) * share).astype(dtype)
            whole = lax.dynamic_update_slice_in_dim(whole, part, (t ^ bit) * share, 0)
        return whole

    inputs_own = shard(tokens, 0).astype(F32)
    hat2, inverse2 = norm_parts(middle)

    def gate_of(rows, tok_levels):
        probs = softmax(dot(rows, w_router, NN))
        onehot = (tok_levels[:, None] == jnp.arange(owners, dtype=F32)[None, :]).astype(F32)
        return jnp.sum(probs * onehot, -1), probs, onehot

    level_all = jnp.concatenate([levels.reshape(-1), near_levels.reshape(-1)], 0)
    gate_all, _, _ = gate_of(n2, level_all)
    grad_all = jnp.concatenate([cotangent, near_cotangent], 0)
    grad_branch = (gate_all[:, None] * grad_all.astype(F32)).astype(BF16)
    kept_own = (level_all >= z.astype(F32))[:, None]
    kept_other = (level_all >= (z ^ 2).astype(F32))[:, None]

    def forward(up, kept):
        act = jnp.where(kept, jnp.maximum(dot(n2, up, NN), 0.0), 0.0)
        return act.astype(BF16), jnp.square(act).astype(BF16)

    act_own, hid_own = forward(up_own, kept_own)
    act_other, hid_other = forward(up_other, kept_other)

    def scatter_sum(total):
        blocks = total.astype(BF16).reshape(2, splits, share, model_width)
        pick = lambda bits: jnp.stack(
            [lax.dynamic_index_in_dim(blocks, t ^ bit, 1, False) for bit in bits], 1
        )
        both = pick((0, 2)).astype(F32) + swap(pick((1, 3)), "tensor", 1).astype(F32)
        one = both[:, 0] + swap(both[:, 1].astype(BF16), "tensor", 2).astype(F32)
        return one[0] + swap(one[1].astype(BF16), "bucket", 1).astype(F32)

    branch_sum = scatter_sum(dot(hid_own, down_own, NN) + dot(hid_other, down_other, NN))

    def backward(act, down):
        grad = dot(grad_branch, down, NT)
        return (grad * 2.0 * act.astype(F32)).astype(BF16)

    gu_own, gu_other = backward(act_own, down_own), backward(act_other, down_other)
    returned = scatter_sum(dot(gu_own, up_own, NT) + dot(gu_other, up_other, NT))

    def reduce_dp(grad, dim):
        return lax.psum_scatter(grad.astype(BF16), "dp", scatter_dimension=dim, tiled=True)

    def owner_sum(own, other):
        return own.astype(F32) + swap(other, "bucket", 2).astype(F32)

    grad_down = owner_sum(
        reduce_dp(dot(grad_branch, hid_own, TN), 0), reduce_dp(dot(grad_branch, hid_other, TN), 0)
    ).T
    grad_up = owner_sum(
        reduce_dp(dot(n2, gu_own, TN), 0), reduce_dp(dot(n2, gu_other, TN), 0)
    )

    branch = branch_sum.astype(BF16).astype(F32)
    level_own = shard(levels.reshape(-1), 0)
    gate, probs, onehot = gate_of(normed2, level_own)
    mixed_own = (middle + gate[:, None] * branch).astype(BF16)
    mixed = natural(spread(mixed_own), BF16)
    grad_output = shard(cotangent, 0).astype(F32)
    grad_gate = jnp.sum(grad_output * branch, -1)
    grad_logits = (grad_gate * gate)[:, None] * (onehot - probs)
    grad_router = dot(normed2.astype(F32), grad_logits, TN)
    grad_norm2 = returned.astype(BF16).astype(F32) + dot(grad_logits, w_router.astype(F32), NT)
    grad_in2, grad_ln2_gain, grad_ln2_bias = norm_backward(grad_norm2, hat2, inverse2, ln2_gain)
    grad_middle = grad_output + grad_in2
    grad_attention = natural(spread(grad_middle.astype(BF16)), BF16)

    def reduce_all(grad):
        return lax.psum_scatter(
            grad.astype(BF16), ("dp", "bucket"), scatter_dimension=0, tiled=True
        ).astype(F32)

    grad_w_out = reduce_all(dot(grad_attention, heads_low, TN)).T
    grad_heads = (dot(grad_attention, w_out, NT).astype(BF16).astype(F32) * keep).astype(BF16)
    grad_projected = attend_back_call(
        queries, keys, values, grad_heads, first, logs, cosine, sine
    )
    partial = qkv_back_call(grad_projected, w3)
    grad_w_qkv = reduce_all(dot(normed1, grad_projected, TN)).reshape(-1, 3, w3.shape[2])
    away = jnp.concatenate([shard(partial, 1), shard(partial, 3)], 0)
    kept = jnp.concatenate([shard(partial, 0), shard(partial, 2)], 0).astype(F32)
    grad_norm1 = gather_sum(away, kept)
    hat1, inverse1 = norm_parts(inputs_own)
    grad_in1, grad_ln1_gain, grad_ln1_bias = norm_backward(grad_norm1, hat1, inverse1, ln1_gain)
    tokens_grad = natural(spread((grad_middle + grad_in1).astype(BF16)), F32)

    def reduce_small(*grads):
        stacked = jnp.stack(grads, 0)
        total = lax.psum(stacked, ("dp", "tensor", "bucket"))
        width = model_width // (copies * owners)
        return lax.dynamic_slice_in_dim(total, (x * owners + z) * width, width, 1)

    small = reduce_small(grad_ln2_gain, grad_ln2_bias, *(grad_router[:, i] for i in range(owners)))
    last = reduce_small(grad_ln1_gain, grad_ln1_bias)
    return (
        mixed,
        tokens_grad,
        last[0],
        last[1],
        grad_w_qkv,
        grad_w_out,
        small[0],
        small[1],
        small[2:].T,
        grad_up.reshape(-1, 1, hidden_width),
        grad_down.reshape(1, hidden_width, -1),
    )


def solution(mesh):
    placed = (
        P(("dp", "bucket"), None),
        P(("dp", "bucket"), None),
        P(("dp", "bucket"), None),
        P(("dp", "bucket")),
        P(("dp", "bucket"), None),
        P(),
        P(),
        P(None, None, "tensor"),
        P("tensor", None),
        P(),
        P(),
        P(),
        P(None, "bucket", "tensor"),
        P("bucket", "tensor", None),
    )
    return jax.shard_map(
        local,
        mesh=mesh,
        in_specs=placed,
        out_specs=(
            P(("dp", "bucket"), None),
            P(("dp", "bucket"), None),
            P(("dp", "bucket")),
            P(("dp", "bucket")),
            P(("dp", "bucket"), None, "tensor"),
            P("tensor", ("dp", "bucket")),
            P(("dp", "bucket")),
            P(("dp", "bucket")),
            P(("dp", "bucket"), None),
            P("dp", "bucket", "tensor"),
            P("bucket", "tensor", "dp"),
        ),
        check_vma=False,
    )
```

```python
import functools
import math

import jax
import jax.numpy as jnp
from jax import lax
from jax.experimental import pallas as pl
from jax.experimental.pallas import tpu as pltpu
from jax.sharding import PartitionSpec as P

HEAD_DIM = 128
QBLOCK = 256
EPS = 1e-05
HIGH = lax.Precision.HIGHEST
NEGATIVE = -1e30
F32 = jnp.float32
BF16 = jnp.bfloat16


def norm_parts(values):
    centred = values - jnp.mean(values, -1, keepdims=True)
    inverse = lax.rsqrt(jnp.mean(centred * centred, -1, keepdims=True) + EPS)
    return centred * inverse, inverse


def norm_backward(grad_in, normed, inverse, gain):
    scaled = grad_in * gain
    inner = (
        scaled
        - jnp.mean(scaled, -1, keepdims=True)
        - normed * jnp.mean(scaled * normed, -1, keepdims=True)
    )
    return inverse * inner, jnp.sum(grad_in * normed, 0), jnp.sum(grad_in, 0)


def layout(lengths_row, tok_rows):
    ends = jnp.cumsum(lengths_row)
    starts = ends - lengths_row
    tok_index = jnp.arange(tok_rows, dtype=jnp.int32)
    segments = jnp.sum((tok_index[:, None] >= ends[None, :]).astype(jnp.int32), 1)
    chosen = segments[:, None] == jnp.arange(lengths_row.shape[0], dtype=jnp.int32)[None, :]
    first = jnp.sum(jnp.where(chosen, starts[None, :], 0), 1)
    return tok_index - first, first


def tables(positions):
    half_dim = HEAD_DIM // 2
    freq = jnp.exp(jnp.arange(half_dim, dtype=F32) * (-math.log(10000.0) / half_dim))
    angle = positions.astype(F32)[:, None] * freq[None, :]
    cosine, sine = jnp.cos(angle), jnp.sin(angle)
    return jnp.concatenate([cosine, cosine], -1), jnp.concatenate([-sine, sine], -1)


def dot(left, right, dims):
    return lax.dot_general(left, right, (dims, ((), ())), preferred_element_type=F32)


NN = ((1,), (0,))
NT = ((1,), (1,))
TN = ((0,), (0,))


def masked_scores(query, keys, first, block, length):
    scores = dot(query, keys, NT) * HEAD_DIM**-0.5
    key_at = lax.broadcasted_iota(jnp.int32, (QBLOCK, length), 1)
    row_at = lax.broadcasted_iota(jnp.int32, (QBLOCK, length), 0) + block * QBLOCK
    allowed = (key_at >= first) & (key_at <= row_at)
    return jnp.where(allowed, scores, NEGATIVE)


def attend_back_kernel(
    q_ref, k_ref, v_ref, go_ref, first_ref, log_ref, cos_ref, sin_ref, g_ref, dk_ref, dv_ref
):
    head, step = pl.program_id(0), pl.program_id(1)
    blocks = pl.num_programs(1)
    own = q_ref.shape[1] * pl.num_programs(0)

    @pl.when(step == 0)
    def _():
        dk_ref[...] = jnp.zeros_like(dk_ref)
        dv_ref[...] = jnp.zeros_like(dv_ref)

    def place(part):
        return pl.ds(pl.multiple_of(part * own + head * HEAD_DIM, HEAD_DIM), HEAD_DIM)

    def turn_back(grad, rows):
        grad = grad.astype(BF16).astype(F32)
        back = grad * cos_ref[rows] - pltpu.roll(grad, HEAD_DIM // 2, 1) * sin_ref[rows]
        return back.astype(BF16)

    for block in range(blocks):

        @pl.when(step == block)
        def _():
            length = (block + 1) * QBLOCK
            rows = slice(block * QBLOCK, length)
            query, keys, grad = q_ref[...], k_ref[:length], go_ref[...]
            scores = masked_scores(query, keys, first_ref[...], block, length)
            probs = jnp.exp(scores - log_ref[0])
            grad_probs = dot(grad, v_ref[:length], NT)
            inner = jnp.sum(probs * grad_probs, -1, keepdims=True)
            grad_scores = (probs * (grad_probs - inner)).astype(BF16)
            dq = dot(grad_scores, keys, NN) * HEAD_DIM**-0.5
            g_ref[rows, place(0)] = turn_back(dq, rows)
            dk_ref[:length] += dot(grad_scores, query, TN)
            dv_ref[:length] += dot(probs.astype(BF16), grad, TN)

    @pl.when(step == blocks - 1)
    def _():
        g_ref[:, place(1)] = turn_back(dk_ref[...] * HEAD_DIM**-0.5, slice(None))
        g_ref[:, place(2)] = dv_ref[...].astype(BF16)


def attend_back_call(queries, keys, values, grads, first, logs, cosine, sine):
    rows, own = queries.shape
    heads, blocks = own // HEAD_DIM, rows // QBLOCK
    part = pl.BlockSpec((QBLOCK, HEAD_DIM), lambda h, i: (i, h))
    whole = pl.BlockSpec((rows, HEAD_DIM), lambda h, i: (0, h))
    column = pl.BlockSpec((QBLOCK, 1), lambda h, i: (i, 0))
    table = pl.BlockSpec((rows, HEAD_DIM), lambda h, i: (0, 0))
    return pl.pallas_call(
        attend_back_kernel,
        grid=(heads, blocks),
        in_specs=[
            part,
            whole,
            whole,
            part,
            column,
            pl.BlockSpec((1, QBLOCK, 1), lambda h, i: (h, i, 0)),
            table,
            table,
        ],
        out_specs=pl.BlockSpec((rows, 3 * own), lambda h, i: (0, 0)),
        out_shape=jax.ShapeDtypeStruct((rows, 3 * own), BF16),
        scratch_shapes=[pltpu.VMEM((rows, HEAD_DIM), F32)] * 2,
        compiler_params=pltpu.CompilerParams(vmem_limit_bytes=40 << 20),
        cost_estimate=pl.CostEstimate(
            flops=10 * rows * rows * own, bytes_accessed=14 * rows * own, transcendentals=heads * rows * rows
        ),
        name="attend_back",
    )(queries, keys, values, grads, first, logs, cosine, sine)


class Copies:
    def __init__(self, send_sems, recv_sems):
        self.send_sems, self.recv_sems, self.used = send_sems, recv_sems, 0

    def make(self, source, target, device):
        slot = self.used
        self.used += 1
        return pltpu.make_async_remote_copy(
            src_ref=source,
            dst_ref=target,
            send_sem=self.send_sems.at[slot],
            recv_sem=self.recv_sems.at[slot],
            device_id=device,
            device_id_type=pl.DeviceIdType.MESH,
        )

    def start(self, source, target, device):
        copy = self.make(source, target, device)
        copy.start()
        return copy


def meet(devices):
    barrier = pltpu.get_barrier_semaphore()
    for device in devices:
        pl.semaphore_signal(barrier, inc=1, device_id=device, device_id_type=pl.DeviceIdType.MESH)
    pl.semaphore_wait(barrier, len(devices))


def front_kernel(
    copies,
    tokens_ref,
    gain1_ref,
    bias1_ref,
    w_ref,
    cos_ref,
    sin_ref,
    first_ref,
    keep_ref,
    w_out_ref,
    gain2_ref,
    bias2_ref,
    up_ref,
    down_ref,
    cot_ref,
    n1_ref,
    q_ref,
    k_ref,
    v_ref,
    heads_ref,
    log_ref,
    middle_ref,
    n2_ref,
    up_other_ref,
    down_other_ref,
    cots_ref,
    away_ref,
    got_core_ref,
    pass_ref,
    got_y_ref,
    own_ref,
    send_sems,
    recv_sems,
    local_sem,
    local_sems,
):
    t, z, x = lax.axis_index("tensor"), lax.axis_index("bucket"), lax.axis_index("dp")
    rows, own = q_ref.shape
    share = own_ref.shape[0]
    heads = own // HEAD_DIM
    core, y_side = {"tensor": t ^ 1}, {"tensor": t ^ 2}
    near, far = {"bucket": z ^ 1}, {"bucket": z ^ 2}
    twins = [{"dp": lax.rem(x + d, copies)} for d in range(1, copies)]
    meet([core, y_side, near, far] + twins)
    links = Copies(send_sems, recv_sems)

    def piece(ref, of):
        size = ref.shape[0] // copies
        return ref.at[pl.ds(pl.multiple_of(of * size, 16), size)]

    def shard(ref, index):
        return ref.at[pl.ds(pl.multiple_of(index * share, share), share)]

    up_piece = links.start(piece(up_ref, x), piece(up_other_ref, x), far)
    parity = lax.rem(t, 2)
    keep_cots = [
        pltpu.make_async_copy(shard(cot_ref, i), cots_ref.at[0, i], local_sems.at[i])
        for i in range(cots_ref.shape[1])
    ]
    for copy in keep_cots:
        copy.start()
    cots = [
        links.start(shard(cot_ref, parity + i), cots_ref.at[1, parity + i], near)
        for i in (0, 2)
    ]
    down_piece = links.start(piece(down_ref, x), piece(down_other_ref, x), far)

    def project(i, carry):
        at = pl.ds(pl.multiple_of(i * QBLOCK, QBLOCK), QBLOCK)
        normed, _ = norm_parts(tokens_ref[at, :].astype(F32))
        low = (normed * gain1_ref[...] + bias1_ref[...]).astype(BF16)
        n1_ref[at, :] = low
        cosine, sine = cos_ref[at, :], sin_ref[at, :]
        for part, out_ref in enumerate((q_ref, k_ref, v_ref)):
            projected = dot(low, w_ref[part], NN)
            if part == 2:
                out_ref[at, :] = projected.astype(BF16)
                continue
            for lane in range(0, own, HEAD_DIM):
                head = projected[:, lane : lane + HEAD_DIM]
                turned = head * cosine + pltpu.roll(head, HEAD_DIM // 2, 1) * sine
                out_ref[at, lane : lane + HEAD_DIM] = turned.astype(BF16)
        return carry

    lax.fori_loop(0, rows // QBLOCK, project, 0)

    for head in range(heads):
        lanes = slice(head * HEAD_DIM, (head + 1) * HEAD_DIM)
        for block in range(rows // QBLOCK):
            length = (block + 1) * QBLOCK
            at = slice(block * QBLOCK, length)
            scores = masked_scores(
                q_ref[at, lanes], k_ref[:length, lanes], first_ref[at], block, length
            )
            most = jnp.max(scores, -1, keepdims=True)
            expo = jnp.exp(scores - most)
            total = jnp.sum(expo, -1, keepdims=True)
            weights = (expo * (1.0 / total)).astype(BF16)
            out = dot(weights, v_ref[:length, lanes], NN)
            heads_ref[at, lanes] = (out * keep_ref[at]).astype(BF16)
            log_ref[at, head : head + 1] = most + jnp.log(total)

    def attended(index):
        at = pl.ds(pl.multiple_of(index * share, share), share)
        return dot(heads_ref[at, :], w_out_ref[...], NN)

    away_ref[1] = attended(t ^ 3).astype(BF16)
    to_core1 = links.start(away_ref.at[1], got_core_ref.at[1], core)
    away_ref[0] = attended(t ^ 1).astype(BF16)
    to_core0 = links.start(away_ref.at[0], got_core_ref.at[0], core)
    passed = attended(t ^ 2)
    to_core1.wait_recv()
    pass_ref[...] = (passed + got_core_ref[1].astype(F32)).astype(BF16)
    to_y = links.start(pass_ref, got_y_ref, y_side)
    middle = attended(t)
    middle += tokens_ref[pl.ds(pl.multiple_of(t * share, share), share), :].astype(F32)
    to_core0.wait_recv()
    middle_ref[...] = middle + got_core_ref[0].astype(F32)

    onward = []

    def pass_on(copy, ref, devices):
        copy.wait_recv()
        onward.extend(links.start(ref, ref, device) for device in devices)

    for i, copy in zip((0, 2), cots):
        pass_on(copy, cots_ref.at[1, parity + i], [core])
    pass_on(up_piece, piece(up_other_ref, x), twins)
    to_y.wait_recv()
    total = middle_ref[...] + got_y_ref[...].astype(F32)
    middle_ref[...] = total
    normed, _ = norm_parts(total)
    own_ref[...] = (normed * gain2_ref[...] + bias2_ref[...]).astype(BF16)
    keep_own = pltpu.make_async_copy(own_ref, n2_ref.at[0, t], local_sem)
    keep_own.start()
    to_near = links.start(own_ref, n2_ref.at[1, t], near)
    own_y = links.start(own_ref, n2_ref.at[0, t], y_side)
    own_core = links.start(own_ref, n2_ref.at[0, t], core)
    own_y.wait_recv()
    y_core = links.start(n2_ref.at[0, t ^ 2], n2_ref.at[0, t ^ 2], core)
    to_near.wait_recv()
    near_y = links.start(n2_ref.at[1, t], n2_ref.at[1, t], y_side)
    near_core = links.start(n2_ref.at[1, t], n2_ref.at[1, t], core)
    near_y.wait_recv()
    near_y_core = links.start(n2_ref.at[1, t ^ 2], n2_ref.at[1, t ^ 2], core)
    pass_on(down_piece, piece(down_other_ref, x), twins)
    for copy in (keep_own, *keep_cots):
        copy.wait()
    for copy in (own_core, y_core, near_core, near_y_core, *onward):
        copy.wait_recv()
    for copy in (
        up_piece, *cots, down_piece, to_core1, to_core0, to_y,
        to_near, own_y, own_core, y_core, near_y, near_core, near_y_core, *onward,
    ):
        copy.wait_send()


def front_call(tokens, ln1, w3, tables_, first, keep, w_out, ln2, up, down, cotangent):
    rows, width = tokens.shape
    own = w3.shape[2]
    splits, copies = lax.axis_size("tensor"), lax.axis_size("dp")
    share = rows // splits
    inside = pl.BlockSpec(memory_space=pltpu.VMEM)
    outside = pl.BlockSpec(memory_space=pl.ANY)
    shape = jax.ShapeDtypeStruct
    total = 14 + 2 * copies
    return pl.pallas_call(
        functools.partial(front_kernel, copies),
        in_specs=[inside] * 11 + [outside] * 3,
        out_specs=[inside] * 7 + [outside] * 4,
        out_shape=[
            shape((rows, width), BF16),
            shape((rows, own), BF16),
            shape((rows, own), BF16),
            shape((rows, own), BF16),
            shape((rows, own), BF16),
            shape((rows, own // HEAD_DIM), F32),
            shape((share, width), F32),
            shape((2, splits, share, width), BF16),
            shape(up.shape, BF16),
            shape(down.shape, BF16),
            shape((2, splits, share, width), BF16),
        ],
        scratch_shapes=[
            pltpu.VMEM((2, share, width), BF16),
            pltpu.VMEM((2, share, width), BF16),
            pltpu.VMEM((share, width), BF16),
            pltpu.VMEM((share, width), BF16),
            pltpu.VMEM((share, width), BF16),
            pltpu.SemaphoreType.DMA((total,)),
            pltpu.SemaphoreType.DMA((total,)),
            pltpu.SemaphoreType.DMA,
            pltpu.SemaphoreType.DMA((splits,)),
        ],
        compiler_params=pltpu.CompilerParams(
            vmem_limit_bytes=56 << 20, collective_id=0, has_side_effects=True
        ),
        cost_estimate=pl.CostEstimate(
            flops=8 * rows * width * own + 4 * rows * rows * own,
            bytes_accessed=60 << 20,
            transcendentals=rows * rows * own // HEAD_DIM,
        ),
        name="front",
    )(tokens, *ln1, w3, *tables_, first, keep, w_out, *ln2, up, down, cotangent)


def block_at(i, t):
    late = i // 4
    near = (1 - late) * (1 - (i // 2) % 2) + late * (1 - i % 2)
    bit = (1 - late) * (3 - 2 * (i % 2)) + late * (2 - 2 * ((i % 4) // 2))
    return near, t ^ bit


def router_gate(rows, w_router_ref, level):
    logits = dot(rows, w_router_ref[...], NN)
    expo = jnp.exp(logits - jnp.max(logits, -1, keepdims=True))
    probs = expo / jnp.sum(expo, -1, keepdims=True)
    number = lax.broadcasted_iota(jnp.int32, probs.shape, 1).astype(F32)
    onehot = (number == level).astype(F32)
    return jnp.sum(probs * onehot, -1, keepdims=True), probs, onehot


def middle_kernel(
    copies,
    n2_ref,
    cot_ref,
    up_own_ref,
    up_other_ref,
    down_own_ref,
    down_other_ref,
    router_ref,
    level_ref,
    x2_ref,
    gain2_ref,
    bias2_ref,
    mixed_ref,
    gx2_ref,
    ga_ref,
    small_ref,
    gf_ref,
    grad_down_ref,
    grad_up_ref,
    got_x_ref,
    n2_in,
    cot_in,
    gf_out,
    hid_ref,
    gu_ref,
    part_f,
    part_g,
    hold_f,
    send_ref,
    core_f,
    core_g,
    got_fz,
    got_fy,
    got_gy,
    got_gz,
    tile_in,
    tile_out,
    core_send_sems,
    core_recv_sems,
    send_sems,
    recv_sems,
    in_sems,
    out_sems,
    tile_sems,
    tile_out_sems,
):
    t, z, x = lax.axis_index("tensor"), lax.axis_index("bucket"), lax.axis_index("dp")
    share, width = gx2_ref.shape
    half = up_own_ref.shape[1]
    core, y_side, near = {"tensor": t ^ 1}, {"tensor": t ^ 2}, {"bucket": z ^ 1}
    twins = [{"dp": lax.rem(x + d, copies)} for d in range(1, copies)]
    splits = n2_ref.shape[1]

    def load(i, slot):
        at, s = block_at(i, t)
        return (
            pltpu.make_async_copy(n2_ref.at[at, s], n2_in.at[slot], in_sems.at[slot, 0]),
            pltpu.make_async_copy(cot_ref.at[at, s], cot_in.at[slot], in_sems.at[slot, 1]),
        )

    def store(i, slot):
        at, s = block_at(i, t)
        return pltpu.make_async_copy(gf_out.at[slot], gf_ref.at[at, s], out_sems.at[slot])

    def to_core(i):
        return [
            pltpu.make_async_remote_copy(
                src_ref=send_ref.at[kind * 2 + i % 2],
                dst_ref=(core_f, core_g)[kind].at[i],
                send_sem=core_send_sems.at[kind, i],
                recv_sem=core_recv_sems.at[kind, i],
                device_id=core,
                device_id_type=pl.DeviceIdType.MESH,
            )
            for kind in (0, 1)
        ]

    for copy in load(0, 0):
        copy.start()
    meet([core, y_side, near] + twins)
    links = Copies(send_sems, recv_sems)
    f_near_y = links.make(send_ref.at[0], got_fz.at[0], near)
    g_near_y = links.make(send_ref.at[1], got_gy.at[0], y_side)
    g_own_y = links.make(send_ref.at[2], got_gy.at[1], y_side)
    f_near = links.make(send_ref.at[3], got_fz.at[1], near)
    f_own_y = links.make(send_ref.at[0], got_fy, y_side)
    g_near = links.make(send_ref.at[1], got_gz, near)

    def work(i, carry):
        slot = i % 2
        at, s = block_at(i, t)
        for copy in load(i, slot):
            copy.wait()

        @pl.when(i < 7)
        def _():
            for copy in load(i + 1, 1 - slot):
                copy.start()

        @pl.when(i >= 2)
        def _():
            store(i - 2, slot).wait()

        spot = pl.ds(pl.multiple_of((at * splits + s) * share, share), share)
        rows = n2_in[slot]
        level = level_ref[spot, :]
        gate, _, _ = router_gate(rows, router_ref, level)
        grad = (gate * cot_in[slot].astype(F32)).astype(BF16)
        gf_out[slot] = grad
        store(i, slot).start()
        for part, (up_ref, down_ref, unit_level) in enumerate(
            ((up_own_ref, down_own_ref, z), (up_other_ref, down_other_ref, z ^ 2))
        ):
            lanes = slice(part * half, (part + 1) * half)
            kept = level >= unit_level.astype(F32)
            act = jnp.where(kept, jnp.maximum(dot(rows, up_ref[...], NN), 0.0), 0.0)
            hid_ref[spot, lanes] = (act * act).astype(BF16)
            back = dot(grad, down_ref[...], NT)
            gu_ref[spot, lanes] = (back * 2.0 * act).astype(BF16)
        for lanes in (slice(0, width // 2), slice(width // 2, width)):
            part_f[:, lanes] = dot(hid_ref[spot, :half], down_own_ref[:, lanes], NN) + dot(
                hid_ref[spot, half:], down_other_ref[:, lanes], NN
            )
            part_g[:, lanes] = dot(gu_ref[spot, :half], up_own_ref[lanes, :], NT) + dot(
                gu_ref[spot, half:], up_other_ref[lanes, :], NT
            )

        @pl.when(i < 4)
        def _():
            @pl.when(i >= 2)
            def _():
                for copy in to_core(i - 2):
                    copy.wait_send()

            send_ref[slot] = part_f[...].astype(BF16)
            send_ref[2 + slot] = part_g[...].astype(BF16)
            for copy in to_core(i):
                copy.start()

        def with_core(kind, at_i):
            to_core(at_i)[kind].wait_recv()
            got = (core_f, core_g)[kind][at_i].astype(F32)
            return (part_f, part_g)[kind][...] + got

        @pl.when(i == 4)
        def _():
            for j in (2, 3):
                for copy in to_core(j):
                    copy.wait_send()
            send_ref[1] = with_core(1, 0).astype(BF16)
            g_near_y.start()
            send_ref[0] = with_core(0, 0).astype(BF16)
            f_near_y.start()

        @pl.when(i == 5)
        def _():
            send_ref[2] = with_core(1, 2).astype(BF16)
            g_own_y.start()
            hold_f[...] = with_core(0, 2)

        @pl.when(i == 6)
        def _():
            send_ref[3] = with_core(0, 1).astype(BF16)
            f_near.start()
            gx2_ref[...] = with_core(1, 1)

        @pl.when(i == 7)
        def _():
            part_f[...] = with_core(0, 3)
            part_g[...] = with_core(1, 3)

        return carry

    lax.fori_loop(0, 8, work, 0)
    store(6, 0).wait()
    store(7, 1).wait()

    tile = tile_in.shape[-1]
    tiles = width // tile

    def weight_grads(source_ref, right_ref, result_ref):
        def fetch(j, slot):
            lanes = pl.ds(pl.multiple_of(j * tile, tile), tile)
            return pltpu.make_async_copy(
                source_ref.at[:, :, :, lanes], tile_in.at[slot], tile_sems.at[slot]
            )

        def put(j, slot):
            rows = pl.ds(pl.multiple_of(j * tile, tile), tile)
            return pltpu.make_async_copy(
                tile_out.at[slot], result_ref.at[rows, :], tile_out_sems.at[slot]
            )

        fetch(0, 0).start()

        def step(j, carry):
            slot = j % 2
            fetch(j, slot).wait()

            @pl.when(j < tiles - 1)
            def _():
                fetch(j + 1, 1 - slot).start()

            @pl.when(j >= 2)
            def _():
                put(j - 2, slot).wait()

            left = tile_in[slot].reshape(-1, tile)
            tile_out[slot] = dot(left, right_ref[...], TN).astype(BF16)
            put(j, slot).start()
            return carry

        lax.fori_loop(0, tiles, step, 0)
        put(tiles - 2, (tiles - 2) % 2).wait()
        put(tiles - 1, (tiles - 1) % 2).wait()

    weight_grads(gf_ref, hid_ref, grad_down_ref)
    size = width // copies
    downs = []
    for d in range(1, copies):
        part = pl.ds(pl.multiple_of(lax.rem(x + d, copies) * size, size), size)
        downs.append(
            links.start(grad_down_ref.at[part, :], got_x_ref.at[d - 1], twins[d - 1])
        )

    f_near_y.wait_recv()
    f_near_y.wait_send()
    send_ref[0] = (hold_f[...] + got_fz[0].astype(F32)).astype(BF16)
    f_own_y.start()
    g_near_y.wait_recv()
    g_near_y.wait_send()
    send_ref[1] = (gx2_ref[...] + got_gy[0].astype(F32)).astype(BF16)
    g_near.start()

    weight_grads(n2_ref, gu_ref, grad_up_ref)

    own = pltpu.make_async_copy(n2_ref.at[0, t], n2_in.at[0], in_sems.at[0, 0])
    own.start()
    own_cot = pltpu.make_async_copy(cot_ref.at[0, t], cot_in.at[0], in_sems.at[0, 1])
    own_cot.start()
    own.wait()
    own_cot.wait()
    for copy in (f_near, f_own_y, g_own_y, g_near):
        copy.wait_recv()
    small_ref[...] = jnp.zeros_like(small_ref)
    few = 64

    def finish(j, carry):
        at = pl.ds(pl.multiple_of(j * few, few), few)
        level = level_ref[pl.ds(pl.multiple_of(t * share + j * few, few), few), :]
        rows = n2_in[0, at, :]
        gate, probs, onehot = router_gate(rows, router_ref, level)
        branch = part_f[at, :] + got_fz[1, at, :].astype(F32) + got_fy[at, :].astype(F32)
        branch = branch.astype(BF16).astype(F32)
        x2 = x2_ref[at, :]
        mixed_ref[at, :] = (x2 + gate * branch).astype(BF16)
        grad_out = cot_in[0, at, :].astype(F32)
        grad_gate = jnp.sum(grad_out * branch, -1, keepdims=True)
        grad_logits = grad_gate * gate * (onehot - probs)
        returned = part_g[at, :] + got_gy[1, at, :].astype(F32) + got_gz[at, :].astype(F32)
        grad_n2 = returned.astype(BF16).astype(F32)
        grad_n2 += lax.dot_general(
            grad_logits,
            router_ref[...].astype(F32),
            (NT, ((), ())),
            precision=HIGH,
            preferred_element_type=F32,
        )
        hat, inverse = norm_parts(x2)
        back, gain_grad, bias_grad = norm_backward(grad_n2, hat, inverse, gain2_ref[...])
        gx2 = grad_out + back
        gx2_ref[at, :] = gx2
        ga_ref[at, :] = gx2.astype(BF16)
        small_ref[0:1, :] += gain_grad[None, :]
        small_ref[1:2, :] += bias_grad[None, :]
        small_ref[2 : 2 + probs.shape[1], :] += lax.dot_general(
            grad_logits, rows.astype(F32), (TN, ((), ())), precision=HIGH, preferred_element_type=F32
        )
        return carry

    lax.fori_loop(0, share // few, finish, 0)
    for copy in downs:
        copy.wait_recv()
    for copy in (g_own_y, f_near, f_own_y, g_near, *downs):
        copy.wait_send()


def middle_call(n2, cotangents, ups, downs, w_router, levels, middle, ln2):
    _, splits, share, width = n2.shape
    copies = lax.axis_size("dp")
    half = ups[0].shape[1]
    rows = 2 * splits * share
    inside = pl.BlockSpec(memory_space=pltpu.VMEM)
    outside = pl.BlockSpec(memory_space=pl.ANY)
    shape = jax.ShapeDtypeStruct
    block = lambda count, dtype=BF16: pltpu.VMEM((*count, share, width), dtype)
    dma = lambda *count: pltpu.SemaphoreType.DMA(count)
    return pl.pallas_call(
        functools.partial(middle_kernel, copies),
        in_specs=[outside] * 2 + [inside] * 9,
        out_specs=[inside] * 4 + [outside] * 4,
        out_shape=[
            shape((share, width), BF16),
            shape((share, width), F32),
            shape((share, width), BF16),
            shape((2 + w_router.shape[1], width), F32),
            shape(n2.shape, BF16),
            shape((width, 2 * half), BF16),
            shape((width, 2 * half), BF16),
            shape((copies - 1, width // copies, 2 * half), BF16),
        ],
        scratch_shapes=[
            block((2,)),
            block((2,)),
            block((2,)),
            pltpu.VMEM((rows, 2 * half), BF16),
            pltpu.VMEM((rows, 2 * half), BF16),
            block((), F32),
            block((), F32),
            block((), F32),
            block((4,)),
            block((4,)),
            block((4,)),
            block((2,)),
            block(()),
            block((2,)),
            block(()),
            pltpu.VMEM((2, 2, splits, share, 256), BF16),
            pltpu.VMEM((2, 256, 2 * half), BF16),
            dma(2, 4),
            dma(2, 4),
            dma(6 + copies - 1),
            dma(6 + copies - 1),
            dma(2, 2),
            dma(2),
            dma(2),
            dma(2),
        ],
        compiler_params=pltpu.CompilerParams(
            vmem_limit_bytes=62 << 20, collective_id=1, has_side_effects=True
        ),
        cost_estimate=pl.CostEstimate(
            flops=12 * rows * width * 2 * half, bytes_accessed=80 << 20, transcendentals=0
        ),
        name="middle",
    )(n2, cotangents, *ups, *downs, w_router, levels, middle, *ln2)


def qkv_back_kernel(g_ref, w_ref, o_ref):
    own = w_ref.shape[2]
    total = dot(g_ref[:, :own], w_ref[0], NT)
    total += dot(g_ref[:, own : 2 * own], w_ref[1], NT)
    total += dot(g_ref[:, 2 * own :], w_ref[2], NT)
    o_ref[...] = total.astype(BF16)


def qkv_back_call(grads, w3):
    rows = grads.shape[0]
    width, own = w3.shape[1], w3.shape[2]
    return pl.pallas_call(
        qkv_back_kernel,
        grid=(rows // QBLOCK,),
        in_specs=[
            pl.BlockSpec((QBLOCK, 3 * own), lambda i: (i, 0)),
            pl.BlockSpec(w3.shape, lambda i: (0, 0, 0)),
        ],
        out_specs=pl.BlockSpec((QBLOCK, width), lambda i: (i, 0)),
        out_shape=jax.ShapeDtypeStruct((rows, width), BF16),
        compiler_params=pltpu.CompilerParams(vmem_limit_bytes=40 << 20),
        cost_estimate=pl.CostEstimate(
            flops=6 * rows * width * own, bytes_accessed=2 * (rows * width + 3 * width * own + 3 * rows * own), transcendentals=0
        ),
        name="qkv_back",
    )(grads, w3)


def swap(values, axis, bit):
    pairs = [(i, i ^ bit) for i in range(lax.axis_size(axis))]
    return lax.ppermute(values, axis, pairs)


def local(
    tokens,
    cotangent,
    lengths,
    head_quarters,
    buckets,
    ln1_gain,
    ln1_bias,
    w_qkv,
    w_out,
    ln2_gain,
    ln2_bias,
    w_router,
    w_up,
    w_down,
):
    tok_rows, model_width = tokens.shape
    owners = lax.axis_size("bucket")
    splits = lax.axis_size("tensor")
    copies = lax.axis_size("dp")
    share = tok_rows // splits
    t, z, x = lax.axis_index("tensor"), lax.axis_index("bucket"), lax.axis_index("dp")
    up_own = w_up.reshape(model_width, -1)
    down_own = w_down.reshape(-1, model_width)
    hidden_width = up_own.shape[1]

    levels = buckets[:, 0].astype(F32).reshape(-1, HEAD_DIM)
    near_levels = swap(levels, "bucket", 1)

    def shard(values, bit):
        return lax.dynamic_slice_in_dim(values, (t ^ bit) * share, share, 0)

    ORDER = (0, 2, 1, 3)

    positions, first = layout(lengths[0], tok_rows)
    first = first[:, None]
    keep = (t < head_quarters).astype(F32)[:, None]
    cosine, sine = tables(positions)
    w3 = jnp.transpose(w_qkv, (1, 0, 2))
    (
        normed1,
        queries,
        keys,
        values,
        heads_low,
        logs,
        middle,
        n2,
        up_other,
        down_other,
        cotangents,
    ) = front_call(
        tokens,
        (ln1_gain.reshape(1, -1), ln1_bias.reshape(1, -1)),
        w3,
        (cosine, sine),
        first,
        keep,
        w_out,
        (ln2_gain.reshape(1, -1), ln2_bias.reshape(1, -1)),
        up_own,
        down_own,
        cotangent,
    )
    logs = logs.T[:, :, None]
    level_all = jnp.concatenate([levels.reshape(-1), near_levels.reshape(-1)], 0)[:, None]
    (
        mixed_own,
        grad_middle,
        grad_attention_own,
        small,
        _,
        down_part,
        up_part,
        got_down,
    ) = middle_call(
        n2,
        cotangents,
        (up_own, up_other),
        (down_own, down_other),
        w_router,
        level_all,
        middle,
        (ln2_gain.reshape(1, -1), ln2_bias.reshape(1, -1)),
    )
    inputs_own = shard(tokens, 0).astype(F32)

    def gather_sum(away, kept):
        both = kept + swap(away.astype(BF16), "tensor", 1).astype(F32)
        half = both.shape[0] // 2
        return both[:half] + swap(both[half:].astype(BF16), "tensor", 2).astype(F32)

    def spread(piece):
        both = jnp.concatenate([piece, swap(piece, "tensor", 2)], 0)
        return jnp.concatenate([both, swap(both, "tensor", 1)], 0)

    def natural(piece, dtype):
        whole = jnp.zeros((tok_rows, model_width), dtype)
        for at, bit in enumerate(ORDER):
            part = lax.slice_in_dim(piece, at * share, (at + 1) * share).astype(dtype)
            whole = lax.dynamic_update_slice_in_dim(whole, part, (t ^ bit) * share, 0)
        return whole

    size = model_width // copies
    down_sum = lax.dynamic_slice_in_dim(down_part, x * size, size, 0).astype(F32)
    down_sum += jnp.sum(got_down.astype(F32), 0)
    up_sum = lax.psum_scatter(up_part, "dp", scatter_dimension=0, tiled=True).astype(F32)

    def owner_sum(total):
        return total[:, :hidden_width] + swap(
            total[:, hidden_width:].astype(BF16), "bucket", 2
        ).astype(F32)

    grad_down = owner_sum(down_sum).T
    grad_up = owner_sum(up_sum)
    mixed = natural(spread(mixed_own), BF16)
    grad_attention = natural(spread(grad_attention_own), BF16)

    def reduce_all(grad):
        return lax.psum_scatter(
            grad.astype(BF16), ("dp", "bucket"), scatter_dimension=0, tiled=True
        ).astype(F32)

    grad_w_out = reduce_all(dot(grad_attention, heads_low, TN)).T
    grad_heads = (dot(grad_attention, w_out, NT).astype(BF16).astype(F32) * keep).astype(BF16)
    grad_projected = attend_back_call(
        queries, keys, values, grad_heads, first, logs, cosine, sine
    )
    partial = qkv_back_call(grad_projected, w3)
    grad_w_qkv = reduce_all(dot(normed1, grad_projected, TN)).reshape(-1, 3, w3.shape[2])
    away = jnp.concatenate([shard(partial, 1), shard(partial, 3)], 0)
    kept = jnp.concatenate([shard(partial, 0), shard(partial, 2)], 0).astype(F32)
    grad_norm1 = gather_sum(away, kept)
    hat1, inverse1 = norm_parts(inputs_own)
    grad_in1, grad_ln1_gain, grad_ln1_bias = norm_backward(grad_norm1, hat1, inverse1, ln1_gain)
    tokens_grad = natural(spread((grad_middle + grad_in1).astype(BF16)), F32)

    def reduce_small(*grads):
        stacked = jnp.stack(grads, 0)
        total = lax.psum(stacked, ("dp", "tensor", "bucket"))
        width = model_width // (copies * owners)
        return lax.dynamic_slice_in_dim(total, (x * owners + z) * width, width, 1)

    small = reduce_small(*(small[i] for i in range(2 + owners)))
    last = reduce_small(grad_ln1_gain, grad_ln1_bias)
    return (
        mixed,
        tokens_grad,
        last[0],
        last[1],
        grad_w_qkv,
        grad_w_out,
        small[0],
        small[1],
        small[2:].T,
        grad_up.reshape(-1, 1, hidden_width),
        grad_down.reshape(1, hidden_width, -1),
    )


def solution(mesh):
    placed = (
        P(("dp", "bucket"), None),
        P(("dp", "bucket"), None),
        P(("dp", "bucket"), None),
        P(("dp", "bucket")),
        P(("dp", "bucket"), None),
        P(),
        P(),
        P(None, None, "tensor"),
        P("tensor", None),
        P(),
        P(),
        P(),
        P(None, "bucket", "tensor"),
        P("bucket", "tensor", None),
    )
    return jax.shard_map(
        local,
        mesh=mesh,
        in_specs=placed,
        out_specs=(
            P(("dp", "bucket"), None),
            P(("dp", "bucket"), None),
            P(("dp", "bucket")),
            P(("dp", "bucket")),
            P(("dp", "bucket"), None, "tensor"),
            P("tensor", ("dp", "bucket")),
            P(("dp", "bucket")),
            P(("dp", "bucket")),
            P(("dp", "bucket"), None),
            P("dp", "bucket", "tensor"),
            P("bucket", "tensor", "dp"),
        ),
        check_vma=False,
    )
```

```python
import functools
import math

import jax
import jax.numpy as jnp
from jax import lax
from jax.experimental import pallas as pl
from jax.experimental.pallas import tpu as pltpu
from jax.sharding import PartitionSpec as P

HEAD_DIM = 128
QBLOCK = 256
EPS = 1e-05
HIGH = lax.Precision.HIGHEST
NEGATIVE = -1e30
F32 = jnp.float32
BF16 = jnp.bfloat16


def norm_parts(values):
    centred = values - jnp.mean(values, -1, keepdims=True)
    inverse = lax.rsqrt(jnp.mean(centred * centred, -1, keepdims=True) + EPS)
    return centred * inverse, inverse


def norm_backward(grad_in, normed, inverse, gain):
    scaled = grad_in * gain
    inner = (
        scaled
        - jnp.mean(scaled, -1, keepdims=True)
        - normed * jnp.mean(scaled * normed, -1, keepdims=True)
    )
    return inverse * inner, jnp.sum(grad_in * normed, 0), jnp.sum(grad_in, 0)


def layout(lengths_row, tok_rows):
    ends = jnp.cumsum(lengths_row)
    starts = ends - lengths_row
    tok_index = jnp.arange(tok_rows, dtype=jnp.int32)
    segments = jnp.sum((tok_index[:, None] >= ends[None, :]).astype(jnp.int32), 1)
    chosen = segments[:, None] == jnp.arange(lengths_row.shape[0], dtype=jnp.int32)[None, :]
    first = jnp.sum(jnp.where(chosen, starts[None, :], 0), 1)
    return tok_index - first, first


def tables(positions):
    half_dim = HEAD_DIM // 2
    freq = jnp.exp(jnp.arange(half_dim, dtype=F32) * (-math.log(10000.0) / half_dim))
    angle = positions.astype(F32)[:, None] * freq[None, :]
    cosine, sine = jnp.cos(angle), jnp.sin(angle)
    return jnp.concatenate([cosine, cosine], -1), jnp.concatenate([-sine, sine], -1)


def dot(left, right, dims):
    return lax.dot_general(left, right, (dims, ((), ())), preferred_element_type=F32)


NN = ((1,), (0,))
NT = ((1,), (1,))
TN = ((0,), (0,))


def masked_scores(query, keys, first, block, length):
    scores = dot(query, keys, NT) * HEAD_DIM**-0.5
    key_at = lax.broadcasted_iota(jnp.int32, (QBLOCK, length), 1)
    row_at = lax.broadcasted_iota(jnp.int32, (QBLOCK, length), 0) + block * QBLOCK
    allowed = (key_at >= first) & (key_at <= row_at)
    return jnp.where(allowed, scores, NEGATIVE)


class Copies:
    def __init__(self, send_sems, recv_sems):
        self.send_sems, self.recv_sems, self.used = send_sems, recv_sems, 0

    def make(self, source, target, device):
        slot = self.used
        self.used += 1
        return pltpu.make_async_remote_copy(
            src_ref=source,
            dst_ref=target,
            send_sem=self.send_sems.at[slot],
            recv_sem=self.recv_sems.at[slot],
            device_id=device,
            device_id_type=pl.DeviceIdType.MESH,
        )

    def start(self, source, target, device):
        copy = self.make(source, target, device)
        copy.start()
        return copy


def meet(devices):
    barrier = pltpu.get_barrier_semaphore()
    for device in devices:
        pl.semaphore_signal(barrier, inc=1, device_id=device, device_id_type=pl.DeviceIdType.MESH)
    pl.semaphore_wait(barrier, len(devices))


def front_kernel(
    copies,
    tokens_ref,
    gain1_ref,
    bias1_ref,
    w_ref,
    cos_ref,
    sin_ref,
    first_ref,
    keep_ref,
    w_out_ref,
    gain2_ref,
    bias2_ref,
    up_ref,
    down_ref,
    cot_ref,
    n1_ref,
    q_ref,
    k_ref,
    v_ref,
    heads_ref,
    log_ref,
    middle_ref,
    n2_ref,
    up_other_ref,
    down_other_ref,
    cots_ref,
    away_ref,
    got_core_ref,
    pass_ref,
    got_y_ref,
    own_ref,
    send_sems,
    recv_sems,
    local_sem,
    local_sems,
):
    t, z, x = lax.axis_index("tensor"), lax.axis_index("bucket"), lax.axis_index("dp")
    rows, own = q_ref.shape
    share = own_ref.shape[0]
    heads = own // HEAD_DIM
    core, y_side = {"tensor": t ^ 1}, {"tensor": t ^ 2}
    near, far = {"bucket": z ^ 1}, {"bucket": z ^ 2}
    twins = [{"dp": lax.rem(x + d, copies)} for d in range(1, copies)]
    meet([core, y_side, near, far] + twins)
    links = Copies(send_sems, recv_sems)

    def piece(ref, of):
        size = ref.shape[0] // copies
        return ref.at[pl.ds(pl.multiple_of(of * size, 16), size)]

    def shard(ref, index):
        return ref.at[pl.ds(pl.multiple_of(index * share, share), share)]

    up_piece = links.start(piece(up_ref, x), piece(up_other_ref, x), far)
    parity = lax.rem(t, 2)
    keep_cots = [
        pltpu.make_async_copy(shard(cot_ref, i), cots_ref.at[0, i], local_sems.at[i])
        for i in range(cots_ref.shape[1])
    ]
    for copy in keep_cots:
        copy.start()
    cots = [
        links.start(shard(cot_ref, parity + i), cots_ref.at[1, parity + i], near)
        for i in (0, 2)
    ]
    down_piece = links.start(piece(down_ref, x), piece(down_other_ref, x), far)

    def project(i, carry):
        at = pl.ds(pl.multiple_of(i * QBLOCK, QBLOCK), QBLOCK)
        normed, _ = norm_parts(tokens_ref[at, :].astype(F32))
        low = (normed * gain1_ref[...] + bias1_ref[...]).astype(BF16)
        n1_ref[at, :] = low
        cosine, sine = cos_ref[at, :], sin_ref[at, :]
        for part, out_ref in enumerate((q_ref, k_ref, v_ref)):
            projected = dot(low, w_ref[part], NN)
            if part == 2:
                out_ref[at, :] = projected.astype(BF16)
                continue
            for lane in range(0, own, HEAD_DIM):
                head = projected[:, lane : lane + HEAD_DIM]
                turned = head * cosine + pltpu.roll(head, HEAD_DIM // 2, 1) * sine
                out_ref[at, lane : lane + HEAD_DIM] = turned.astype(BF16)
        return carry

    lax.fori_loop(0, rows // QBLOCK, project, 0)

    for head in range(heads):
        lanes = slice(head * HEAD_DIM, (head + 1) * HEAD_DIM)
        for block in range(rows // QBLOCK):
            length = (block + 1) * QBLOCK
            at = slice(block * QBLOCK, length)
            scores = masked_scores(
                q_ref[at, lanes], k_ref[:length, lanes], first_ref[at], block, length
            )
            most = jnp.max(scores, -1, keepdims=True)
            expo = jnp.exp(scores - most)
            total = jnp.sum(expo, -1, keepdims=True)
            weights = (expo * (1.0 / total)).astype(BF16)
            out = dot(weights, v_ref[:length, lanes], NN)
            heads_ref[at, lanes] = (out * keep_ref[at]).astype(BF16)
            log_ref[at, head : head + 1] = most + jnp.log(total)

    def attended(index):
        at = pl.ds(pl.multiple_of(index * share, share), share)
        return dot(heads_ref[at, :], w_out_ref[...], NN)

    away_ref[1] = attended(t ^ 3).astype(BF16)
    to_core1 = links.start(away_ref.at[1], got_core_ref.at[1], core)
    away_ref[0] = attended(t ^ 1).astype(BF16)
    to_core0 = links.start(away_ref.at[0], got_core_ref.at[0], core)
    passed = attended(t ^ 2)
    to_core1.wait_recv()
    pass_ref[...] = (passed + got_core_ref[1].astype(F32)).astype(BF16)
    to_y = links.start(pass_ref, got_y_ref, y_side)
    middle = attended(t)
    middle += tokens_ref[pl.ds(pl.multiple_of(t * share, share), share), :].astype(F32)
    to_core0.wait_recv()
    middle_ref[...] = middle + got_core_ref[0].astype(F32)

    onward = []

    def pass_on(copy, ref, devices):
        copy.wait_recv()
        onward.extend(links.start(ref, ref, device) for device in devices)

    for i, copy in zip((0, 2), cots):
        pass_on(copy, cots_ref.at[1, parity + i], [core])
    pass_on(up_piece, piece(up_other_ref, x), twins)
    to_y.wait_recv()
    total = middle_ref[...] + got_y_ref[...].astype(F32)
    middle_ref[...] = total
    normed, _ = norm_parts(total)
    own_ref[...] = (normed * gain2_ref[...] + bias2_ref[...]).astype(BF16)
    keep_own = pltpu.make_async_copy(own_ref, n2_ref.at[0, t], local_sem)
    keep_own.start()
    to_near = links.start(own_ref, n2_ref.at[1, t], near)
    own_y = links.start(own_ref, n2_ref.at[0, t], y_side)
    own_core = links.start(own_ref, n2_ref.at[0, t], core)
    own_y.wait_recv()
    y_core = links.start(n2_ref.at[0, t ^ 2], n2_ref.at[0, t ^ 2], core)
    to_near.wait_recv()
    near_y = links.start(n2_ref.at[1, t], n2_ref.at[1, t], y_side)
    near_core = links.start(n2_ref.at[1, t], n2_ref.at[1, t], core)
    near_y.wait_recv()
    near_y_core = links.start(n2_ref.at[1, t ^ 2], n2_ref.at[1, t ^ 2], core)
    pass_on(down_piece, piece(down_other_ref, x), twins)
    for copy in (keep_own, *keep_cots):
        copy.wait()
    for copy in (own_core, y_core, near_core, near_y_core, *onward):
        copy.wait_recv()
    for copy in (
        up_piece, *cots, down_piece, to_core1, to_core0, to_y,
        to_near, own_y, own_core, y_core, near_y, near_core, near_y_core, *onward,
    ):
        copy.wait_send()


def front_call(tokens, ln1, w3, tables_, first, keep, w_out, ln2, up, down, cotangent):
    rows, width = tokens.shape
    own = w3.shape[2]
    splits, copies = lax.axis_size("tensor"), lax.axis_size("dp")
    share = rows // splits
    inside = pl.BlockSpec(memory_space=pltpu.VMEM)
    outside = pl.BlockSpec(memory_space=pl.ANY)
    shape = jax.ShapeDtypeStruct
    total = 14 + 2 * copies
    return pl.pallas_call(
        functools.partial(front_kernel, copies),
        in_specs=[inside] * 11 + [outside] * 3,
        out_specs=[inside] * 7 + [outside] * 4,
        out_shape=[
            shape((rows, width), BF16),
            shape((rows, own), BF16),
            shape((rows, own), BF16),
            shape((rows, own), BF16),
            shape((rows, own), BF16),
            shape((rows, own // HEAD_DIM), F32),
            shape((share, width), F32),
            shape((2, splits, share, width), BF16),
            shape(up.shape, BF16),
            shape(down.shape, BF16),
            shape((2, splits, share, width), BF16),
        ],
        scratch_shapes=[
            pltpu.VMEM((2, share, width), BF16),
            pltpu.VMEM((2, share, width), BF16),
            pltpu.VMEM((share, width), BF16),
            pltpu.VMEM((share, width), BF16),
            pltpu.VMEM((share, width), BF16),
            pltpu.SemaphoreType.DMA((total,)),
            pltpu.SemaphoreType.DMA((total,)),
            pltpu.SemaphoreType.DMA,
            pltpu.SemaphoreType.DMA((splits,)),
        ],
        compiler_params=pltpu.CompilerParams(
            vmem_limit_bytes=56 << 20, collective_id=0, has_side_effects=True
        ),
        cost_estimate=pl.CostEstimate(
            flops=8 * rows * width * own + 4 * rows * rows * own,
            bytes_accessed=60 << 20,
            transcendentals=rows * rows * own // HEAD_DIM,
        ),
        name="front",
    )(tokens, *ln1, w3, *tables_, first, keep, w_out, *ln2, up, down, cotangent)


def block_at(i, t):
    late = i // 4
    near = (1 - late) * (1 - (i // 2) % 2) + late * (1 - i % 2)
    bit = (1 - late) * (3 - 2 * (i % 2)) + late * (2 - 2 * ((i % 4) // 2))
    return near, t ^ bit


def router_gate(rows, w_router_ref, level):
    logits = dot(rows, w_router_ref[...], NN)
    expo = jnp.exp(logits - jnp.max(logits, -1, keepdims=True))
    probs = expo / jnp.sum(expo, -1, keepdims=True)
    number = lax.broadcasted_iota(jnp.int32, probs.shape, 1).astype(F32)
    onehot = (number == level).astype(F32)
    return jnp.sum(probs * onehot, -1, keepdims=True), probs, onehot


def middle_kernel(
    copies,
    n2_ref,
    cot_ref,
    up_own_ref,
    up_other_ref,
    down_own_ref,
    down_other_ref,
    router_ref,
    level_ref,
    x2_ref,
    gain2_ref,
    bias2_ref,
    mixed_ref,
    gx2_ref,
    ga_ref,
    small_ref,
    gf_ref,
    grad_down_ref,
    grad_up_ref,
    got_x_ref,
    n2_in,
    cot_in,
    gf_out,
    hid_ref,
    gu_ref,
    part_f,
    part_g,
    hold_f,
    send_ref,
    core_f,
    core_g,
    got_fz,
    got_fy,
    got_gy,
    got_gz,
    tile_in,
    tile_out,
    core_send_sems,
    core_recv_sems,
    send_sems,
    recv_sems,
    in_sems,
    out_sems,
    tile_sems,
    tile_out_sems,
):
    t, z, x = lax.axis_index("tensor"), lax.axis_index("bucket"), lax.axis_index("dp")
    share, width = gx2_ref.shape
    half = up_own_ref.shape[1]
    core, y_side, near = {"tensor": t ^ 1}, {"tensor": t ^ 2}, {"bucket": z ^ 1}
    twins = [{"dp": lax.rem(x + d, copies)} for d in range(1, copies)]
    splits = n2_ref.shape[1]

    def load(i, slot):
        at, s = block_at(i, t)
        return (
            pltpu.make_async_copy(n2_ref.at[at, s], n2_in.at[slot], in_sems.at[slot, 0]),
            pltpu.make_async_copy(cot_ref.at[at, s], cot_in.at[slot], in_sems.at[slot, 1]),
        )

    def store(i, slot):
        at, s = block_at(i, t)
        return pltpu.make_async_copy(gf_out.at[slot], gf_ref.at[at, s], out_sems.at[slot])

    def to_core(i):
        return [
            pltpu.make_async_remote_copy(
                src_ref=send_ref.at[kind * 2 + i % 2],
                dst_ref=(core_f, core_g)[kind].at[i],
                send_sem=core_send_sems.at[kind, i],
                recv_sem=core_recv_sems.at[kind, i],
                device_id=core,
                device_id_type=pl.DeviceIdType.MESH,
            )
            for kind in (0, 1)
        ]

    for copy in load(0, 0):
        copy.start()
    meet([core, y_side, near] + twins)
    links = Copies(send_sems, recv_sems)
    f_near_y = links.make(send_ref.at[0], got_fz.at[0], near)
    g_near_y = links.make(send_ref.at[1], got_gy.at[0], y_side)
    g_own_y = links.make(send_ref.at[2], got_gy.at[1], y_side)
    f_near = links.make(send_ref.at[3], got_fz.at[1], near)
    f_own_y = links.make(send_ref.at[0], got_fy, y_side)
    g_near = links.make(send_ref.at[1], got_gz, near)

    def work(i, carry):
        slot = i % 2
        at, s = block_at(i, t)
        for copy in load(i, slot):
            copy.wait()

        @pl.when(i < 7)
        def _():
            for copy in load(i + 1, 1 - slot):
                copy.start()

        @pl.when(i >= 2)
        def _():
            store(i - 2, slot).wait()

        spot = pl.ds(pl.multiple_of((at * splits + s) * share, share), share)
        rows = n2_in[slot]
        level = level_ref[spot, :]
        gate, _, _ = router_gate(rows, router_ref, level)
        grad = (gate * cot_in[slot].astype(F32)).astype(BF16)
        gf_out[slot] = grad
        store(i, slot).start()
        for part, (up_ref, down_ref, unit_level) in enumerate(
            ((up_own_ref, down_own_ref, z), (up_other_ref, down_other_ref, z ^ 2))
        ):
            lanes = slice(part * half, (part + 1) * half)
            kept = level >= unit_level.astype(F32)
            act = jnp.where(kept, jnp.maximum(dot(rows, up_ref[...], NN), 0.0), 0.0)
            hid_ref[spot, lanes] = (act * act).astype(BF16)
            back = dot(grad, down_ref[...], NT)
            gu_ref[spot, lanes] = (back * 2.0 * act).astype(BF16)
        for lanes in (slice(0, width // 2), slice(width // 2, width)):
            part_f[:, lanes] = dot(hid_ref[spot, :half], down_own_ref[:, lanes], NN) + dot(
                hid_ref[spot, half:], down_other_ref[:, lanes], NN
            )
            part_g[:, lanes] = dot(gu_ref[spot, :half], up_own_ref[lanes, :], NT) + dot(
                gu_ref[spot, half:], up_other_ref[lanes, :], NT
            )

        @pl.when(i < 4)
        def _():
            @pl.when(i >= 2)
            def _():
                for copy in to_core(i - 2):
                    copy.wait_send()

            send_ref[slot] = part_f[...].astype(BF16)
            send_ref[2 + slot] = part_g[...].astype(BF16)
            for copy in to_core(i):
                copy.start()

        def with_core(kind, at_i):
            to_core(at_i)[kind].wait_recv()
            got = (core_f, core_g)[kind][at_i].astype(F32)
            return (part_f, part_g)[kind][...] + got

        @pl.when(i == 4)
        def _():
            for j in (2, 3):
                for copy in to_core(j):
                    copy.wait_send()
            send_ref[1] = with_core(1, 0).astype(BF16)
            g_near_y.start()
            send_ref[0] = with_core(0, 0).astype(BF16)
            f_near_y.start()

        @pl.when(i == 5)
        def _():
            send_ref[2] = with_core(1, 2).astype(BF16)
            g_own_y.start()
            hold_f[...] = with_core(0, 2)

        @pl.when(i == 6)
        def _():
            send_ref[3] = with_core(0, 1).astype(BF16)
            f_near.start()
            gx2_ref[...] = with_core(1, 1)

        @pl.when(i == 7)
        def _():
            part_f[...] = with_core(0, 3)
            part_g[...] = with_core(1, 3)

        return carry

    lax.fori_loop(0, 8, work, 0)
    store(6, 0).wait()
    store(7, 1).wait()

    tile = tile_in.shape[-1]
    tiles = width // tile

    def weight_grads(source_ref, right_ref, result_ref):
        def fetch(j, slot):
            lanes = pl.ds(pl.multiple_of(j * tile, tile), tile)
            return pltpu.make_async_copy(
                source_ref.at[:, :, :, lanes], tile_in.at[slot], tile_sems.at[slot]
            )

        def put(j, slot):
            rows = pl.ds(pl.multiple_of(j * tile, tile), tile)
            return pltpu.make_async_copy(
                tile_out.at[slot], result_ref.at[rows, :], tile_out_sems.at[slot]
            )

        fetch(0, 0).start()

        def step(j, carry):
            slot = j % 2
            fetch(j, slot).wait()

            @pl.when(j < tiles - 1)
            def _():
                fetch(j + 1, 1 - slot).start()

            @pl.when(j >= 2)
            def _():
                put(j - 2, slot).wait()

            left = tile_in[slot].reshape(-1, tile)
            tile_out[slot] = dot(left, right_ref[...], TN).astype(BF16)
            put(j, slot).start()
            return carry

        lax.fori_loop(0, tiles, step, 0)
        put(tiles - 2, (tiles - 2) % 2).wait()
        put(tiles - 1, (tiles - 1) % 2).wait()

    weight_grads(gf_ref, hid_ref, grad_down_ref)
    size = width // copies
    downs = []
    for d in range(1, copies):
        part = pl.ds(pl.multiple_of(lax.rem(x + d, copies) * size, size), size)
        downs.append(
            links.start(grad_down_ref.at[part, :], got_x_ref.at[d - 1], twins[d - 1])
        )

    f_near_y.wait_recv()
    f_near_y.wait_send()
    send_ref[0] = (hold_f[...] + got_fz[0].astype(F32)).astype(BF16)
    f_own_y.start()
    g_near_y.wait_recv()
    g_near_y.wait_send()
    send_ref[1] = (gx2_ref[...] + got_gy[0].astype(F32)).astype(BF16)
    g_near.start()

    weight_grads(n2_ref, gu_ref, grad_up_ref)

    own = pltpu.make_async_copy(n2_ref.at[0, t], n2_in.at[0], in_sems.at[0, 0])
    own.start()
    own_cot = pltpu.make_async_copy(cot_ref.at[0, t], cot_in.at[0], in_sems.at[0, 1])
    own_cot.start()
    own.wait()
    own_cot.wait()
    for copy in (f_near, f_own_y, g_own_y, g_near):
        copy.wait_recv()
    small_ref[...] = jnp.zeros_like(small_ref)
    few = 64

    def finish(j, carry):
        at = pl.ds(pl.multiple_of(j * few, few), few)
        level = level_ref[pl.ds(pl.multiple_of(t * share + j * few, few), few), :]
        rows = n2_in[0, at, :]
        gate, probs, onehot = router_gate(rows, router_ref, level)
        branch = part_f[at, :] + got_fz[1, at, :].astype(F32) + got_fy[at, :].astype(F32)
        branch = branch.astype(BF16).astype(F32)
        x2 = x2_ref[at, :]
        mixed_ref[at, :] = (x2 + gate * branch).astype(BF16)
        grad_out = cot_in[0, at, :].astype(F32)
        grad_gate = jnp.sum(grad_out * branch, -1, keepdims=True)
        grad_logits = grad_gate * gate * (onehot - probs)
        returned = part_g[at, :] + got_gy[1, at, :].astype(F32) + got_gz[at, :].astype(F32)
        grad_n2 = returned.astype(BF16).astype(F32)
        grad_n2 += lax.dot_general(
            grad_logits,
            router_ref[...].astype(F32),
            (NT, ((), ())),
            precision=HIGH,
            preferred_element_type=F32,
        )
        hat, inverse = norm_parts(x2)
        back, gain_grad, bias_grad = norm_backward(grad_n2, hat, inverse, gain2_ref[...])
        gx2 = grad_out + back
        gx2_ref[at, :] = gx2
        ga_ref[at, :] = gx2.astype(BF16)
        small_ref[0:1, :] += gain_grad[None, :]
        small_ref[1:2, :] += bias_grad[None, :]
        small_ref[2 : 2 + probs.shape[1], :] += lax.dot_general(
            grad_logits, rows.astype(F32), (TN, ((), ())), precision=HIGH, preferred_element_type=F32
        )
        return carry

    lax.fori_loop(0, share // few, finish, 0)
    for copy in downs:
        copy.wait_recv()
    for copy in (g_own_y, f_near, f_own_y, g_near, *downs):
        copy.wait_send()


def middle_call(n2, cotangents, ups, downs, w_router, levels, middle, ln2):
    _, splits, share, width = n2.shape
    copies = lax.axis_size("dp")
    half = ups[0].shape[1]
    rows = 2 * splits * share
    inside = pl.BlockSpec(memory_space=pltpu.VMEM)
    outside = pl.BlockSpec(memory_space=pl.ANY)
    shape = jax.ShapeDtypeStruct
    block = lambda count, dtype=BF16: pltpu.VMEM((*count, share, width), dtype)
    dma = lambda *count: pltpu.SemaphoreType.DMA(count)
    return pl.pallas_call(
        functools.partial(middle_kernel, copies),
        in_specs=[outside] * 2 + [inside] * 9,
        out_specs=[inside] * 4 + [outside] * 4,
        out_shape=[
            shape((share, width), BF16),
            shape((share, width), F32),
            shape((share, width), BF16),
            shape((2 + w_router.shape[1], width), F32),
            shape(n2.shape, BF16),
            shape((width, 2 * half), BF16),
            shape((width, 2 * half), BF16),
            shape((copies - 1, width // copies, 2 * half), BF16),
        ],
        scratch_shapes=[
            block((2,)),
            block((2,)),
            block((2,)),
            pltpu.VMEM((rows, 2 * half), BF16),
            pltpu.VMEM((rows, 2 * half), BF16),
            block((), F32),
            block((), F32),
            block((), F32),
            block((4,)),
            block((4,)),
            block((4,)),
            block((2,)),
            block(()),
            block((2,)),
            block(()),
            pltpu.VMEM((2, 2, splits, share, 256), BF16),
            pltpu.VMEM((2, 256, 2 * half), BF16),
            dma(2, 4),
            dma(2, 4),
            dma(6 + copies - 1),
            dma(6 + copies - 1),
            dma(2, 2),
            dma(2),
            dma(2),
            dma(2),
        ],
        compiler_params=pltpu.CompilerParams(
            vmem_limit_bytes=62 << 20, collective_id=1, has_side_effects=True
        ),
        cost_estimate=pl.CostEstimate(
            flops=12 * rows * width * 2 * half, bytes_accessed=80 << 20, transcendentals=0
        ),
        name="middle",
    )(n2, cotangents, *ups, *downs, w_router, levels, middle, *ln2)


def back_kernel(
    copies,
    q_ref,
    k_ref,
    v_ref,
    heads_ref,
    log_ref,
    first_ref,
    keep_ref,
    cos_ref,
    sin_ref,
    w_out_ref,
    w_ref,
    gain1_ref,
    tokens_ref,
    gx2_ref,
    small_in_ref,
    ga_in_ref,
    mixed_in_ref,
    n1_ref,
    down_ref,
    got_down_ref,
    up_ref,
    sums_ref,
    small_ref,
    mixed_ref,
    tg_ref,
    down_own_ref,
    down_got_ref,
    up_own_ref,
    up_got_ref,
    got_up_ref,
    leave_ref,
    ga_ref,
    go_ref,
    gp_ref,
    dk_ref,
    dv_ref,
    got_core_ref,
    got_y_ref,
    part_ref,
    tg_own_ref,
    tile_in,
    tile_out,
    fold_a,
    fold_b,
    fold_send,
    fold_out,
    kept_ref,
    got_x_ref,
    z_send,
    z_kept,
    got_z1,
    got_z2,
    got_small,
    small_send,
    send_sems,
    recv_sems,
    local_sems,
    tile_sems,
    tile_out_sems,
    fold_sems,
    fold_out_sems,
):
    t, z, x = lax.axis_index("tensor"), lax.axis_index("bucket"), lax.axis_index("dp")
    rows, own = q_ref.shape
    splits, share, width = ga_ref.shape
    heads, blocks = own // HEAD_DIM, rows // QBLOCK
    reach = width // copies
    part = got_z2.shape[1]
    core, y_side = {"tensor": t ^ 1}, {"tensor": t ^ 2}
    near, far = {"bucket": z ^ 1}, {"bucket": z ^ 2}
    twins = [{"dp": lax.rem(x + d, copies)} for d in range(1, copies)]
    meet([core, y_side, near, far] + twins)
    links = Copies(send_sems, recv_sems)
    begun = []

    def send(source, target, device):
        copy = links.start(source, target, device)
        begun.append(copy)
        return copy

    def span(start, size):
        return pl.ds(pl.multiple_of(start, size), size)

    ga_y = send(ga_in_ref, ga_ref.at[t], y_side)
    ga_core = send(ga_in_ref, ga_ref.at[t], core)
    ga_own = pltpu.make_async_copy(ga_in_ref, ga_ref.at[t], local_sems.at[0])
    ga_own.start()
    ups = [
        send(up_ref.at[span(lax.rem(x + d, copies) * reach, reach)], got_up_ref.at[d - 1], twins[d - 1])
        for d in range(1, copies)
    ]
    mixed_y = send(mixed_in_ref, mixed_ref.at[t], y_side)
    mixed_core = send(mixed_in_ref, mixed_ref.at[t], core)
    mixed_own = pltpu.make_async_copy(mixed_in_ref, mixed_ref.at[t], local_sems.at[1])
    mixed_own.start()

    few = fold_a.shape[1]
    half = fold_out.shape[2]

    def fold(which, source_ref, got_ref, own_ref, target_ref):
        def loads(k, slot):
            mine = pltpu.make_async_copy(
                source_ref.at[span(x * reach + k * few, few)], fold_a.at[slot], fold_sems.at[0, slot]
            )
            theirs = [
                pltpu.make_async_copy(
                    got_ref.at[d, span(k * few, few)], fold_b.at[slot, d], fold_sems.at[1 + d, slot]
                )
                for d in range(copies - 1)
            ]
            return [mine] + theirs

        def put(k, slot):
            return pltpu.make_async_copy(
                fold_out.at[slot], own_ref.at[span(k * few, few)], fold_out_sems.at[slot]
            )

        for copy in loads(0, 0):
            copy.start()
        steps = reach // few

        def step(k, carry):
            slot = k % 2
            for copy in loads(k, slot):
                copy.wait()

            @pl.when(k < steps - 1)
            def _():
                for copy in loads(k + 1, 1 - slot):
                    copy.start()

            @pl.when(k >= 2)
            def _():
                put(k - 2, slot).wait()

            total = fold_a[slot].astype(F32)
            for d in range(copies - 1):
                total += fold_b[slot, d].astype(F32)
            fold_out[slot] = total[:, :half]
            fold_send[which, span(k * few, few), :] = total[:, half:].astype(BF16)
            put(k, slot).start()
            return carry

        lax.fori_loop(0, steps, step, 0)
        for k in range(max(0, steps - 2), steps):
            put(k, k % 2).wait()
        return send(fold_send.at[which], target_ref, far)

    down_far = fold(0, down_ref, got_down_ref, down_own_ref, down_got_ref)

    def grad_heads(s):
        at = span(s * share, share)
        grad = dot(ga_ref[s], w_out_ref[...], NT).astype(BF16).astype(F32)
        go_ref[at, :] = (grad * keep_ref[at, :]).astype(BF16)

    ga_own.wait()
    grad_heads(t)
    ga_core.wait_recv()
    grad_heads(t ^ 1)
    ga_y.wait_recv()
    ga_y_core = send(ga_ref.at[t ^ 2], ga_ref.at[t ^ 2], core)
    grad_heads(t ^ 2)
    ga_y_core.wait_recv()
    grad_heads(t ^ 3)

    tile = tile_in.shape[-1]
    per = reach // tile

    def put_tile(slot, place, chunk, count):
        d, k = place
        return pltpu.make_async_copy(
            tile_out.at[slot, pl.ds(0, count)],
            leave_ref.at[d, pl.ds(chunk, count), span(k * tile, tile)],
            tile_out_sems.at[slot],
        )

    def store_tile(index, total, chunk, count):
        slot = index % 2
        d, k = index // per, index % per
        leaving = index < per * (copies - 1)

        @pl.when(leaving)
        def _():
            @pl.when(index >= 2)
            def _():
                put_tile(slot, ((index - 2) // per, (index - 2) % per), chunk, count).wait()

            for c in range(count):
                tile_out[slot, c] = total[:, c * own : (c + 1) * own].astype(BF16)
            put_tile(slot, (d, k), chunk, count).start()

        @pl.when(jnp.logical_not(leaving))
        def _():
            for c in range(count):
                kept_ref[chunk + c, span(k * tile, tile), :] = total[
                    :, c * own : (c + 1) * own
                ].astype(BF16)

    def tile_row(index):
        return lax.rem(x + 1 + index // per, copies) * per + index % per

    last = per * (copies - 1)

    def settle(chunk, count):
        for index in range(max(0, last - 2), last):
            put_tile(index % 2, (index // per, index % per), chunk, count).wait()
        return [
            [
                send(leave_ref.at[d - 1, chunk + c], got_x_ref.at[d - 1, chunk + c], twins[d - 1])
                for d in range(1, copies)
            ]
            for c in range(count)
        ]

    def out_tile(index, carry):
        lanes = span(tile_row(index) * tile, tile)
        left = ga_ref[:, :, lanes].reshape(rows, tile)
        store_tile(index, dot(left, heads_ref[...], TN), 0, 1)
        return carry

    lax.fori_loop(0, last, out_tile, 0)
    crossing = settle(0, 1)
    lax.fori_loop(last, last + per, out_tile, 0)

    def turn_back(grad, at):
        grad = grad.astype(BF16).astype(F32)
        back = grad * cos_ref[at] - pltpu.roll(grad, HEAD_DIM // 2, 1) * sin_ref[at]
        return back.astype(BF16)

    for head in range(heads):
        lanes = slice(head * HEAD_DIM, (head + 1) * HEAD_DIM)
        for block in reversed(range(blocks)):
            length = (block + 1) * QBLOCK
            at = slice(block * QBLOCK, length)
            query, keys, grad = q_ref[at, lanes], k_ref[:length, lanes], go_ref[at, lanes]
            scores = masked_scores(query, keys, first_ref[at], block, length)
            probs = jnp.exp(scores - log_ref[at, head : head + 1])
            grad_probs = dot(grad, v_ref[:length, lanes], NT)
            inner = jnp.sum(probs * grad_probs, -1, keepdims=True)
            grad_scores = (probs * (grad_probs - inner)).astype(BF16)
            dq = dot(grad_scores, keys, NN) * HEAD_DIM**-0.5
            gp_ref[at, lanes] = turn_back(dq, at)
            dk = dot(grad_scores, query, TN)
            dv = dot(probs.astype(BF16), grad, TN)
            if block == blocks - 1:
                dk_ref[...] = dk
                dv_ref[...] = dv
            else:
                dk_ref[:length] += dk
                dv_ref[:length] += dv
        gp_ref[:, own + head * HEAD_DIM : own + (head + 1) * HEAD_DIM] = turn_back(
            dk_ref[...] * HEAD_DIM**-0.5, slice(None)
        )
        gp_ref[:, 2 * own + head * HEAD_DIM : 2 * own + (head + 1) * HEAD_DIM] = dv_ref[
            ...
        ].astype(BF16)

    ga_y.wait_send()
    ga_y_core.wait_send()

    def norm1_part(s):
        at = span(s * share, share)
        for lanes in (slice(0, width // 2), slice(width // 2, width)):
            total = dot(gp_ref[at, :own], w_ref[0, lanes, :], NT)
            total += dot(gp_ref[at, own : 2 * own], w_ref[1, lanes, :], NT)
            total += dot(gp_ref[at, 2 * own :], w_ref[2, lanes, :], NT)
            part_ref[:, lanes] = total

    norm1_part(t ^ 3)
    ga_ref[0] = part_ref[...].astype(BF16)
    core_pass = send(ga_ref.at[0], got_core_ref.at[0], core)
    norm1_part(t ^ 1)
    ga_ref[1] = part_ref[...].astype(BF16)
    core_own = send(ga_ref.at[1], got_core_ref.at[1], core)
    norm1_part(t ^ 2)
    core_pass.wait_recv()
    ga_ref[2] = (part_ref[...] + got_core_ref[0].astype(F32)).astype(BF16)
    y_own = send(ga_ref.at[2], got_y_ref, y_side)
    norm1_part(t)

    mixed_y.wait_recv()
    mixed_y_core = send(mixed_ref.at[t ^ 2], mixed_ref.at[t ^ 2], core)

    def fetch(index, slot):
        lanes = span(tile_row(index) * tile, tile)
        return pltpu.make_async_copy(n1_ref.at[:, lanes], tile_in.at[slot], tile_sems.at[slot])

    fetch(0, 0).start()

    def qkv_tile(index, carry):
        slot = index % 2
        fetch(index, slot).wait()

        @pl.when(index < last + per - 1)
        def _():
            fetch(index + 1, 1 - slot).start()

        store_tile(index, dot(tile_in[slot], gp_ref[...], TN), 1, 3)
        return carry

    lax.fori_loop(0, last, qkv_tile, 0)
    crossing += settle(1, 3)
    lax.fori_loop(last, last + per, qkv_tile, 0)

    for copy in ups:
        copy.wait_recv()
    up_far = fold(1, up_ref, got_up_ref, up_own_ref, up_got_ref)

    def first_step(chunk):
        for copy in crossing[chunk]:
            copy.wait_recv()

        def total(index):
            at = span(index * part, part)
            value = kept_ref[chunk, at, :].astype(F32)
            for d in range(copies - 1):
                value += got_x_ref[d, chunk, at, :].astype(F32)
            return value

        z_send[chunk, 1] = total(z ^ 3).astype(BF16)
        one = send(z_send.at[chunk, 1], got_z1.at[chunk, 1], near)
        z_send[chunk, 0] = total(z ^ 1).astype(BF16)
        two = send(z_send.at[chunk, 0], got_z1.at[chunk, 0], near)
        z_kept[chunk] = total(z ^ 2)
        sums_ref[chunk] = total(z)
        return one, two

    def second_step(chunk, pair):
        one, two = pair
        one.wait_recv()
        one.wait_send()
        begun[:] = [copy for copy in begun if copy is not one]
        z_send[chunk, 1] = (z_kept[chunk] + got_z1[chunk, 1].astype(F32)).astype(BF16)
        gone = send(z_send.at[chunk, 1], got_z2.at[chunk], far)
        two.wait_recv()
        sums_ref[chunk] += got_z1[chunk, 0].astype(F32)
        return gone

    def third_step(chunk, gone):
        gone.wait_recv()
        sums_ref[chunk] += got_z2[chunk].astype(F32)

    core_own.wait_recv()
    y_own.wait_recv()
    small_ref[...] = small_in_ref[...]
    lines = 64
    count = small_in_ref.shape[0] - 2

    def finish(j, carry):
        at = span(j * lines, lines)
        grad = part_ref[at, :] + got_core_ref[1, at, :].astype(F32) + got_y_ref[at, :].astype(F32)
        hat, inverse = norm_parts(tokens_ref[at, :].astype(F32))
        back, gain_grad, bias_grad = norm_backward(grad, hat, inverse, gain1_ref[...])
        tg_own_ref[at, :] = (gx2_ref[at, :] + back).astype(BF16)
        small_ref[count : count + 1, :] += gain_grad[None, :]
        small_ref[count + 1 : count + 2, :] += bias_grad[None, :]
        return carry

    lax.fori_loop(0, share // lines, finish, 0)
    tg_y = send(tg_own_ref, tg_ref.at[t], y_side)
    tg_core = send(tg_own_ref, tg_ref.at[t], core)
    tg_own = pltpu.make_async_copy(tg_own_ref, tg_ref.at[t], local_sems.at[2])
    tg_own.start()

    for step, devices in enumerate(([core], [y_side], [near], [far], twins)):
        small_send[step] = small_ref[...]
        exchanged = [
            send(small_send.at[step], got_small.at[step + d], device)
            for d, device in enumerate(devices)
        ]
        for d, copy in enumerate(exchanged):
            copy.wait_recv()
            small_ref[...] += got_small[step + d]
        if step == 1:
            out_first = first_step(0)
        if step == 3:
            out_second = second_step(0, out_first)

    tg_y.wait_recv()
    tg_y_core = send(tg_ref.at[t ^ 2], tg_ref.at[t ^ 2], core)
    firsts = {1: first_step(1)}
    third_step(0, out_second)
    firsts[2] = first_step(2)
    seconds = {1: second_step(1, firsts[1])}
    firsts[3] = first_step(3)
    seconds[2] = second_step(2, firsts[2])
    third_step(1, seconds[1])
    seconds[3] = second_step(3, firsts[3])
    third_step(2, seconds[2])
    third_step(3, seconds[3])
    for copy in (core_own, mixed_core, mixed_y_core, tg_core, tg_y_core, down_far, up_far):
        if copy is not core_own:
            copy.wait_recv()
    for copy in (mixed_own, tg_own):
        copy.wait()
    for copy in begun:
        if copy is not ga_y and copy is not ga_y_core:
            copy.wait_send()


def back_call(
    queries, keys, values, heads, logs, first, keep, tables_, w_out, w3, gain1, tokens_own,
    grad_middle, small, grad_own, mixed_own, normed1, down_part, got_down, up_part,
):
    rows, own = queries.shape
    share, width = grad_own.shape
    copies, owners = lax.axis_size("dp"), lax.axis_size("bucket")
    splits = rows // share
    reach = width // copies
    part = reach // owners
    half = down_part.shape[1] // 2
    inside = pl.BlockSpec(memory_space=pltpu.VMEM)
    outside = pl.BlockSpec(memory_space=pl.ANY)
    shape = jax.ShapeDtypeStruct
    dma = lambda *count: pltpu.SemaphoreType.DMA(count)
    vmem = lambda dtype, *size: pltpu.VMEM(size, dtype)
    others = copies - 1
    few = 128
    sends = 3 + 3 + 3 + 2 + 3 + 12 + 4 + 6 * others
    return pl.pallas_call(
        functools.partial(back_kernel, copies),
        in_specs=[inside] * 15 + [outside] * 6,
        out_specs=[inside] * 2 + [outside] * 8,
        out_shape=[
            shape((4, part, own), F32),
            shape(small.shape, F32),
            shape((splits, share, width), BF16),
            shape((splits, share, width), BF16),
            shape((reach, half), F32),
            shape((reach, half), BF16),
            shape((reach, half), F32),
            shape((reach, half), BF16),
            shape((others, reach, 2 * half), BF16),
            shape((others, 4, reach, own), BF16),
        ],
        scratch_shapes=[
            vmem(BF16, splits, share, width),
            vmem(BF16, rows, own),
            vmem(BF16, rows, 3 * own),
            vmem(F32, rows, HEAD_DIM),
            vmem(F32, rows, HEAD_DIM),
            vmem(BF16, 2, share, width),
            vmem(BF16, share, width),
            vmem(F32, share, width),
            vmem(BF16, share, width),
            vmem(BF16, 2, rows, 256),
            vmem(BF16, 2, 3, 256, own),
            vmem(BF16, 2, few, 2 * half),
            vmem(BF16, 2, others, few, 2 * half),
            vmem(BF16, 2, reach, half),
            vmem(F32, 2, few, half),
            vmem(BF16, 4, reach, own),
            vmem(BF16, others, 4, reach, own),
            vmem(BF16, 4, 2, part, own),
            vmem(F32, 4, part, own),
            vmem(BF16, 4, 2, part, own),
            vmem(BF16, 4, part, own),
            vmem(F32, 4 + others, *small.shape),
            vmem(F32, 5, *small.shape),
            dma(sends),
            dma(sends),
            dma(3),
            dma(2),
            dma(2),
            dma(copies, 2),
            dma(2),
        ],
        compiler_params=pltpu.CompilerParams(
            vmem_limit_bytes=62 << 20, collective_id=2, has_side_effects=True
        ),
        cost_estimate=pl.CostEstimate(
            flops=16 * rows * width * own + 10 * rows * rows * own,
            bytes_accessed=80 << 20,
            transcendentals=rows * rows * own // HEAD_DIM,
        ),
        name="back",
    )(
        queries, keys, values, heads, logs, first, keep, *tables_, w_out, w3, gain1, tokens_own,
        grad_middle, small, grad_own, mixed_own, normed1, down_part, got_down, up_part,
    )


def swap(values, axis, bit):
    pairs = [(i, i ^ bit) for i in range(lax.axis_size(axis))]
    return lax.ppermute(values, axis, pairs)


def local(
    tokens,
    cotangent,
    lengths,
    head_quarters,
    buckets,
    ln1_gain,
    ln1_bias,
    w_qkv,
    w_out,
    ln2_gain,
    ln2_bias,
    w_router,
    w_up,
    w_down,
):
    tok_rows, model_width = tokens.shape
    owners = lax.axis_size("bucket")
    splits = lax.axis_size("tensor")
    copies = lax.axis_size("dp")
    share = tok_rows // splits
    t, z, x = lax.axis_index("tensor"), lax.axis_index("bucket"), lax.axis_index("dp")
    up_own = w_up.reshape(model_width, -1)
    down_own = w_down.reshape(-1, model_width)
    hidden_width = up_own.shape[1]

    levels = buckets[:, 0].astype(F32).reshape(-1, HEAD_DIM)
    near_levels = swap(levels, "bucket", 1)

    def shard(values, bit):
        return lax.dynamic_slice_in_dim(values, (t ^ bit) * share, share, 0)

    positions, first = layout(lengths[0], tok_rows)
    first = first[:, None]
    keep = (t < head_quarters).astype(F32)[:, None]
    cosine, sine = tables(positions)
    w3 = jnp.transpose(w_qkv, (1, 0, 2))
    (
        normed1,
        queries,
        keys,
        values,
        heads_low,
        logs,
        middle,
        n2,
        up_other,
        down_other,
        cotangents,
    ) = front_call(
        tokens,
        (ln1_gain.reshape(1, -1), ln1_bias.reshape(1, -1)),
        w3,
        (cosine, sine),
        first,
        keep,
        w_out,
        (ln2_gain.reshape(1, -1), ln2_bias.reshape(1, -1)),
        up_own,
        down_own,
        cotangent,
    )
    level_all = jnp.concatenate([levels.reshape(-1), near_levels.reshape(-1)], 0)[:, None]
    (
        mixed_own,
        grad_middle,
        grad_attention_own,
        small,
        _,
        down_part,
        up_part,
        got_down,
    ) = middle_call(
        n2,
        cotangents,
        (up_own, up_other),
        (down_own, down_other),
        w_router,
        level_all,
        middle,
        (ln2_gain.reshape(1, -1), ln2_bias.reshape(1, -1)),
    )
    sums, small, mixed, tokens_grad, down_own, down_got, up_own, up_got, _, _ = back_call(
        queries,
        keys,
        values,
        heads_low,
        logs,
        first,
        keep,
        (cosine, sine),
        w_out,
        w3,
        ln1_gain.reshape(1, -1),
        shard(tokens, 0),
        grad_middle,
        jnp.concatenate([small, jnp.zeros((2, model_width), F32)], 0),
        grad_attention_own,
        mixed_own,
        normed1,
        down_part,
        got_down,
        up_part,
    )
    grad_down = (down_own + down_got.astype(F32)).T
    grad_up = up_own + up_got.astype(F32)
    width = model_width // (copies * owners)
    small = lax.dynamic_slice_in_dim(small, (x * owners + z) * width, width, 1)
    return (
        mixed.reshape(tok_rows, model_width),
        tokens_grad.reshape(tok_rows, model_width).astype(F32),
        small[2 + owners],
        small[3 + owners],
        jnp.transpose(sums[1:], (1, 0, 2)),
        sums[0].T,
        small[0],
        small[1],
        small[2 : 2 + owners].T,
        grad_up.reshape(-1, 1, hidden_width),
        grad_down.reshape(1, hidden_width, -1),
    )


def solution(mesh):
    placed = (
        P(("dp", "bucket"), None),
        P(("dp", "bucket"), None),
        P(("dp", "bucket"), None),
        P(("dp", "bucket")),
        P(("dp", "bucket"), None),
        P(),
        P(),
        P(None, None, "tensor"),
        P("tensor", None),
        P(),
        P(),
        P(),
        P(None, "bucket", "tensor"),
        P("bucket", "tensor", None),
    )
    return jax.shard_map(
        local,
        mesh=mesh,
        in_specs=placed,
        out_specs=(
            P(("dp", "bucket"), None),
            P(("dp", "bucket"), None),
            P(("dp", "bucket")),
            P(("dp", "bucket")),
            P(("dp", "bucket"), None, "tensor"),
            P("tensor", ("dp", "bucket")),
            P(("dp", "bucket")),
            P(("dp", "bucket")),
            P(("dp", "bucket"), None),
            P("dp", "bucket", "tensor"),
            P("bucket", "tensor", "dp"),
        ),
        check_vma=False,
    )
```

```python
import functools
import math

import jax
import jax.numpy as jnp
from jax import lax
from jax.experimental import pallas as pl
from jax.experimental.pallas import tpu as pltpu
from jax.sharding import PartitionSpec as P

HEAD_DIM = 128
QBLOCK = 256
EPS = 1e-05
HIGH = lax.Precision.HIGHEST
NEGATIVE = -1e30
F32 = jnp.float32
BF16 = jnp.bfloat16


def norm_parts(values):
    centred = values - jnp.mean(values, -1, keepdims=True)
    inverse = lax.rsqrt(jnp.mean(centred * centred, -1, keepdims=True) + EPS)
    return centred * inverse, inverse


def norm_backward(grad_in, normed, inverse, gain):
    scaled = grad_in * gain
    inner = (
        scaled
        - jnp.mean(scaled, -1, keepdims=True)
        - normed * jnp.mean(scaled * normed, -1, keepdims=True)
    )
    return inverse * inner, jnp.sum(grad_in * normed, 0), jnp.sum(grad_in, 0)


def layout(lengths_row, tok_rows):
    ends = jnp.cumsum(lengths_row)
    starts = ends - lengths_row
    tok_index = jnp.arange(tok_rows, dtype=jnp.int32)
    segments = jnp.sum((tok_index[:, None] >= ends[None, :]).astype(jnp.int32), 1)
    chosen = segments[:, None] == jnp.arange(lengths_row.shape[0], dtype=jnp.int32)[None, :]
    return jnp.sum(jnp.where(chosen, starts[None, :], 0), 1)


def dot(left, right, dims):
    return lax.dot_general(left, right, (dims, ((), ())), preferred_element_type=F32)


NN = ((1,), (0,))
NT = ((1,), (1,))
TN = ((0,), (0,))


def masked_scores(query, keys, first, block, length):
    scores = dot(query, keys, NT) * HEAD_DIM**-0.5
    key_at = lax.broadcasted_iota(jnp.int32, (QBLOCK, length), 1)
    row_at = lax.broadcasted_iota(jnp.int32, (QBLOCK, length), 0) + block * QBLOCK
    allowed = (key_at >= first) & (key_at <= row_at)
    return jnp.where(allowed, scores, NEGATIVE)


class Copies:
    def __init__(self, send_sems, recv_sems):
        self.send_sems, self.recv_sems, self.used = send_sems, recv_sems, 0

    def make(self, source, target, device):
        slot = self.used
        self.used += 1
        return pltpu.make_async_remote_copy(
            src_ref=source,
            dst_ref=target,
            send_sem=self.send_sems.at[slot],
            recv_sem=self.recv_sems.at[slot],
            device_id=device,
            device_id_type=pl.DeviceIdType.MESH,
        )

    def start(self, source, target, device):
        copy = self.make(source, target, device)
        copy.start()
        return copy


def meet(devices):
    barrier = pltpu.get_barrier_semaphore()
    for device in devices:
        pl.semaphore_signal(barrier, inc=1, device_id=device, device_id_type=pl.DeviceIdType.MESH)
    pl.semaphore_wait(barrier, len(devices))


def front_kernel(
    copies,
    gain1_ref,
    bias1_ref,
    first_ref,
    keep_ref,
    gain2_ref,
    bias2_ref,
    tokens_in,
    w_in,
    w_out_in,
    up_ref,
    down_ref,
    cot_ref,
    level_ref,
    log_ref,
    middle_ref,
    cos_ref,
    sin_ref,
    n1_out,
    q_out,
    k_out,
    v_out,
    heads_out,
    n2_ref,
    up_other_ref,
    down_other_ref,
    near_cot_ref,
    near_level_ref,
    tokens_ref,
    w_ref,
    w_out_ref,
    n1_ref,
    q_ref,
    k_ref,
    v_ref,
    heads_ref,
    away_ref,
    got_core_ref,
    pass_ref,
    got_y_ref,
    own_ref,
    send_sems,
    recv_sems,
    in_sems,
    out_sems,
):
    t, z, x = lax.axis_index("tensor"), lax.axis_index("bucket"), lax.axis_index("dp")
    rows, own = q_ref.shape
    share = own_ref.shape[0]
    heads = own // HEAD_DIM
    blocks = rows // QBLOCK
    core, y_side = {"tensor": t ^ 1}, {"tensor": t ^ 2}
    near, far = {"bucket": z ^ 1}, {"bucket": z ^ 2}
    twins = [{"dp": lax.rem(x + d, copies)} for d in range(1, copies)]

    def token_block(i):
        at = pl.ds(pl.multiple_of(i * QBLOCK, QBLOCK), QBLOCK)
        return pltpu.make_async_copy(tokens_in.at[at], tokens_ref.at[at], in_sems.at[i])

    w_copies = [
        pltpu.make_async_copy(w_in.at[part], w_ref.at[part], in_sems.at[blocks + part])
        for part in range(3)
    ]
    w_out_copy = pltpu.make_async_copy(w_out_in, w_out_ref, in_sems.at[blocks + 3])
    token_block(0).start()
    for copy in w_copies:
        copy.start()
    for i in range(1, blocks):
        token_block(i).start()
    w_out_copy.start()

    meet([core, y_side, near, far] + twins)
    links = Copies(send_sems, recv_sems)
    begun = []

    def send(source, target, device):
        copy = links.start(source, target, device)
        begun.append(copy)
        return copy

    def piece(ref, quarter):
        size = ref.shape[0] // copies // 4
        return ref.at[pl.ds(pl.multiple_of((x * 4 + quarter) * size, 16), size)]

    def fetch(ref, other_ref, quarter):
        return send(piece(ref, quarter), piece(other_ref, quarter), far)

    onward = []

    def pass_on(copy, ref, devices):
        copy.wait_recv()
        onward.extend(send(ref, ref, device) for device in devices)

    few = share // 4

    def cot_rows(ref, s, chunk):
        return ref.at[s, pl.ds(chunk * few, few)]

    cots = [
        send(cot_rows(cot_ref, t, chunk), cot_rows(near_cot_ref, t, chunk), near)
        for chunk in range(4)
    ]
    up_copies = [fetch(up_ref, up_other_ref, quarter) for quarter in range(4)]
    near_level = send(level_ref, near_level_ref, near)
    cots_y = []

    def pass_cots(chunk):
        cots[chunk].wait_recv()
        rows_here = cot_rows(near_cot_ref, t, chunk)
        cots_y.append(send(rows_here, rows_here, y_side))
        onward.append(send(rows_here, rows_here, core))

    half = HEAD_DIM // 2
    lane = lax.broadcasted_iota(jnp.int32, (1, HEAD_DIM), 1)
    freq = jnp.exp((lane % half).astype(F32) * (-math.log(10000.0) / half))
    side = jnp.where(lane < half, -1.0, 1.0)

    def project(i, carry):
        at = pl.ds(pl.multiple_of(i * QBLOCK, QBLOCK), QBLOCK)
        token_block(i).wait()
        normed, _ = norm_parts(tokens_ref[at, :].astype(F32))
        low = (normed * gain1_ref[...] + bias1_ref[...]).astype(BF16)
        n1_ref[at, :] = low
        token = lax.broadcasted_iota(jnp.int32, (QBLOCK, 1), 0) + i * QBLOCK
        angle = (token - first_ref[at, :]).astype(F32) * freq
        cosine, sine = jnp.cos(angle), jnp.sin(angle) * side
        cos_ref[at, :] = cosine
        sin_ref[at, :] = sine
        for part, out_ref in enumerate((q_ref, k_ref, v_ref)):

            @pl.when(i == 0)
            def _():
                w_copies[part].wait()

            projected = dot(low, w_ref[part], NN)
            if part == 2:
                out_ref[at, :] = projected.astype(BF16)
                continue
            for start in range(0, own, HEAD_DIM):
                head = projected[:, start : start + HEAD_DIM]
                turned = head * cosine + pltpu.roll(head, half, 1) * sine
                out_ref[at, start : start + HEAD_DIM] = turned.astype(BF16)
        return carry

    lax.fori_loop(0, blocks, project, 0)
    outs = [
        pltpu.make_async_copy(ref, out, out_sems.at[i])
        for i, (ref, out) in enumerate(
            ((n1_ref, n1_out), (q_ref, q_out), (k_ref, k_out), (v_ref, v_out), (heads_ref, heads_out))
        )
    ]
    for copy in outs[:4]:
        copy.start()

    for head in range(heads):
        lanes = slice(head * HEAD_DIM, (head + 1) * HEAD_DIM)
        for block in range(rows // QBLOCK):
            length = (block + 1) * QBLOCK
            at = slice(block * QBLOCK, length)
            scores = masked_scores(
                q_ref[at, lanes], k_ref[:length, lanes], first_ref[at], block, length
            )
            most = jnp.max(scores, -1, keepdims=True)
            expo = jnp.exp(scores - most)
            total = jnp.sum(expo, -1, keepdims=True)
            weights = (expo * (1.0 / total)).astype(BF16)
            out = dot(weights, v_ref[:length, lanes], NN)
            heads_ref[at, lanes] = (out * keep_ref[at]).astype(BF16)
            log_ref[at, head : head + 1] = most + jnp.log(total)
        if head < 4:
            pass_cots(head)

    for chunk in range(heads, 4):
        pass_cots(chunk)
    outs[4].start()
    w_out_copy.wait()

    def attended(index):
        at = pl.ds(pl.multiple_of(index * share, share), share)
        return dot(heads_ref[at, :], w_out_ref[...], NN)

    away_ref[1] = attended(t ^ 3).astype(BF16)
    to_core1 = send(away_ref.at[1], got_core_ref.at[1], core)
    away_ref[0] = attended(t ^ 1).astype(BF16)
    to_core0 = send(away_ref.at[0], got_core_ref.at[0], core)
    passed = attended(t ^ 2)
    to_core1.wait_recv()
    pass_ref[...] = (passed + got_core_ref[1].astype(F32)).astype(BF16)
    to_y = send(pass_ref, got_y_ref, y_side)
    middle = attended(t)
    middle += tokens_ref[pl.ds(pl.multiple_of(t * share, share), share), :].astype(F32)
    to_core0.wait_recv()
    middle_ref[...] = middle + got_core_ref[0].astype(F32)

    for chunk, copy in enumerate(cots_y):
        pass_on(copy, cot_rows(near_cot_ref, t ^ 2, chunk), [core])
    down_copies = []
    for quarter, copy in enumerate(up_copies):
        pass_on(copy, piece(up_other_ref, quarter), twins)
        if quarter >= 2:
            down_copies.append(fetch(down_ref, down_other_ref, quarter - 2))
    to_y.wait_recv()
    total = middle_ref[...] + got_y_ref[...].astype(F32)
    middle_ref[...] = total
    normed, _ = norm_parts(total)
    own_ref[...] = (normed * gain2_ref[...] + bias2_ref[...]).astype(BF16)
    keep_own = pltpu.make_async_copy(own_ref, n2_ref.at[0, t], in_sems.at[0])
    keep_own.start()
    to_near = send(own_ref, n2_ref.at[1, t], near)
    own_y = send(own_ref, n2_ref.at[0, t], y_side)
    own_core = send(own_ref, n2_ref.at[0, t], core)
    down_copies += [fetch(down_ref, down_other_ref, quarter) for quarter in (2, 3)]
    own_y.wait_recv()
    y_core = send(n2_ref.at[0, t ^ 2], n2_ref.at[0, t ^ 2], core)
    to_near.wait_recv()
    near_y = send(n2_ref.at[1, t], n2_ref.at[1, t], y_side)
    near_core = send(n2_ref.at[1, t], n2_ref.at[1, t], core)
    for quarter in (0, 1):
        pass_on(down_copies[quarter], piece(down_other_ref, quarter), twins)
    pass_on(down_copies[2], piece(down_other_ref, 2), twins)
    near_y.wait_recv()
    near_y_core = send(n2_ref.at[1, t ^ 2], n2_ref.at[1, t ^ 2], core)
    pass_on(down_copies[3], piece(down_other_ref, 3), twins)
    keep_own.wait()
    for copy in outs:
        copy.wait()
    for copy in (near_level, own_core, y_core, near_core, near_y_core, *onward):
        copy.wait_recv()
    for copy in begun:
        copy.wait_send()


def front_call(tokens, ln1, w3, first, keep, w_out, ln2, up, down, cotangent, levels):
    rows, width = tokens.shape
    own = w3.shape[2]
    splits, copies = lax.axis_size("tensor"), lax.axis_size("dp")
    share = rows // splits
    inside = pl.BlockSpec(memory_space=pltpu.VMEM)
    outside = pl.BlockSpec(memory_space=pl.ANY)
    shape = jax.ShapeDtypeStruct
    vmem = lambda dtype, *size: pltpu.VMEM(size, dtype)
    total = 35 + 8 * (copies - 1)
    narrow = shape((rows, own), BF16)
    return pl.pallas_call(
        functools.partial(front_kernel, copies),
        in_specs=[inside] * 6 + [outside] * 7,
        out_specs=[inside] * 4 + [outside] * 10,
        out_shape=[
            shape((rows, own // HEAD_DIM), F32),
            shape((share, width), F32),
            shape((rows, HEAD_DIM), F32),
            shape((rows, HEAD_DIM), F32),
            shape((rows, width), BF16),
            narrow,
            narrow,
            narrow,
            narrow,
            shape((2, splits, share, width), BF16),
            shape(up.shape, BF16),
            shape(down.shape, BF16),
            shape((splits, share, width), BF16),
            shape(levels.shape, F32),
        ],
        scratch_shapes=[
            vmem(BF16, rows, width),
            vmem(BF16, *w3.shape),
            vmem(BF16, *w_out.shape),
            vmem(BF16, rows, width),
            vmem(BF16, rows, own),
            vmem(BF16, rows, own),
            vmem(BF16, rows, own),
            vmem(BF16, rows, own),
            vmem(BF16, 2, share, width),
            vmem(BF16, 2, share, width),
            vmem(BF16, share, width),
            vmem(BF16, share, width),
            vmem(BF16, share, width),
            pltpu.SemaphoreType.DMA((total,)),
            pltpu.SemaphoreType.DMA((total,)),
            pltpu.SemaphoreType.DMA((rows // QBLOCK + 4,)),
            pltpu.SemaphoreType.DMA((5,)),
        ],
        compiler_params=pltpu.CompilerParams(
            vmem_limit_bytes=56 << 20, collective_id=0, has_side_effects=True
        ),
        cost_estimate=pl.CostEstimate(
            flops=8 * rows * width * own + 4 * rows * rows * own,
            bytes_accessed=60 << 20,
            transcendentals=rows * rows * own // HEAD_DIM,
        ),
        name="front",
    )(*ln1, first, keep, *ln2, tokens, w3, w_out, up, down, cotangent, levels)


def block_at(i, t):
    late = i // 4
    near = (1 - late) * (1 - (i // 2) % 2) + late * (1 - i % 2)
    bit = (1 - late) * (3 - 2 * (i % 2)) + late * (2 - 2 * ((i % 4) // 2))
    return near, t ^ bit


def router_gate(rows, w_router_ref, level):
    logits = dot(rows, w_router_ref[...], NN)
    expo = jnp.exp(logits - jnp.max(logits, -1, keepdims=True))
    probs = expo / jnp.sum(expo, -1, keepdims=True)
    number = lax.broadcasted_iota(jnp.int32, probs.shape, 1).astype(F32)
    onehot = (number == level).astype(F32)
    return jnp.sum(probs * onehot, -1, keepdims=True), probs, onehot


def middle_kernel(
    copies,
    n2_ref,
    cot_ref,
    near_cot_ref,
    up_own_ref,
    up_other_ref,
    down_own_ref,
    down_other_ref,
    router_ref,
    level_ref,
    x2_ref,
    gain2_ref,
    bias2_ref,
    mixed_ref,
    gx2_ref,
    ga_ref,
    small_ref,
    gf_ref,
    grad_down_ref,
    grad_up_ref,
    got_x_ref,
    n2_in,
    cot_in,
    gf_out,
    hid_ref,
    gu_ref,
    part_f,
    part_g,
    hold_f,
    send_ref,
    core_f,
    core_g,
    got_fz,
    got_fy,
    got_gy,
    got_gz,
    tile_in,
    tile_out,
    core_send_sems,
    core_recv_sems,
    send_sems,
    recv_sems,
    in_sems,
    out_sems,
    tile_sems,
    tile_out_sems,
):
    t, z, x = lax.axis_index("tensor"), lax.axis_index("bucket"), lax.axis_index("dp")
    share, width = gx2_ref.shape
    half = up_own_ref.shape[1]
    core, y_side, near = {"tensor": t ^ 1}, {"tensor": t ^ 2}, {"bucket": z ^ 1}
    twins = [{"dp": lax.rem(x + d, copies)} for d in range(1, copies)]
    splits = n2_ref.shape[1]

    def load(i, slot):
        at, s = block_at(i, t)
        return pltpu.make_async_copy(n2_ref.at[at, s], n2_in.at[slot], in_sems.at[slot, 0])

    def load_cot(i, slot, act):
        at, s = block_at(i, t)
        for index, ref in enumerate((cot_ref, near_cot_ref)):

            @pl.when(at == index)
            def _():
                act(pltpu.make_async_copy(ref.at[s], cot_in.at[slot], in_sems.at[slot, 1]))

    def store(i, slot):
        at, s = block_at(i, t)
        return pltpu.make_async_copy(gf_out.at[slot], gf_ref.at[at, s], out_sems.at[slot])

    def to_core(i):
        return [
            pltpu.make_async_remote_copy(
                src_ref=send_ref.at[kind * 2 + i % 2],
                dst_ref=(core_f, core_g)[kind].at[i],
                send_sem=core_send_sems.at[kind, i],
                recv_sem=core_recv_sems.at[kind, i],
                device_id=core,
                device_id_type=pl.DeviceIdType.MESH,
            )
            for kind in (0, 1)
        ]

    load(0, 0).start()
    load_cot(0, 0, lambda copy: copy.start())
    meet([core, y_side, near] + twins)
    links = Copies(send_sems, recv_sems)
    f_near_y = links.make(send_ref.at[0], got_fz.at[0], near)
    g_near_y = links.make(send_ref.at[1], got_gy.at[0], y_side)
    g_own_y = links.make(send_ref.at[2], got_gy.at[1], y_side)
    f_near = links.make(send_ref.at[3], got_fz.at[1], near)
    f_own_y = links.make(send_ref.at[0], got_fy, y_side)
    g_near = links.make(send_ref.at[1], got_gz, near)

    def work(i, carry):
        slot = i % 2
        at, s = block_at(i, t)
        load(i, slot).wait()
        load_cot(i, slot, lambda copy: copy.wait())

        @pl.when(i < 7)
        def _():
            load(i + 1, 1 - slot).start()
            load_cot(i + 1, 1 - slot, lambda copy: copy.start())

        @pl.when(i >= 2)
        def _():
            store(i - 2, slot).wait()

        spot = pl.ds(pl.multiple_of((at * splits + s) * share, share), share)
        rows = n2_in[slot]
        level = level_ref[spot, :]
        gate, _, _ = router_gate(rows, router_ref, level)
        grad = (gate * cot_in[slot].astype(F32)).astype(BF16)
        gf_out[slot] = grad
        store(i, slot).start()
        for part, (up_ref, down_ref, unit_level) in enumerate(
            ((up_own_ref, down_own_ref, z), (up_other_ref, down_other_ref, z ^ 2))
        ):
            lanes = slice(part * half, (part + 1) * half)
            kept = level >= unit_level.astype(F32)
            act = jnp.where(kept, jnp.maximum(dot(rows, up_ref[...], NN), 0.0), 0.0)
            hid_ref[spot, lanes] = (act * act).astype(BF16)
            back = dot(grad, down_ref[...], NT)
            gu_ref[spot, lanes] = (back * 2.0 * act).astype(BF16)
        for lanes in (slice(0, width // 2), slice(width // 2, width)):
            part_f[:, lanes] = dot(hid_ref[spot, :half], down_own_ref[:, lanes], NN) + dot(
                hid_ref[spot, half:], down_other_ref[:, lanes], NN
            )
            part_g[:, lanes] = dot(gu_ref[spot, :half], up_own_ref[lanes, :], NT) + dot(
                gu_ref[spot, half:], up_other_ref[lanes, :], NT
            )

        @pl.when(i < 4)
        def _():
            @pl.when(i >= 2)
            def _():
                for copy in to_core(i - 2):
                    copy.wait_send()

            send_ref[slot] = part_f[...].astype(BF16)
            send_ref[2 + slot] = part_g[...].astype(BF16)
            for copy in to_core(i):
                copy.start()

        def with_core(kind, at_i):
            to_core(at_i)[kind].wait_recv()
            got = (core_f, core_g)[kind][at_i].astype(F32)
            return (part_f, part_g)[kind][...] + got

        @pl.when(i == 4)
        def _():
            for j in (2, 3):
                for copy in to_core(j):
                    copy.wait_send()
            send_ref[1] = with_core(1, 0).astype(BF16)
            g_near_y.start()
            send_ref[0] = with_core(0, 0).astype(BF16)
            f_near_y.start()

        @pl.when(i == 5)
        def _():
            send_ref[2] = with_core(1, 2).astype(BF16)
            g_own_y.start()
            hold_f[...] = with_core(0, 2)

        @pl.when(i == 6)
        def _():
            send_ref[3] = with_core(0, 1).astype(BF16)
            f_near.start()
            gx2_ref[...] = with_core(1, 1)

        @pl.when(i == 7)
        def _():
            part_f[...] = with_core(0, 3)
            part_g[...] = with_core(1, 3)

        return carry

    lax.fori_loop(0, 8, work, 0)
    store(6, 0).wait()
    store(7, 1).wait()

    tile = tile_in.shape[-1]
    tiles = width // tile

    def weight_grads(source_ref, right_ref, result_ref):
        def fetch(j, slot):
            lanes = pl.ds(pl.multiple_of(j * tile, tile), tile)
            return pltpu.make_async_copy(
                source_ref.at[:, :, :, lanes], tile_in.at[slot], tile_sems.at[slot]
            )

        def put(j, slot):
            rows = pl.ds(pl.multiple_of(j * tile, tile), tile)
            return pltpu.make_async_copy(
                tile_out.at[slot], result_ref.at[rows, :], tile_out_sems.at[slot]
            )

        fetch(0, 0).start()

        def step(j, carry):
            slot = j % 2
            fetch(j, slot).wait()

            @pl.when(j < tiles - 1)
            def _():
                fetch(j + 1, 1 - slot).start()

            @pl.when(j >= 2)
            def _():
                put(j - 2, slot).wait()

            left = tile_in[slot].reshape(-1, tile)
            tile_out[slot] = dot(left, right_ref[...], TN).astype(BF16)
            put(j, slot).start()
            return carry

        lax.fori_loop(0, tiles, step, 0)
        put(tiles - 2, (tiles - 2) % 2).wait()
        put(tiles - 1, (tiles - 1) % 2).wait()

    weight_grads(gf_ref, hid_ref, grad_down_ref)
    size = width // copies
    downs = []
    for d in range(1, copies):
        part = pl.ds(pl.multiple_of(lax.rem(x + d, copies) * size, size), size)
        downs.append(
            links.start(grad_down_ref.at[part, :], got_x_ref.at[d - 1], twins[d - 1])
        )

    f_near_y.wait_recv()
    f_near_y.wait_send()
    send_ref[0] = (hold_f[...] + got_fz[0].astype(F32)).astype(BF16)
    f_own_y.start()
    g_near_y.wait_recv()
    g_near_y.wait_send()
    send_ref[1] = (gx2_ref[...] + got_gy[0].astype(F32)).astype(BF16)
    g_near.start()

    weight_grads(n2_ref, gu_ref, grad_up_ref)

    own = pltpu.make_async_copy(n2_ref.at[0, t], n2_in.at[0], in_sems.at[0, 0])
    own.start()
    own_cot = pltpu.make_async_copy(cot_ref.at[t], cot_in.at[0], in_sems.at[0, 1])
    own_cot.start()
    own.wait()
    own_cot.wait()
    for copy in (f_near, f_own_y, g_own_y, g_near):
        copy.wait_recv()
    small_ref[...] = jnp.zeros_like(small_ref)
    few = 64

    def finish(j, carry):
        at = pl.ds(pl.multiple_of(j * few, few), few)
        level = level_ref[pl.ds(pl.multiple_of(t * share + j * few, few), few), :]
        rows = n2_in[0, at, :]
        gate, probs, onehot = router_gate(rows, router_ref, level)
        branch = part_f[at, :] + got_fz[1, at, :].astype(F32) + got_fy[at, :].astype(F32)
        branch = branch.astype(BF16).astype(F32)
        x2 = x2_ref[at, :]
        mixed_ref[at, :] = (x2 + gate * branch).astype(BF16)
        grad_out = cot_in[0, at, :].astype(F32)
        grad_gate = jnp.sum(grad_out * branch, -1, keepdims=True)
        grad_logits = grad_gate * gate * (onehot - probs)
        returned = part_g[at, :] + got_gy[1, at, :].astype(F32) + got_gz[at, :].astype(F32)
        grad_n2 = returned.astype(BF16).astype(F32)
        grad_n2 += lax.dot_general(
            grad_logits,
            router_ref[...].astype(F32),
            (NT, ((), ())),
            precision=HIGH,
            preferred_element_type=F32,
        )
        hat, inverse = norm_parts(x2)
        back, gain_grad, bias_grad = norm_backward(grad_n2, hat, inverse, gain2_ref[...])
        gx2 = grad_out + back
        gx2_ref[at, :] = gx2
        ga_ref[at, :] = gx2.astype(BF16)
        small_ref[0:1, :] += gain_grad[None, :]
        small_ref[1:2, :] += bias_grad[None, :]
        small_ref[2 : 2 + probs.shape[1], :] += lax.dot_general(
            grad_logits, rows.astype(F32), (TN, ((), ())), precision=HIGH, preferred_element_type=F32
        )
        return carry

    lax.fori_loop(0, share // few, finish, 0)
    for copy in downs:
        copy.wait_recv()
    for copy in (g_own_y, f_near, f_own_y, g_near, *downs):
        copy.wait_send()


def middle_call(n2, cotangent, near_cotangent, ups, downs, w_router, levels, middle, ln2):
    _, splits, share, width = n2.shape
    copies = lax.axis_size("dp")
    half = ups[0].shape[1]
    rows = 2 * splits * share
    inside = pl.BlockSpec(memory_space=pltpu.VMEM)
    outside = pl.BlockSpec(memory_space=pl.ANY)
    shape = jax.ShapeDtypeStruct
    block = lambda count, dtype=BF16: pltpu.VMEM((*count, share, width), dtype)
    dma = lambda *count: pltpu.SemaphoreType.DMA(count)
    return pl.pallas_call(
        functools.partial(middle_kernel, copies),
        in_specs=[outside] * 3 + [inside] * 9,
        out_specs=[inside] * 4 + [outside] * 4,
        out_shape=[
            shape((share, width), BF16),
            shape((share, width), F32),
            shape((share, width), BF16),
            shape((2 + w_router.shape[1], width), F32),
            shape(n2.shape, BF16),
            shape((width, 2 * half), BF16),
            shape((width, 2 * half), BF16),
            shape((copies - 1, width // copies, 2 * half), BF16),
        ],
        scratch_shapes=[
            block((2,)),
            block((2,)),
            block((2,)),
            pltpu.VMEM((rows, 2 * half), BF16),
            pltpu.VMEM((rows, 2 * half), BF16),
            block((), F32),
            block((), F32),
            block((), F32),
            block((4,)),
            block((4,)),
            block((4,)),
            block((2,)),
            block(()),
            block((2,)),
            block(()),
            pltpu.VMEM((2, 2, splits, share, 256), BF16),
            pltpu.VMEM((2, 256, 2 * half), BF16),
            dma(2, 4),
            dma(2, 4),
            dma(6 + copies - 1),
            dma(6 + copies - 1),
            dma(2, 2),
            dma(2),
            dma(2),
            dma(2),
        ],
        compiler_params=pltpu.CompilerParams(
            vmem_limit_bytes=62 << 20, collective_id=1, has_side_effects=True
        ),
        cost_estimate=pl.CostEstimate(
            flops=12 * rows * width * 2 * half, bytes_accessed=80 << 20, transcendentals=0
        ),
        name="middle",
    )(n2, cotangent.reshape(splits, share, width), near_cotangent, *ups, *downs, w_router, levels, middle, *ln2)


def back_kernel(
    copies,
    log_ref,
    first_ref,
    keep_ref,
    cos_ref,
    sin_ref,
    w_out_ref,
    gain1_ref,
    tokens_ref,
    gx2_ref,
    small_in_ref,
    q_in,
    k_in,
    v_in,
    heads_in,
    w_in,
    ga_in_ref,
    mixed_in_ref,
    n1_ref,
    down_ref,
    got_down_ref,
    up_ref,
    sums_ref,
    small_ref,
    mixed_ref,
    tg_ref,
    down_own_ref,
    down_got_ref,
    up_own_ref,
    up_got_ref,
    got_up_ref,
    leave_ref,
    q_ref,
    k_ref,
    v_ref,
    heads_ref,
    w_ref,
    ga_ref,
    go_ref,
    gp_ref,
    dk_ref,
    dv_ref,
    got_core_ref,
    got_y_ref,
    part_ref,
    tg_own_ref,
    tile_in,
    tile_out,
    fold_a,
    fold_b,
    fold_send,
    fold_out,
    kept_ref,
    got_x_ref,
    z_send,
    z_kept,
    got_z1,
    got_z2,
    got_small,
    small_send,
    send_sems,
    recv_sems,
    local_sems,
    tile_sems,
    tile_out_sems,
    fold_sems,
    fold_out_sems,
    in_sems,
):
    t, z, x = lax.axis_index("tensor"), lax.axis_index("bucket"), lax.axis_index("dp")
    rows, own = q_ref.shape
    splits, share, width = ga_ref.shape
    heads, blocks = own // HEAD_DIM, rows // QBLOCK
    reach = width // copies
    part = got_z2.shape[1]
    core, y_side = {"tensor": t ^ 1}, {"tensor": t ^ 2}
    near, far = {"bucket": z ^ 1}, {"bucket": z ^ 2}
    twins = [{"dp": lax.rem(x + d, copies)} for d in range(1, copies)]
    meet([core, y_side, near, far] + twins)
    links = Copies(send_sems, recv_sems)
    begun = []

    def send(source, target, device):
        copy = links.start(source, target, device)
        begun.append(copy)
        return copy

    def span(start, size):
        return pl.ds(pl.multiple_of(start, size), size)

    ga_y = send(ga_in_ref, ga_ref.at[t], y_side)
    ga_core = send(ga_in_ref, ga_ref.at[t], core)
    ga_own = pltpu.make_async_copy(ga_in_ref, ga_ref.at[t], local_sems.at[0])
    ga_own.start()
    ups = [
        send(up_ref.at[span(lax.rem(x + d, copies) * reach, reach)], got_up_ref.at[d - 1], twins[d - 1])
        for d in range(1, copies)
    ]
    mixed_y = send(mixed_in_ref, mixed_ref.at[t], y_side)
    mixed_core = send(mixed_in_ref, mixed_ref.at[t], core)
    mixed_take = pltpu.make_async_copy(mixed_in_ref, tg_own_ref, local_sems.at[1])
    mixed_take.start()
    mixed_own = pltpu.make_async_copy(tg_own_ref, mixed_ref.at[t], local_sems.at[3])

    loaded = [
        pltpu.make_async_copy(source, target, in_sems.at[index])
        for index, (source, target) in enumerate(
            ((heads_in, heads_ref), (q_in, q_ref), (k_in, k_ref), (v_in, v_ref), (w_in, w_ref))
        )
    ]
    for copy in loaded:
        copy.start()

    few = fold_a.shape[1]
    half = fold_out.shape[2]

    def fold(which, source_ref, got_ref, own_ref, target_ref):
        def loads(k, slot):
            mine = pltpu.make_async_copy(
                source_ref.at[span(x * reach + k * few, few)], fold_a.at[slot], fold_sems.at[0, slot]
            )
            theirs = [
                pltpu.make_async_copy(
                    got_ref.at[d, span(k * few, few)], fold_b.at[slot, d], fold_sems.at[1 + d, slot]
                )
                for d in range(copies - 1)
            ]
            return [mine] + theirs

        def put(k, slot):
            return pltpu.make_async_copy(
                fold_out.at[slot], own_ref.at[span(k * few, few)], fold_out_sems.at[slot]
            )

        for copy in loads(0, 0):
            copy.start()
        steps = reach // few

        def step(k, carry):
            slot = k % 2
            for copy in loads(k, slot):
                copy.wait()

            @pl.when(k < steps - 1)
            def _():
                for copy in loads(k + 1, 1 - slot):
                    copy.start()

            @pl.when(k >= 2)
            def _():
                put(k - 2, slot).wait()

            total = fold_a[slot].astype(F32)
            for d in range(copies - 1):
                total += fold_b[slot, d].astype(F32)
            fold_out[slot] = total[:, :half]
            fold_send[which, span(k * few, few), :] = total[:, half:].astype(BF16)
            put(k, slot).start()
            return carry

        lax.fori_loop(0, steps, step, 0)
        for k in range(max(0, steps - 2), steps):
            put(k, k % 2).wait()
        return send(fold_send.at[which], target_ref, far)

    down_far = fold(0, down_ref, got_down_ref, down_own_ref, down_got_ref)

    def grad_heads(s):
        at = span(s * share, share)
        grad = dot(ga_ref[s], w_out_ref[...], NT).astype(BF16).astype(F32)
        go_ref[at, :] = (grad * keep_ref[at, :]).astype(BF16)

    ga_own.wait()
    grad_heads(t)
    mixed_take.wait()
    mixed_own.start()
    ga_core.wait_recv()
    grad_heads(t ^ 1)
    ga_y.wait_recv()
    ga_y_core = send(ga_ref.at[t ^ 2], ga_ref.at[t ^ 2], core)
    grad_heads(t ^ 2)
    ga_y_core.wait_recv()
    grad_heads(t ^ 3)

    tile = tile_in.shape[-1]
    per = reach // tile

    def put_tile(slot, place, chunk, count):
        d, k = place
        return pltpu.make_async_copy(
            tile_out.at[slot, pl.ds(0, count)],
            leave_ref.at[d, pl.ds(chunk, count), span(k * tile, tile)],
            tile_out_sems.at[slot],
        )

    def store_tile(index, total, chunk, count):
        slot = index % 2
        d, k = index // per, index % per
        leaving = index < per * (copies - 1)

        @pl.when(leaving)
        def _():
            @pl.when(index >= 2)
            def _():
                put_tile(slot, ((index - 2) // per, (index - 2) % per), chunk, count).wait()

            for c in range(count):
                tile_out[slot, c] = total[:, c * own : (c + 1) * own].astype(BF16)
            put_tile(slot, (d, k), chunk, count).start()

        @pl.when(jnp.logical_not(leaving))
        def _():
            for c in range(count):
                kept_ref[chunk + c, span(k * tile, tile), :] = total[
                    :, c * own : (c + 1) * own
                ].astype(BF16)

    def tile_row(index):
        return lax.rem(x + 1 + index // per, copies) * per + index % per

    last = per * (copies - 1)

    def settle(chunk, count):
        for index in range(max(0, last - 2), last):
            put_tile(index % 2, (index // per, index % per), chunk, count).wait()
        return [
            [
                send(leave_ref.at[d - 1, chunk + c], got_x_ref.at[d - 1, chunk + c], twins[d - 1])
                for d in range(1, copies)
            ]
            for c in range(count)
        ]

    def out_tile(index, carry):
        lanes = span(tile_row(index) * tile, tile)
        left = ga_ref[:, :, lanes].reshape(rows, tile)
        store_tile(index, dot(left, heads_ref[...], TN), 0, 1)
        return carry

    loaded[0].wait()
    lax.fori_loop(0, last, out_tile, 0)
    crossing = settle(0, 1)
    lax.fori_loop(last, last + per, out_tile, 0)

    for copy in loaded[1:]:
        copy.wait()

    def turn_back(grad, at):
        grad = grad.astype(BF16).astype(F32)
        back = grad * cos_ref[at] - pltpu.roll(grad, HEAD_DIM // 2, 1) * sin_ref[at]
        return back.astype(BF16)

    for head in range(heads):
        lanes = slice(head * HEAD_DIM, (head + 1) * HEAD_DIM)
        for block in reversed(range(blocks)):
            length = (block + 1) * QBLOCK
            at = slice(block * QBLOCK, length)
            query, keys, grad = q_ref[at, lanes], k_ref[:length, lanes], go_ref[at, lanes]
            scores = masked_scores(query, keys, first_ref[at], block, length)
            probs = jnp.exp(scores - log_ref[at, head : head + 1])
            grad_probs = dot(grad, v_ref[:length, lanes], NT)
            inner = jnp.sum(probs * grad_probs, -1, keepdims=True)
            grad_scores = (probs * (grad_probs - inner)).astype(BF16)
            dq = dot(grad_scores, keys, NN) * HEAD_DIM**-0.5
            gp_ref[at, lanes] = turn_back(dq, at)
            dk = dot(grad_scores, query, TN)
            dv = dot(probs.astype(BF16), grad, TN)
            if block == blocks - 1:
                dk_ref[...] = dk
                dv_ref[...] = dv
            else:
                dk_ref[:length] += dk
                dv_ref[:length] += dv
        gp_ref[:, own + head * HEAD_DIM : own + (head + 1) * HEAD_DIM] = turn_back(
            dk_ref[...] * HEAD_DIM**-0.5, slice(None)
        )
        gp_ref[:, 2 * own + head * HEAD_DIM : 2 * own + (head + 1) * HEAD_DIM] = dv_ref[
            ...
        ].astype(BF16)

    ga_y.wait_send()
    ga_y_core.wait_send()

    def norm1_part(s):
        at = span(s * share, share)
        for lanes in (slice(0, width // 2), slice(width // 2, width)):
            total = dot(gp_ref[at, :own], w_ref[0, lanes, :], NT)
            total += dot(gp_ref[at, own : 2 * own], w_ref[1, lanes, :], NT)
            total += dot(gp_ref[at, 2 * own :], w_ref[2, lanes, :], NT)
            part_ref[:, lanes] = total

    norm1_part(t ^ 3)
    ga_ref[0] = part_ref[...].astype(BF16)
    core_pass = send(ga_ref.at[0], got_core_ref.at[0], core)
    norm1_part(t ^ 1)
    ga_ref[1] = part_ref[...].astype(BF16)
    core_own = send(ga_ref.at[1], got_core_ref.at[1], core)
    norm1_part(t ^ 2)
    core_pass.wait_recv()
    ga_ref[2] = (part_ref[...] + got_core_ref[0].astype(F32)).astype(BF16)
    y_own = send(ga_ref.at[2], got_y_ref, y_side)
    norm1_part(t)

    mixed_y.wait_recv()
    mixed_y_core = send(mixed_ref.at[t ^ 2], mixed_ref.at[t ^ 2], core)

    def fetch(index, slot):
        lanes = span(tile_row(index) * tile, tile)
        return pltpu.make_async_copy(n1_ref.at[:, lanes], tile_in.at[slot], tile_sems.at[slot])

    fetch(0, 0).start()

    def qkv_tile(index, carry):
        slot = index % 2
        fetch(index, slot).wait()

        @pl.when(index < last + per - 1)
        def _():
            fetch(index + 1, 1 - slot).start()

        store_tile(index, dot(tile_in[slot], gp_ref[...], TN), 1, 3)
        return carry

    lax.fori_loop(0, last, qkv_tile, 0)
    crossing += settle(1, 3)
    lax.fori_loop(last, last + per, qkv_tile, 0)

    for copy in ups:
        copy.wait_recv()
    up_far = fold(1, up_ref, got_up_ref, up_own_ref, up_got_ref)

    def first_step(chunk):
        for copy in crossing[chunk]:
            copy.wait_recv()

        def total(index):
            at = span(index * part, part)
            value = kept_ref[chunk, at, :].astype(F32)
            for d in range(copies - 1):
                value += got_x_ref[d, chunk, at, :].astype(F32)
            return value

        z_send[chunk, 1] = total(z ^ 3).astype(BF16)
        one = send(z_send.at[chunk, 1], got_z1.at[chunk, 1], near)
        z_send[chunk, 0] = total(z ^ 1).astype(BF16)
        two = send(z_send.at[chunk, 0], got_z1.at[chunk, 0], near)
        z_kept[chunk] = total(z ^ 2)
        sums_ref[chunk] = total(z)
        return one, two

    def second_step(chunk, pair):
        one, two = pair
        one.wait_recv()
        one.wait_send()
        begun[:] = [copy for copy in begun if copy is not one]
        z_send[chunk, 1] = (z_kept[chunk] + got_z1[chunk, 1].astype(F32)).astype(BF16)
        gone = send(z_send.at[chunk, 1], got_z2.at[chunk], far)
        two.wait_recv()
        sums_ref[chunk] += got_z1[chunk, 0].astype(F32)
        return gone

    def third_step(chunk, gone):
        gone.wait_recv()
        sums_ref[chunk] += got_z2[chunk].astype(F32)

    mixed_own.wait()
    core_own.wait_recv()
    y_own.wait_recv()
    small_ref[...] = small_in_ref[...]
    lines = 64
    count = small_in_ref.shape[0] - 2

    def finish(j, carry):
        at = span(j * lines, lines)
        grad = part_ref[at, :] + got_core_ref[1, at, :].astype(F32) + got_y_ref[at, :].astype(F32)
        hat, inverse = norm_parts(tokens_ref[at, :].astype(F32))
        back, gain_grad, bias_grad = norm_backward(grad, hat, inverse, gain1_ref[...])
        tg_own_ref[at, :] = (gx2_ref[at, :] + back).astype(BF16)
        small_ref[count : count + 1, :] += gain_grad[None, :]
        small_ref[count + 1 : count + 2, :] += bias_grad[None, :]
        return carry

    lax.fori_loop(0, share // lines, finish, 0)
    tg_y = send(tg_own_ref, tg_ref.at[t], y_side)
    tg_core = send(tg_own_ref, tg_ref.at[t], core)
    tg_own = pltpu.make_async_copy(tg_own_ref, tg_ref.at[t], local_sems.at[2])
    tg_own.start()

    def small_step(step, devices):
        small_send[step] = small_ref[...]
        exchanged = [
            send(small_send.at[step], got_small.at[step + d], device)
            for d, device in enumerate(devices)
        ]
        for d, copy in enumerate(exchanged):
            copy.wait_recv()
            small_ref[...] += got_small[step + d]

    small_step(0, [core])
    pairs = {0: first_step(0)}
    gone = {0: second_step(0, pairs[0])}
    tg_y.wait_recv()
    tg_y_core = send(tg_ref.at[t ^ 2], tg_ref.at[t ^ 2], core)
    small_step(1, [y_side])
    for chunk in (1, 2, 3):
        pairs[chunk] = first_step(chunk)
        third_step(chunk - 1, gone[chunk - 1])
        if chunk == 3:
            small_step(4, twins)
        gone[chunk] = second_step(chunk, pairs[chunk])
    small_step(2, [near])
    third_step(3, gone[3])
    small_step(3, [far])
    for copy in (core_own, mixed_core, mixed_y_core, tg_core, tg_y_core, down_far, up_far):
        if copy is not core_own:
            copy.wait_recv()
    tg_own.wait()
    for copy in begun:
        if copy is not ga_y and copy is not ga_y_core:
            copy.wait_send()


def back_call(
    queries, keys, values, heads, logs, first, keep, tables_, w_out, w3, gain1, tokens_own,
    grad_middle, small, grad_own, mixed_own, normed1, down_part, got_down, up_part,
):
    rows, own = queries.shape
    share, width = grad_own.shape
    copies, owners = lax.axis_size("dp"), lax.axis_size("bucket")
    splits = rows // share
    reach = width // copies
    part = reach // owners
    half = down_part.shape[1] // 2
    inside = pl.BlockSpec(memory_space=pltpu.VMEM)
    outside = pl.BlockSpec(memory_space=pl.ANY)
    shape = jax.ShapeDtypeStruct
    dma = lambda *count: pltpu.SemaphoreType.DMA(count)
    vmem = lambda dtype, *size: pltpu.VMEM(size, dtype)
    others = copies - 1
    few = 128
    sends = 3 + 3 + 3 + 2 + 3 + 12 + 4 + 6 * others
    return pl.pallas_call(
        functools.partial(back_kernel, copies),
        in_specs=[inside] * 10 + [outside] * 11,
        out_specs=[inside] * 2 + [outside] * 8,
        out_shape=[
            shape((4, part, own), F32),
            shape(small.shape, F32),
            shape((splits, share, width), BF16),
            shape((splits, share, width), BF16),
            shape((reach, half), F32),
            shape((reach, half), BF16),
            shape((reach, half), F32),
            shape((reach, half), BF16),
            shape((others, reach, 2 * half), BF16),
            shape((others, 4, reach, own), BF16),
        ],
        scratch_shapes=[
            vmem(BF16, rows, own),
            vmem(BF16, rows, own),
            vmem(BF16, rows, own),
            vmem(BF16, rows, own),
            vmem(BF16, *w3.shape),
            vmem(BF16, splits, share, width),
            vmem(BF16, rows, own),
            vmem(BF16, rows, 3 * own),
            vmem(F32, rows, HEAD_DIM),
            vmem(F32, rows, HEAD_DIM),
            vmem(BF16, 2, share, width),
            vmem(BF16, share, width),
            vmem(F32, share, width),
            vmem(BF16, share, width),
            vmem(BF16, 2, rows, 256),
            vmem(BF16, 2, 3, 256, own),
            vmem(BF16, 2, few, 2 * half),
            vmem(BF16, 2, others, few, 2 * half),
            vmem(BF16, 2, reach, half),
            vmem(F32, 2, few, half),
            vmem(BF16, 4, reach, own),
            vmem(BF16, others, 4, reach, own),
            vmem(BF16, 4, 2, part, own),
            vmem(F32, 4, part, own),
            vmem(BF16, 4, 2, part, own),
            vmem(BF16, 4, part, own),
            vmem(F32, 4 + others, *small.shape),
            vmem(F32, 5, *small.shape),
            dma(sends),
            dma(sends),
            dma(4),
            dma(2),
            dma(2),
            dma(copies, 2),
            dma(2),
            dma(5),
        ],
        compiler_params=pltpu.CompilerParams(
            vmem_limit_bytes=62 << 20, collective_id=2, has_side_effects=True
        ),
        cost_estimate=pl.CostEstimate(
            flops=16 * rows * width * own + 10 * rows * rows * own,
            bytes_accessed=80 << 20,
            transcendentals=rows * rows * own // HEAD_DIM,
        ),
        name="back",
    )(
        logs, first, keep, *tables_, w_out, gain1, tokens_own, grad_middle, small,
        queries, keys, values, heads, w3, grad_own, mixed_own, normed1, down_part, got_down, up_part,
    )


def local(
    tokens,
    cotangent,
    lengths,
    head_quarters,
    buckets,
    ln1_gain,
    ln1_bias,
    w_qkv,
    w_out,
    ln2_gain,
    ln2_bias,
    w_router,
    w_up,
    w_down,
):
    tok_rows, model_width = tokens.shape
    owners = lax.axis_size("bucket")
    splits = lax.axis_size("tensor")
    copies = lax.axis_size("dp")
    share = tok_rows // splits
    t, z, x = lax.axis_index("tensor"), lax.axis_index("bucket"), lax.axis_index("dp")
    up_own = w_up.reshape(model_width, -1)
    down_own = w_down.reshape(-1, model_width)
    hidden_width = up_own.shape[1]

    levels = buckets[:, 0].astype(F32).reshape(-1, HEAD_DIM)

    def shard(values, bit):
        return lax.dynamic_slice_in_dim(values, (t ^ bit) * share, share, 0)

    first = layout(lengths[0], tok_rows)[:, None]
    keep = (t < head_quarters).astype(F32)[:, None]
    w3 = jnp.transpose(w_qkv, (1, 0, 2))
    (
        logs,
        middle,
        cosine,
        sine,
        normed1,
        queries,
        keys,
        values,
        heads_low,
        n2,
        up_other,
        down_other,
        near_cotangent,
        near_levels,
    ) = front_call(
        tokens,
        (ln1_gain.reshape(1, -1), ln1_bias.reshape(1, -1)),
        w3,
        first,
        keep,
        w_out,
        (ln2_gain.reshape(1, -1), ln2_bias.reshape(1, -1)),
        up_own,
        down_own,
        cotangent.reshape(splits, share, model_width),
        levels,
    )
    level_all = jnp.concatenate([levels.reshape(-1), near_levels.reshape(-1)], 0)[:, None]
    (
        mixed_own,
        grad_middle,
        grad_attention_own,
        small,
        _,
        down_part,
        up_part,
        got_down,
    ) = middle_call(
        n2,
        cotangent,
        near_cotangent,
        (up_own, up_other),
        (down_own, down_other),
        w_router,
        level_all,
        middle,
        (ln2_gain.reshape(1, -1), ln2_bias.reshape(1, -1)),
    )
    sums, small, mixed, tokens_grad, down_own, down_got, up_own, up_got, _, _ = back_call(
        queries,
        keys,
        values,
        heads_low,
        logs,
        first,
        keep,
        (cosine, sine),
        w_out,
        w3,
        ln1_gain.reshape(1, -1),
        shard(tokens, 0),
        grad_middle,
        jnp.concatenate([small, jnp.zeros((2, model_width), F32)], 0),
        grad_attention_own,
        mixed_own,
        normed1,
        down_part,
        got_down,
        up_part,
    )
    grad_down = (down_own + down_got.astype(F32)).T
    grad_up = up_own + up_got.astype(F32)
    width = model_width // (copies * owners)
    small = lax.dynamic_slice_in_dim(small, (x * owners + z) * width, width, 1)
    return (
        mixed.reshape(tok_rows, model_width),
        tokens_grad.reshape(tok_rows, model_width).astype(F32),
        small[2 + owners],
        small[3 + owners],
        jnp.transpose(sums[1:], (1, 0, 2)),
        sums[0].T,
        small[0],
        small[1],
        small[2 : 2 + owners].T,
        grad_up.reshape(-1, 1, hidden_width),
        grad_down.reshape(1, hidden_width, -1),
    )


def solution(mesh):
    placed = (
        P(("dp", "bucket"), None),
        P(("dp", "bucket"), None),
        P(("dp", "bucket"), None),
        P(("dp", "bucket")),
        P(("dp", "bucket"), None),
        P(),
        P(),
        P(None, None, "tensor"),
        P("tensor", None),
        P(),
        P(),
        P(),
        P(None, "bucket", "tensor"),
        P("bucket", "tensor", None),
    )
    return jax.shard_map(
        local,
        mesh=mesh,
        in_specs=placed,
        out_specs=(
            P(("dp", "bucket"), None),
            P(("dp", "bucket"), None),
            P(("dp", "bucket")),
            P(("dp", "bucket")),
            P(("dp", "bucket"), None, "tensor"),
            P("tensor", ("dp", "bucket")),
            P(("dp", "bucket")),
            P(("dp", "bucket")),
            P(("dp", "bucket"), None),
            P("dp", "bucket", "tensor"),
            P("bucket", "tensor", "dp"),
        ),
        check_vma=False,
    )
```

```python
import functools
import math

import jax
import jax.numpy as jnp
from jax import lax
from jax.experimental import pallas as pl
from jax.experimental.pallas import tpu as pltpu
from jax.sharding import PartitionSpec as P

HEAD_DIM = 128
QBLOCK = 256
EPS = 1e-05
HIGH = lax.Precision.HIGHEST
NEGATIVE = -1e30
F32 = jnp.float32
BF16 = jnp.bfloat16


def norm_parts(values):
    centred = values - jnp.mean(values, -1, keepdims=True)
    inverse = lax.rsqrt(jnp.mean(centred * centred, -1, keepdims=True) + EPS)
    return centred * inverse, inverse


def norm_backward(grad_in, normed, inverse, gain):
    scaled = grad_in * gain
    inner = (
        scaled
        - jnp.mean(scaled, -1, keepdims=True)
        - normed * jnp.mean(scaled * normed, -1, keepdims=True)
    )
    return inverse * inner, jnp.sum(grad_in * normed, 0), jnp.sum(grad_in, 0)


def layout(lengths_row, tok_rows):
    ends = jnp.cumsum(lengths_row)
    starts = ends - lengths_row
    tok_index = jnp.arange(tok_rows, dtype=jnp.int32)
    segments = jnp.sum((tok_index[:, None] >= ends[None, :]).astype(jnp.int32), 1)
    chosen = segments[:, None] == jnp.arange(lengths_row.shape[0], dtype=jnp.int32)[None, :]
    return jnp.sum(jnp.where(chosen, starts[None, :], 0), 1)


def dot(left, right, dims):
    return lax.dot_general(left, right, (dims, ((), ())), preferred_element_type=F32)


NN = ((1,), (0,))
NT = ((1,), (1,))
TN = ((0,), (0,))


def masked_scores(query, keys, first, block, length):
    scores = dot(query, keys, NT) * HEAD_DIM**-0.5
    key_at = lax.broadcasted_iota(jnp.int32, (QBLOCK, length), 1)
    row_at = lax.broadcasted_iota(jnp.int32, (QBLOCK, length), 0) + block * QBLOCK
    allowed = (key_at >= first) & (key_at <= row_at)
    return jnp.where(allowed, scores, NEGATIVE)


class Copies:
    def __init__(self, send_sems, recv_sems):
        self.send_sems, self.recv_sems, self.used = send_sems, recv_sems, 0

    def make(self, source, target, device):
        slot = self.used
        self.used += 1
        return pltpu.make_async_remote_copy(
            src_ref=source,
            dst_ref=target,
            send_sem=self.send_sems.at[slot],
            recv_sem=self.recv_sems.at[slot],
            device_id=device,
            device_id_type=pl.DeviceIdType.MESH,
        )

    def start(self, source, target, device):
        copy = self.make(source, target, device)
        copy.start()
        return copy


def meet(devices):
    barrier = pltpu.get_barrier_semaphore()
    for device in devices:
        pl.semaphore_signal(barrier, inc=1, device_id=device, device_id_type=pl.DeviceIdType.MESH)
    pl.semaphore_wait(barrier, len(devices))


def front_kernel(
    copies,
    gain1_ref,
    bias1_ref,
    first_ref,
    keep_ref,
    gain2_ref,
    bias2_ref,
    tokens_in,
    w_in,
    w_out_in,
    up_ref,
    down_ref,
    cot_ref,
    level_ref,
    log_ref,
    middle_ref,
    cos_ref,
    sin_ref,
    n1_out,
    q_out,
    k_out,
    v_out,
    heads_out,
    n2_ref,
    up_other_ref,
    down_other_ref,
    near_cot_ref,
    near_level_ref,
    tokens_ref,
    w_ref,
    w_out_ref,
    n1_ref,
    q_ref,
    k_ref,
    v_ref,
    heads_ref,
    away_ref,
    got_core_ref,
    pass_ref,
    got_y_ref,
    own_ref,
    send_sems,
    recv_sems,
    in_sems,
    out_sems,
):
    t, z, x = lax.axis_index("tensor"), lax.axis_index("bucket"), lax.axis_index("dp")
    rows, own = q_ref.shape
    share = own_ref.shape[0]
    heads = own // HEAD_DIM
    blocks = rows // QBLOCK
    core, y_side = {"tensor": t ^ 1}, {"tensor": t ^ 2}
    near, far = {"bucket": z ^ 1}, {"bucket": z ^ 2}
    twins = [{"dp": lax.rem(x + d, copies)} for d in range(1, copies)]

    def token_block(i):
        at = pl.ds(pl.multiple_of(i * QBLOCK, QBLOCK), QBLOCK)
        return pltpu.make_async_copy(tokens_in.at[at], tokens_ref.at[at], in_sems.at[i])

    w_copies = [
        pltpu.make_async_copy(w_in.at[part], w_ref.at[part], in_sems.at[blocks + part])
        for part in range(3)
    ]
    w_out_copy = pltpu.make_async_copy(w_out_in, w_out_ref, in_sems.at[blocks + 3])
    token_block(0).start()
    for copy in w_copies:
        copy.start()
    for i in range(1, blocks):
        token_block(i).start()
    w_out_copy.start()

    meet([core, y_side, near, far] + twins)
    links = Copies(send_sems, recv_sems)
    begun = []

    def send(source, target, device):
        copy = links.start(source, target, device)
        begun.append(copy)
        return copy

    def piece(ref, quarter):
        size = ref.shape[0] // copies // 4
        return ref.at[pl.ds(pl.multiple_of((x * 4 + quarter) * size, 16), size)]

    def fetch(ref, other_ref, quarter):
        copy = links.make(piece(ref, quarter), piece(other_ref, quarter), far)
        begun.append(copy)
        return copy

    outer = lax.rem(z, 2) == z // 2
    pieces = [fetch(up_ref, up_other_ref, quarter) for quarter in range(4)]
    pieces += [fetch(down_ref, down_other_ref, quarter) for quarter in range(4)]
    parity = lax.rem(t, 2)
    cots = [
        links.make(cot_ref.at[parity + i], near_cot_ref.at[parity + i], near) for i in (0, 2)
    ]
    begun.extend(cots)
    to_twins = [
        [links.make(ref, ref, device) for device in twins]
        for ref in [piece(up_other_ref, quarter) for quarter in range(4)]
        + [piece(down_other_ref, quarter) for quarter in range(4)]
    ]
    to_core_cots = [
        links.make(near_cot_ref.at[parity + i], near_cot_ref.at[parity + i], core) for i in (0, 2)
    ]

    def begin(copies_):
        for copy in copies_:
            copy.start()

    def pass_weights(indices):
        for index in indices:
            pieces[index].wait_recv()
            begin(to_twins[index])

    def pass_cots():
        for copy, onward_copy in zip(cots, to_core_cots):
            copy.wait_recv()
            onward_copy.start()

    @pl.when(outer)
    def _():
        begin(pieces)

    @pl.when(jnp.logical_not(outer))
    def _():
        begin(cots)

    near_level = send(level_ref, near_level_ref, near)

    half = HEAD_DIM // 2
    lane = lax.broadcasted_iota(jnp.int32, (1, HEAD_DIM), 1)
    freq = jnp.exp((lane % half).astype(F32) * (-math.log(10000.0) / half))
    side = jnp.where(lane < half, -1.0, 1.0)

    def project(i, carry):
        at = pl.ds(pl.multiple_of(i * QBLOCK, QBLOCK), QBLOCK)
        token_block(i).wait()
        normed, _ = norm_parts(tokens_ref[at, :].astype(F32))
        low = (normed * gain1_ref[...] + bias1_ref[...]).astype(BF16)
        n1_ref[at, :] = low
        token = lax.broadcasted_iota(jnp.int32, (QBLOCK, 1), 0) + i * QBLOCK
        angle = (token - first_ref[at, :]).astype(F32) * freq
        cosine, sine = jnp.cos(angle), jnp.sin(angle) * side
        cos_ref[at, :] = cosine
        sin_ref[at, :] = sine
        for part, out_ref in enumerate((q_ref, k_ref, v_ref)):

            @pl.when(i == 0)
            def _():
                w_copies[part].wait()

            projected = dot(low, w_ref[part], NN)
            if part == 2:
                out_ref[at, :] = projected.astype(BF16)
                continue
            for start in range(0, own, HEAD_DIM):
                head = projected[:, start : start + HEAD_DIM]
                turned = head * cosine + pltpu.roll(head, half, 1) * sine
                out_ref[at, start : start + HEAD_DIM] = turned.astype(BF16)
        return carry

    lax.fori_loop(0, blocks, project, 0)
    outs = [
        pltpu.make_async_copy(ref, out, out_sems.at[i])
        for i, (ref, out) in enumerate(
            ((n1_ref, n1_out), (q_ref, q_out), (k_ref, k_out), (v_ref, v_out), (heads_ref, heads_out))
        )
    ]
    for copy in outs[:4]:
        copy.start()

    for head in range(heads):
        lanes = slice(head * HEAD_DIM, (head + 1) * HEAD_DIM)
        for block in range(rows // QBLOCK):
            length = (block + 1) * QBLOCK
            at = slice(block * QBLOCK, length)
            scores = masked_scores(
                q_ref[at, lanes], k_ref[:length, lanes], first_ref[at], block, length
            )
            most = jnp.max(scores, -1, keepdims=True)
            expo = jnp.exp(scores - most)
            total = jnp.sum(expo, -1, keepdims=True)
            weights = (expo * (1.0 / total)).astype(BF16)
            out = dot(weights, v_ref[:length, lanes], NN)
            heads_ref[at, lanes] = (out * keep_ref[at]).astype(BF16)
            log_ref[at, head : head + 1] = most + jnp.log(total)

    outs[4].start()
    w_out_copy.wait()

    def attended(index):
        at = pl.ds(pl.multiple_of(index * share, share), share)
        return dot(heads_ref[at, :], w_out_ref[...], NN)

    away_ref[1] = attended(t ^ 3).astype(BF16)
    to_core1 = send(away_ref.at[1], got_core_ref.at[1], core)
    away_ref[0] = attended(t ^ 1).astype(BF16)
    to_core0 = send(away_ref.at[0], got_core_ref.at[0], core)
    passed = attended(t ^ 2)
    to_core1.wait_recv()
    pass_ref[...] = (passed + got_core_ref[1].astype(F32)).astype(BF16)
    to_y = send(pass_ref, got_y_ref, y_side)
    middle = attended(t)
    middle += tokens_ref[pl.ds(pl.multiple_of(t * share, share), share), :].astype(F32)
    to_core0.wait_recv()
    middle_ref[...] = middle + got_core_ref[0].astype(F32)

    @pl.when(jnp.logical_not(outer))
    def _():
        pass_weights(range(8))
        begin(pieces)

    @pl.when(outer)
    def _():
        begin(cots)
        pass_cots()

    to_y.wait_recv()
    total = middle_ref[...] + got_y_ref[...].astype(F32)
    middle_ref[...] = total
    normed, _ = norm_parts(total)
    own_ref[...] = (normed * gain2_ref[...] + bias2_ref[...]).astype(BF16)
    own_y = send(own_ref, n2_ref.at[t], y_side)
    own_core = send(own_ref, n2_ref.at[t], core)
    keep_own = pltpu.make_async_copy(own_ref, n2_ref.at[t], in_sems.at[0])
    keep_own.start()

    @pl.when(outer)
    def _():
        pass_weights(range(4))

    own_y.wait_recv()
    y_core = send(n2_ref.at[t ^ 2], n2_ref.at[t ^ 2], core)

    @pl.when(outer)
    def _():
        pass_weights(range(4, 8))

    @pl.when(jnp.logical_not(outer))
    def _():
        pass_cots()

    keep_own.wait()
    for copy in outs:
        copy.wait()
    for copy in (near_level, own_core, y_core, *to_core_cots, *sum(to_twins, [])):
        copy.wait_recv()
    for copy in (*begun, *to_core_cots, *sum(to_twins, [])):
        copy.wait_send()


def front_call(tokens, ln1, w3, first, keep, w_out, ln2, up, down, cotangent, levels):
    rows, width = tokens.shape
    own = w3.shape[2]
    splits, copies = lax.axis_size("tensor"), lax.axis_size("dp")
    share = rows // splits
    inside = pl.BlockSpec(memory_space=pltpu.VMEM)
    outside = pl.BlockSpec(memory_space=pl.ANY)
    shape = jax.ShapeDtypeStruct
    vmem = lambda dtype, *size: pltpu.VMEM(size, dtype)
    total = 19 + 8 * (copies - 1)
    narrow = shape((rows, own), BF16)
    return pl.pallas_call(
        functools.partial(front_kernel, copies),
        in_specs=[inside] * 6 + [outside] * 7,
        out_specs=[inside] * 4 + [outside] * 10,
        out_shape=[
            shape((rows, own // HEAD_DIM), F32),
            shape((share, width), F32),
            shape((rows, HEAD_DIM), F32),
            shape((rows, HEAD_DIM), F32),
            shape((rows, width), BF16),
            narrow,
            narrow,
            narrow,
            narrow,
            shape((splits, share, width), BF16),
            shape(up.shape, BF16),
            shape(down.shape, BF16),
            shape((splits, share, width), BF16),
            shape(levels.shape, F32),
        ],
        scratch_shapes=[
            vmem(BF16, rows, width),
            vmem(BF16, *w3.shape),
            vmem(BF16, *w_out.shape),
            vmem(BF16, rows, width),
            vmem(BF16, rows, own),
            vmem(BF16, rows, own),
            vmem(BF16, rows, own),
            vmem(BF16, rows, own),
            vmem(BF16, 2, share, width),
            vmem(BF16, 2, share, width),
            vmem(BF16, share, width),
            vmem(BF16, share, width),
            vmem(BF16, share, width),
            pltpu.SemaphoreType.DMA((total,)),
            pltpu.SemaphoreType.DMA((total,)),
            pltpu.SemaphoreType.DMA((rows // QBLOCK + 4,)),
            pltpu.SemaphoreType.DMA((5,)),
        ],
        compiler_params=pltpu.CompilerParams(
            vmem_limit_bytes=56 << 20, collective_id=0, has_side_effects=True
        ),
        cost_estimate=pl.CostEstimate(
            flops=8 * rows * width * own + 4 * rows * rows * own,
            bytes_accessed=60 << 20,
            transcendentals=rows * rows * own // HEAD_DIM,
        ),
        name="front",
    )(*ln1, first, keep, *ln2, tokens, w3, w_out, up, down, cotangent, levels)


def block_at(i, t):
    near, j = i // 4, i % 4
    own_bit = (1 - j // 2) * (3 - 2 * j) + (j // 2) * (6 - 2 * j)
    bit = (1 - near) * own_bit + near * (j + 1 - 2 * (j % 2))
    return near, t ^ bit


def router_gate(rows, w_router_ref, level):
    logits = dot(rows, w_router_ref[...], NN)
    expo = jnp.exp(logits - jnp.max(logits, -1, keepdims=True))
    probs = expo / jnp.sum(expo, -1, keepdims=True)
    number = lax.broadcasted_iota(jnp.int32, probs.shape, 1).astype(F32)
    onehot = (number == level).astype(F32)
    return jnp.sum(probs * onehot, -1, keepdims=True), probs, onehot


def middle_kernel(
    copies,
    n2_ref,
    cot_ref,
    near_cot_ref,
    up_own_ref,
    up_other_ref,
    down_own_ref,
    down_other_ref,
    router_ref,
    level_ref,
    gain2_ref,
    bias2_ref,
    x2_in,
    mixed_ref,
    gx2_ref,
    ga_ref,
    small_ref,
    near_n2_ref,
    gf_ref,
    down_own_grad,
    down_other_grad,
    up_own_grad,
    up_other_grad,
    got_down_ref,
    got_up_ref,
    n2_in,
    cot_in,
    gf_out,
    hid_ref,
    gu_ref,
    part_f,
    part_g,
    hold_f,
    send_ref,
    core_f,
    core_g,
    got_fz,
    got_fy,
    got_gy,
    got_gz,
    tile_in,
    tile_out,
    core_send_sems,
    core_recv_sems,
    send_sems,
    recv_sems,
    in_sems,
    out_sems,
    tile_sems,
    tile_out_sems,
    x2_sem,
):
    t, z, x = lax.axis_index("tensor"), lax.axis_index("bucket"), lax.axis_index("dp")
    share, width = gx2_ref.shape
    half = up_own_ref.shape[1]
    core, y_side, near = {"tensor": t ^ 1}, {"tensor": t ^ 2}, {"bucket": z ^ 1}
    twins = [{"dp": lax.rem(x + d, copies)} for d in range(1, copies)]
    splits = n2_ref.shape[0]

    def load(i, slot, act):
        at, s = block_at(i, t)
        for index, (rows_ref, grads_ref) in enumerate(
            ((n2_ref, cot_ref), (near_n2_ref, near_cot_ref))
        ):

            @pl.when(at == index)
            def _():
                act(pltpu.make_async_copy(rows_ref.at[s], n2_in.at[slot], in_sems.at[slot, 0]))
                act(pltpu.make_async_copy(grads_ref.at[s], cot_in.at[slot], in_sems.at[slot, 1]))

    def begin(copy):
        copy.start()

    def finish_load(copy):
        copy.wait()

    def store(i, slot):
        at, s = block_at(i, t)
        return pltpu.make_async_copy(gf_out.at[slot], gf_ref.at[at, s], out_sems.at[slot])

    def to_core(a):
        return [
            pltpu.make_async_remote_copy(
                src_ref=send_ref.at[kind * 2 + int(a == 1)],
                dst_ref=(core_f, core_g)[kind].at[a],
                send_sem=core_send_sems.at[kind, a],
                recv_sem=core_recv_sems.at[kind, a],
                device_id=core,
                device_id_type=pl.DeviceIdType.MESH,
            )
            for kind in (0, 1)
        ]

    load(0, 0, begin)
    meet([core, y_side, near] + twins)
    links = Copies(send_sems, recv_sems)
    few = share // 2
    late = pl.ds(few, few)
    early = pl.ds(0, few)
    to_near = [
        links.start(n2_ref.at[t, late], near_n2_ref.at[t, late], near),
        links.start(n2_ref.at[t, early], near_n2_ref.at[t, early], near),
        links.start(n2_ref.at[t ^ 2, early], near_n2_ref.at[t ^ 2, early], near),
    ]
    near_y = links.make(near_n2_ref.at[t, late], near_n2_ref.at[t, late], y_side)
    near_core = links.make(near_n2_ref.at[t], near_n2_ref.at[t], core)
    near_y_core = links.make(near_n2_ref.at[t ^ 2], near_n2_ref.at[t ^ 2], core)
    g_own_y = links.make(send_ref.at[4], got_gy.at[1], y_side)
    f_near = links.make(send_ref.at[1], got_fz.at[1], near)
    g_near_y = links.make(send_ref.at[0], got_gy.at[0], y_side)
    f_near_y = links.make(send_ref.at[2], got_fz.at[0], near)
    f_own_y = links.make(send_ref.at[3], got_fy, y_side)
    g_near = links.make(send_ref.at[4], got_gz, near)

    def work(i, carry):
        slot = i % 2
        at, s = block_at(i, t)
        load(i, slot, finish_load)

        @pl.when((i != 3) & (i != 5) & (i != 7))
        def _():
            load(i + 1, 1 - slot, begin)

        @pl.when(i >= 2)
        def _():
            store(i - 2, slot).wait()

        spot = pl.ds(pl.multiple_of((at * splits + s) * share, share), share)
        rows = n2_in[slot]
        level = level_ref[spot, :]
        gate, _, _ = router_gate(rows, router_ref, level)
        grad = (gate * cot_in[slot].astype(F32)).astype(BF16)
        gf_out[slot] = grad
        store(i, slot).start()
        for part, (up_ref, down_ref, unit_level) in enumerate(
            ((up_own_ref, down_own_ref, z), (up_other_ref, down_other_ref, z ^ 2))
        ):
            lanes = slice(part * half, (part + 1) * half)
            kept = level >= unit_level.astype(F32)
            act = jnp.where(kept, jnp.maximum(dot(rows, up_ref[...], NN), 0.0), 0.0)
            hid_ref[spot, lanes] = (act * act).astype(BF16)
            back = dot(grad, down_ref[...], NT)
            gu_ref[spot, lanes] = (back * 2.0 * act).astype(BF16)
        for lanes in (slice(0, width // 2), slice(width // 2, width)):
            part_f[:, lanes] = dot(hid_ref[spot, :half], down_own_ref[:, lanes], NN) + dot(
                hid_ref[spot, half:], down_other_ref[:, lanes], NN
            )
            part_g[:, lanes] = dot(gu_ref[spot, :half], up_own_ref[lanes, :], NT) + dot(
                gu_ref[spot, half:], up_other_ref[lanes, :], NT
            )

        def leave(a):
            for before in {2: (0,), 3: (2,)}.get(a, ()):
                for copy in to_core(before):
                    copy.wait_send()
            send_ref[int(a == 1)] = part_f[...].astype(BF16)
            send_ref[2 + int(a == 1)] = part_g[...].astype(BF16)
            for copy in to_core(a):
                copy.start()

        for a, index in enumerate((0, 1, 4, 6)):

            @pl.when(i == index)
            def _():
                leave(a)

        def with_core(kind, a):
            to_core(a)[kind].wait_recv()
            got = (core_f, core_g)[kind][a].astype(F32)
            return (part_f, part_g)[kind][...] + got

        @pl.when(i == 1)
        def _():
            to_near[0].wait_recv()
            near_y.start()

        @pl.when(i == 4)
        def _():
            to_near[2].wait_recv()
            near_y.wait_recv()
            near_y_core.start()

        @pl.when(i == 2)
        def _():
            send_ref[4] = with_core(1, 0).astype(BF16)
            g_own_y.start()
            hold_f[...] = with_core(0, 0)

        @pl.when(i == 3)
        def _():
            mixed_ref[...] = with_core(0, 1).astype(BF16)
            ga_ref[...] = with_core(1, 1).astype(BF16)
            to_near[1].wait_recv()
            near_core.start()
            near_core.wait_recv()
            load(i + 1, 1 - slot, begin)

        @pl.when(i == 5)
        def _():
            for copy in to_core(1):
                copy.wait_send()
            send_ref[1] = with_core(0, 2).astype(BF16)
            f_near.start()
            gx2_ref[...] = with_core(1, 2)
            near_y_core.wait_recv()
            load(i + 1, 1 - slot, begin)

        @pl.when(i == 7)
        def _():
            for copy in to_core(3):
                copy.wait_send()
            send_ref[0] = with_core(1, 3).astype(BF16)
            g_near_y.start()
            send_ref[2] = with_core(0, 3).astype(BF16)
            f_near_y.start()

        return carry

    lax.fori_loop(0, 8, work, 0)
    store(6, 0).wait()
    store(7, 1).wait()
    x2_ref = part_f
    x2_copy = pltpu.make_async_copy(x2_in, x2_ref, x2_sem)
    x2_copy.start()

    tile = tile_in.shape[-1]
    tiles = width // tile

    def weight_grads(sources, right_ref, results):
        def fetch(j, slot):
            lanes = pl.ds(pl.multiple_of(j * tile, tile), tile)
            return [
                pltpu.make_async_copy(
                    source.at[:, :, lanes], tile_in.at[slot, index], tile_sems.at[slot, index]
                )
                for index, source in enumerate(sources)
            ]

        def put(j, slot):
            rows = pl.ds(pl.multiple_of(j * tile, tile), tile)
            return [
                pltpu.make_async_copy(
                    tile_out.at[slot, index], result.at[rows, :], tile_out_sems.at[slot, index]
                )
                for index, result in enumerate(results)
            ]

        for copy in fetch(0, 0):
            copy.start()

        def step(j, carry):
            slot = j % 2
            for copy in fetch(j, slot):
                copy.wait()

            @pl.when(j < tiles - 1)
            def _():
                for copy in fetch(j + 1, 1 - slot):
                    copy.start()

            @pl.when(j >= 2)
            def _():
                for copy in put(j - 2, slot):
                    copy.wait()

            left = tile_in[slot].reshape(-1, tile)
            total = dot(left, right_ref[...], TN).astype(BF16)
            for index in (0, 1):
                tile_out[slot, index] = total[:, index * half : (index + 1) * half]
            for copy in put(j, slot):
                copy.start()
            return carry

        lax.fori_loop(0, tiles, step, 0)
        for j in (tiles - 2, tiles - 1):
            for copy in put(j, j % 2):
                copy.wait()

    size = width // copies

    def to_twins(grad_ref, got_ref):
        return [
            links.start(
                grad_ref.at[pl.ds(pl.multiple_of(lax.rem(x + d, copies) * size, size), size), :],
                got_ref.at[d - 1],
                twins[d - 1],
            )
            for d in range(1, copies)
        ]

    weight_grads((gf_ref.at[0], gf_ref.at[1]), hid_ref, (down_own_grad, down_other_grad))
    crossing = to_twins(down_other_grad, got_down_ref)

    weight_grads((n2_ref, near_n2_ref), gu_ref, (up_own_grad, up_other_grad))
    crossing += to_twins(up_other_grad, got_up_ref)

    f_near_y.wait_recv()
    send_ref[3] = (hold_f[...] + got_fz[0].astype(F32)).astype(BF16)
    f_own_y.start()
    g_near_y.wait_recv()
    g_own_y.wait_send()
    send_ref[4] = (gx2_ref[...] + got_gy[0].astype(F32)).astype(BF16)
    g_near.start()

    own = pltpu.make_async_copy(n2_ref.at[t], n2_in.at[0], in_sems.at[0, 0])
    own.start()
    own_cot = pltpu.make_async_copy(cot_ref.at[t], cot_in.at[0], in_sems.at[0, 1])
    own_cot.start()
    own.wait()
    own_cot.wait()
    for copy in (f_near, f_own_y, g_own_y, g_near):
        copy.wait_recv()
    x2_copy.wait()
    small_ref[...] = jnp.zeros_like(small_ref)
    few = 64

    def finish(j, carry):
        at = pl.ds(pl.multiple_of(j * few, few), few)
        level = level_ref[pl.ds(pl.multiple_of(t * share + j * few, few), few), :]
        rows = n2_in[0, at, :]
        gate, probs, onehot = router_gate(rows, router_ref, level)
        branch = mixed_ref[at, :].astype(F32) + got_fz[1, at, :].astype(F32) + got_fy[at, :].astype(F32)
        branch = branch.astype(BF16).astype(F32)
        x2 = x2_ref[at, :]
        mixed_ref[at, :] = (x2 + gate * branch).astype(BF16)
        grad_out = cot_in[0, at, :].astype(F32)
        grad_gate = jnp.sum(grad_out * branch, -1, keepdims=True)
        grad_logits = grad_gate * gate * (onehot - probs)
        returned = ga_ref[at, :].astype(F32) + got_gy[1, at, :].astype(F32) + got_gz[at, :].astype(F32)
        grad_n2 = returned.astype(BF16).astype(F32)
        grad_n2 += lax.dot_general(
            grad_logits,
            router_ref[...].astype(F32),
            (NT, ((), ())),
            precision=HIGH,
            preferred_element_type=F32,
        )
        hat, inverse = norm_parts(x2)
        back, gain_grad, bias_grad = norm_backward(grad_n2, hat, inverse, gain2_ref[...])
        gx2 = grad_out + back
        gx2_ref[at, :] = gx2
        ga_ref[at, :] = gx2.astype(BF16)
        small_ref[0:1, :] += gain_grad[None, :]
        small_ref[1:2, :] += bias_grad[None, :]
        small_ref[2 : 2 + probs.shape[1], :] += lax.dot_general(
            grad_logits, rows.astype(F32), (TN, ((), ())), precision=HIGH, preferred_element_type=F32
        )
        return carry

    lax.fori_loop(0, share // few, finish, 0)
    for copy in crossing:
        copy.wait_recv()
    for copy in (
        *to_near, near_y, near_core, near_y_core, f_near,
        g_near_y, f_near_y, f_own_y, g_near, *crossing,
    ):
        copy.wait_send()


def middle_call(n2, cotangent, near_cotangent, ups, downs, w_router, levels, middle, ln2):
    splits, share, width = n2.shape
    copies = lax.axis_size("dp")
    half = ups[0].shape[1]
    rows = 2 * splits * share
    inside = pl.BlockSpec(memory_space=pltpu.VMEM)
    outside = pl.BlockSpec(memory_space=pl.ANY)
    shape = jax.ShapeDtypeStruct
    block = lambda count, dtype=BF16: pltpu.VMEM((*count, share, width), dtype)
    dma = lambda *count: pltpu.SemaphoreType.DMA(count)
    return pl.pallas_call(
        functools.partial(middle_kernel, copies),
        in_specs=[outside] * 3 + [inside] * 8 + [outside],
        out_specs=[inside] * 4 + [outside] * 8,
        out_shape=[
            shape((share, width), BF16),
            shape((share, width), F32),
            shape((share, width), BF16),
            shape((2 + w_router.shape[1], width), F32),
            shape(n2.shape, BF16),
            shape((2, *n2.shape), BF16),
            *[shape((width, half), BF16)] * 4,
            *[shape((copies - 1, width // copies, half), BF16)] * 2,
        ],
        scratch_shapes=[
            block((2,)),
            block((2,)),
            block((2,)),
            pltpu.VMEM((rows, 2 * half), BF16),
            pltpu.VMEM((rows, 2 * half), BF16),
            block((), F32),
            block((), F32),
            block((), F32),
            block((5,)),
            block((4,)),
            block((4,)),
            block((2,)),
            block(()),
            block((2,)),
            block(()),
            pltpu.VMEM((2, 2, splits, share, 256), BF16),
            pltpu.VMEM((2, 2, 256, half), BF16),
            dma(2, 4),
            dma(2, 4),
            dma(12 + 2 * (copies - 1)),
            dma(12 + 2 * (copies - 1)),
            dma(2, 2),
            dma(2),
            dma(2, 2),
            dma(2, 2),
            pltpu.SemaphoreType.DMA,
        ],
        compiler_params=pltpu.CompilerParams(
            vmem_limit_bytes=62 << 20, collective_id=1, has_side_effects=True
        ),
        cost_estimate=pl.CostEstimate(
            flops=12 * rows * width * 2 * half, bytes_accessed=80 << 20, transcendentals=0
        ),
        name="middle",
    )(n2, cotangent.reshape(splits, share, width), near_cotangent, *ups, *downs, w_router, levels, *ln2, middle)


def back_kernel(
    copies,
    log_ref,
    first_ref,
    keep_ref,
    cos_ref,
    sin_ref,
    w_out_ref,
    gain1_ref,
    tokens_ref,
    gx2_ref,
    small_in_ref,
    q_in,
    k_in,
    v_in,
    heads_in,
    w_in,
    ga_in_ref,
    mixed_in_ref,
    n1_ref,
    down_ref,
    got_down_ref,
    up_ref,
    got_up_ref,
    down_own_ref,
    up_own_ref,
    sums_ref,
    small_ref,
    mixed_ref,
    tg_ref,
    down_far_ref,
    up_far_ref,
    down_twin_ref,
    up_twin_ref,
    leave_ref,
    q_ref,
    k_ref,
    v_ref,
    heads_ref,
    w_ref,
    ga_ref,
    go_ref,
    gp_ref,
    dk_ref,
    dv_ref,
    got_core_ref,
    got_y_ref,
    part_ref,
    tg_own_ref,
    tile_in,
    tile_out,
    fold_a,
    fold_b,
    fold_send,
    kept_ref,
    got_x_ref,
    z_send,
    z_kept,
    got_z1,
    got_z2,
    got_small,
    small_send,
    send_sems,
    recv_sems,
    local_sems,
    tile_sems,
    tile_out_sems,
    fold_sems,
    in_sems,
):
    t, z, x = lax.axis_index("tensor"), lax.axis_index("bucket"), lax.axis_index("dp")
    rows, own = q_ref.shape
    splits, share, width = ga_ref.shape
    heads, blocks = own // HEAD_DIM, rows // QBLOCK
    reach = width // copies
    part = got_z2.shape[1]
    core, y_side = {"tensor": t ^ 1}, {"tensor": t ^ 2}
    near, far = {"bucket": z ^ 1}, {"bucket": z ^ 2}
    twins = [{"dp": lax.rem(x + d, copies)} for d in range(1, copies)]
    meet([core, y_side, near, far] + twins)
    links = Copies(send_sems, recv_sems)
    begun = []

    def send(source, target, device):
        copy = links.start(source, target, device)
        begun.append(copy)
        return copy

    def span(start, size):
        return pl.ds(pl.multiple_of(start, size), size)

    ga_y = send(ga_in_ref, ga_ref.at[t], y_side)
    ga_core = send(ga_in_ref, ga_ref.at[t], core)
    ga_own = pltpu.make_async_copy(ga_in_ref, ga_ref.at[t], local_sems.at[0])
    ga_own.start()

    def to_twins(source_ref, target_ref):
        for d in range(1, copies):
            rows_there = span(lax.rem(x + d, copies) * reach, reach)
            twin_copies.append(send(source_ref.at[rows_there], target_ref.at[d - 1], twins[d - 1]))

    twin_copies = []
    to_twins(up_own_ref, up_twin_ref)
    mixed_y = send(mixed_in_ref, mixed_ref.at[t], y_side)
    mixed_core = send(mixed_in_ref, mixed_ref.at[t], core)
    mixed_take = pltpu.make_async_copy(mixed_in_ref, tg_own_ref, local_sems.at[1])
    mixed_take.start()
    mixed_own = pltpu.make_async_copy(tg_own_ref, mixed_ref.at[t], local_sems.at[3])

    loaded = [
        pltpu.make_async_copy(source, target, in_sems.at[index])
        for index, (source, target) in enumerate(
            ((heads_in, heads_ref), (q_in, q_ref), (k_in, k_ref), (v_in, v_ref), (w_in, w_ref))
        )
    ]
    for copy in loaded:
        copy.start()

    few = fold_a.shape[1]

    def fold(which, source_ref, got_ref, target_ref):
        def loads(k, slot):
            mine = pltpu.make_async_copy(
                source_ref.at[span(x * reach + k * few, few)], fold_a.at[slot], fold_sems.at[0, slot]
            )
            theirs = [
                pltpu.make_async_copy(
                    got_ref.at[d, span(k * few, few)], fold_b.at[slot, d], fold_sems.at[1 + d, slot]
                )
                for d in range(copies - 1)
            ]
            return [mine] + theirs

        for copy in loads(0, 0):
            copy.start()
        steps = reach // few

        def step(k, carry):
            slot = k % 2
            for copy in loads(k, slot):
                copy.wait()

            @pl.when(k < steps - 1)
            def _():
                for copy in loads(k + 1, 1 - slot):
                    copy.start()

            total = fold_a[slot].astype(F32)
            for d in range(copies - 1):
                total += fold_b[slot, d].astype(F32)
            fold_send[which, span(k * few, few), :] = total.astype(BF16)
            return carry

        lax.fori_loop(0, steps, step, 0)
        return send(fold_send.at[which], target_ref, far)

    down_far = fold(0, down_ref, got_down_ref, down_far_ref)
    up_far = fold(1, up_ref, got_up_ref, up_far_ref)

    def grad_heads(s):
        at = span(s * share, share)
        grad = dot(ga_ref[s], w_out_ref[...], NT).astype(BF16).astype(F32)
        go_ref[at, :] = (grad * keep_ref[at, :]).astype(BF16)

    ga_own.wait()
    grad_heads(t)
    mixed_take.wait()
    mixed_own.start()
    ga_core.wait_recv()
    grad_heads(t ^ 1)
    ga_y.wait_recv()
    ga_y_core = send(ga_ref.at[t ^ 2], ga_ref.at[t ^ 2], core)
    grad_heads(t ^ 2)
    ga_y_core.wait_recv()
    grad_heads(t ^ 3)

    tile = tile_in.shape[-1]
    per = reach // tile

    def put_tile(slot, place, chunk, count):
        d, k = place
        return pltpu.make_async_copy(
            tile_out.at[slot, pl.ds(0, count)],
            leave_ref.at[d, pl.ds(chunk, count), span(k * tile, tile)],
            tile_out_sems.at[slot],
        )

    def store_tile(index, total, chunk, count):
        slot = index % 2
        d, k = index // per, index % per
        leaving = index < per * (copies - 1)

        @pl.when(leaving)
        def _():
            @pl.when(index >= 2)
            def _():
                put_tile(slot, ((index - 2) // per, (index - 2) % per), chunk, count).wait()

            for c in range(count):
                tile_out[slot, c] = total[:, c * own : (c + 1) * own].astype(BF16)
            put_tile(slot, (d, k), chunk, count).start()

        @pl.when(jnp.logical_not(leaving))
        def _():
            for c in range(count):
                kept_ref[chunk + c, span(k * tile, tile), :] = total[
                    :, c * own : (c + 1) * own
                ].astype(BF16)

    def tile_row(index):
        return lax.rem(x + 1 + index // per, copies) * per + index % per

    last = per * (copies - 1)

    def settle(chunk, count):
        for index in range(max(0, last - 2), last):
            put_tile(index % 2, (index // per, index % per), chunk, count).wait()
        return [
            [
                send(leave_ref.at[d - 1, chunk + c], got_x_ref.at[d - 1, chunk + c], twins[d - 1])
                for d in range(1, copies)
            ]
            for c in range(count)
        ]

    def out_tile(index, carry):
        lanes = span(tile_row(index) * tile, tile)
        left = ga_ref[:, :, lanes].reshape(rows, tile)
        store_tile(index, dot(left, heads_ref[...], TN), 0, 1)
        return carry

    loaded[0].wait()
    lax.fori_loop(0, last, out_tile, 0)
    crossing = settle(0, 1)
    lax.fori_loop(last, last + per, out_tile, 0)

    for copy in loaded[1:]:
        copy.wait()

    def turn_back(grad, at):
        grad = grad.astype(BF16).astype(F32)
        back = grad * cos_ref[at] - pltpu.roll(grad, HEAD_DIM // 2, 1) * sin_ref[at]
        return back.astype(BF16)

    for head in range(heads):
        lanes = slice(head * HEAD_DIM, (head + 1) * HEAD_DIM)
        for block in reversed(range(blocks)):
            length = (block + 1) * QBLOCK
            at = slice(block * QBLOCK, length)
            query, keys, grad = q_ref[at, lanes], k_ref[:length, lanes], go_ref[at, lanes]
            scores = masked_scores(query, keys, first_ref[at], block, length)
            probs = jnp.exp(scores - log_ref[at, head : head + 1])
            grad_probs = dot(grad, v_ref[:length, lanes], NT)
            inner = jnp.sum(probs * grad_probs, -1, keepdims=True)
            grad_scores = (probs * (grad_probs - inner)).astype(BF16)
            dq = dot(grad_scores, keys, NN) * HEAD_DIM**-0.5
            gp_ref[at, lanes] = turn_back(dq, at)
            dk = dot(grad_scores, query, TN)
            dv = dot(probs.astype(BF16), grad, TN)
            if block == blocks - 1:
                dk_ref[...] = dk
                dv_ref[...] = dv
            else:
                dk_ref[:length] += dk
                dv_ref[:length] += dv
        gp_ref[:, own + head * HEAD_DIM : own + (head + 1) * HEAD_DIM] = turn_back(
            dk_ref[...] * HEAD_DIM**-0.5, slice(None)
        )
        gp_ref[:, 2 * own + head * HEAD_DIM : 2 * own + (head + 1) * HEAD_DIM] = dv_ref[
            ...
        ].astype(BF16)

    ga_y.wait_send()
    ga_y_core.wait_send()

    def norm1_part(s):
        at = span(s * share, share)
        for lanes in (slice(0, width // 2), slice(width // 2, width)):
            total = dot(gp_ref[at, :own], w_ref[0, lanes, :], NT)
            total += dot(gp_ref[at, own : 2 * own], w_ref[1, lanes, :], NT)
            total += dot(gp_ref[at, 2 * own :], w_ref[2, lanes, :], NT)
            part_ref[:, lanes] = total

    norm1_part(t ^ 3)
    ga_ref[0] = part_ref[...].astype(BF16)
    core_pass = send(ga_ref.at[0], got_core_ref.at[0], core)
    norm1_part(t ^ 1)
    ga_ref[1] = part_ref[...].astype(BF16)
    core_own = send(ga_ref.at[1], got_core_ref.at[1], core)
    norm1_part(t ^ 2)
    core_pass.wait_recv()
    ga_ref[2] = (part_ref[...] + got_core_ref[0].astype(F32)).astype(BF16)
    y_own = send(ga_ref.at[2], got_y_ref, y_side)
    norm1_part(t)

    mixed_y.wait_recv()
    mixed_y_core = send(mixed_ref.at[t ^ 2], mixed_ref.at[t ^ 2], core)

    def fetch(index, slot):
        lanes = span(tile_row(index) * tile, tile)
        return pltpu.make_async_copy(n1_ref.at[:, lanes], tile_in.at[slot], tile_sems.at[slot])

    fetch(0, 0).start()

    def qkv_tile(index, carry):
        slot = index % 2
        fetch(index, slot).wait()

        @pl.when(index < last + per - 1)
        def _():
            fetch(index + 1, 1 - slot).start()

        store_tile(index, dot(tile_in[slot], gp_ref[...], TN), 1, 3)
        return carry

    lax.fori_loop(0, last, qkv_tile, 0)
    crossing += settle(1, 3)
    to_twins(down_own_ref, down_twin_ref)
    lax.fori_loop(last, last + per, qkv_tile, 0)

    def first_step(chunk):
        for copy in crossing[chunk]:
            copy.wait_recv()

        def total(index):
            at = span(index * part, part)
            value = kept_ref[chunk, at, :].astype(F32)
            for d in range(copies - 1):
                value += got_x_ref[d, chunk, at, :].astype(F32)
            return value

        z_send[chunk, 1] = total(z ^ 3).astype(BF16)
        one = send(z_send.at[chunk, 1], got_z1.at[chunk, 1], near)
        z_send[chunk, 0] = total(z ^ 1).astype(BF16)
        two = send(z_send.at[chunk, 0], got_z1.at[chunk, 0], near)
        z_kept[chunk] = total(z ^ 2)
        sums_ref[chunk] = total(z)
        return one, two

    def second_step(chunk, pair):
        one, two = pair
        one.wait_recv()
        one.wait_send()
        begun[:] = [copy for copy in begun if copy is not one]
        z_send[chunk, 1] = (z_kept[chunk] + got_z1[chunk, 1].astype(F32)).astype(BF16)
        gone = send(z_send.at[chunk, 1], got_z2.at[chunk], far)
        two.wait_recv()
        sums_ref[chunk] += got_z1[chunk, 0].astype(F32)
        return gone

    def third_step(chunk, gone):
        gone.wait_recv()
        sums_ref[chunk] += got_z2[chunk].astype(F32)

    mixed_own.wait()
    core_own.wait_recv()
    y_own.wait_recv()
    small_ref[...] = small_in_ref[...]
    lines = 64
    count = small_in_ref.shape[0] - 2

    def finish(j, carry):
        at = span(j * lines, lines)
        grad = part_ref[at, :] + got_core_ref[1, at, :].astype(F32) + got_y_ref[at, :].astype(F32)
        hat, inverse = norm_parts(tokens_ref[at, :].astype(F32))
        back, gain_grad, bias_grad = norm_backward(grad, hat, inverse, gain1_ref[...])
        tg_own_ref[at, :] = (gx2_ref[at, :] + back).astype(BF16)
        small_ref[count : count + 1, :] += gain_grad[None, :]
        small_ref[count + 1 : count + 2, :] += bias_grad[None, :]
        return carry

    lax.fori_loop(0, share // lines, finish, 0)
    tg_y = send(tg_own_ref, tg_ref.at[t], y_side)
    tg_core = send(tg_own_ref, tg_ref.at[t], core)
    tg_own = pltpu.make_async_copy(tg_own_ref, tg_ref.at[t], local_sems.at[2])
    tg_own.start()

    def small_step(step, devices):
        small_send[step] = small_ref[...]
        exchanged = [
            send(small_send.at[step], got_small.at[step + d], device)
            for d, device in enumerate(devices)
        ]
        for d, copy in enumerate(exchanged):
            copy.wait_recv()
            small_ref[...] += got_small[step + d]

    small_step(0, [core])
    pairs = {0: first_step(0)}
    gone = {0: second_step(0, pairs[0])}
    tg_y.wait_recv()
    tg_y_core = send(tg_ref.at[t ^ 2], tg_ref.at[t ^ 2], core)
    small_step(1, [y_side])
    for chunk in (1, 2, 3):
        pairs[chunk] = first_step(chunk)
        third_step(chunk - 1, gone[chunk - 1])
        if chunk == 3:
            small_step(4, twins)
        gone[chunk] = second_step(chunk, pairs[chunk])
    small_step(2, [near])
    third_step(3, gone[3])
    small_step(3, [far])
    for copy in (core_own, mixed_core, mixed_y_core, tg_core, tg_y_core, down_far, up_far, *twin_copies):
        if copy is not core_own:
            copy.wait_recv()
    tg_own.wait()
    for copy in begun:
        if copy is not ga_y and copy is not ga_y_core:
            copy.wait_send()


def back_call(
    queries, keys, values, heads, logs, first, keep, tables_, w_out, w3, gain1, tokens_own,
    grad_middle, small, grad_own, mixed_own, normed1, *level_grads,
):
    rows, own = queries.shape
    share, width = grad_own.shape
    copies, owners = lax.axis_size("dp"), lax.axis_size("bucket")
    splits = rows // share
    reach = width // copies
    part = reach // owners
    half = level_grads[0].shape[1]
    inside = pl.BlockSpec(memory_space=pltpu.VMEM)
    outside = pl.BlockSpec(memory_space=pl.ANY)
    shape = jax.ShapeDtypeStruct
    dma = lambda *count: pltpu.SemaphoreType.DMA(count)
    vmem = lambda dtype, *size: pltpu.VMEM(size, dtype)
    others = copies - 1
    few = 256
    sends = 30 + 7 * others
    return pl.pallas_call(
        functools.partial(back_kernel, copies),
        in_specs=[inside] * 10 + [outside] * 14,
        out_specs=[inside] * 2 + [outside] * 7,
        out_shape=[
            shape((4, part, own), F32),
            shape(small.shape, F32),
            shape((splits, share, width), BF16),
            shape((splits, share, width), BF16),
            *[shape((reach, half), BF16)] * 2,
            *[shape((others, reach, half), BF16)] * 2,
            shape((others, 4, reach, own), BF16),
        ],
        scratch_shapes=[
            vmem(BF16, rows, own),
            vmem(BF16, rows, own),
            vmem(BF16, rows, own),
            vmem(BF16, rows, own),
            vmem(BF16, *w3.shape),
            vmem(BF16, splits, share, width),
            vmem(BF16, rows, own),
            vmem(BF16, rows, 3 * own),
            vmem(F32, rows, HEAD_DIM),
            vmem(F32, rows, HEAD_DIM),
            vmem(BF16, 2, share, width),
            vmem(BF16, share, width),
            vmem(F32, share, width),
            vmem(BF16, share, width),
            vmem(BF16, 2, rows, 256),
            vmem(BF16, 2, 3, 256, own),
            vmem(BF16, 2, few, half),
            vmem(BF16, 2, others, few, half),
            vmem(BF16, 2, reach, half),
            vmem(BF16, 4, reach, own),
            vmem(BF16, others, 4, reach, own),
            vmem(BF16, 4, 2, part, own),
            vmem(F32, 4, part, own),
            vmem(BF16, 4, 2, part, own),
            vmem(BF16, 4, part, own),
            vmem(F32, 4 + others, *small.shape),
            vmem(F32, 5, *small.shape),
            dma(sends),
            dma(sends),
            dma(4),
            dma(2),
            dma(2),
            dma(copies, 2),
            dma(5),
        ],
        compiler_params=pltpu.CompilerParams(
            vmem_limit_bytes=62 << 20, collective_id=2, has_side_effects=True
        ),
        cost_estimate=pl.CostEstimate(
            flops=16 * rows * width * own + 10 * rows * rows * own,
            bytes_accessed=80 << 20,
            transcendentals=rows * rows * own // HEAD_DIM,
        ),
        name="back",
    )(
        logs, first, keep, *tables_, w_out, gain1, tokens_own, grad_middle, small,
        queries, keys, values, heads, w3, grad_own, mixed_own, normed1, *level_grads,
    )


def local(
    tokens,
    cotangent,
    lengths,
    head_quarters,
    buckets,
    ln1_gain,
    ln1_bias,
    w_qkv,
    w_out,
    ln2_gain,
    ln2_bias,
    w_router,
    w_up,
    w_down,
):
    tok_rows, model_width = tokens.shape
    owners = lax.axis_size("bucket")
    splits = lax.axis_size("tensor")
    copies = lax.axis_size("dp")
    share = tok_rows // splits
    t, z, x = lax.axis_index("tensor"), lax.axis_index("bucket"), lax.axis_index("dp")
    up_own = w_up.reshape(model_width, -1)
    down_own = w_down.reshape(-1, model_width)
    hidden_width = up_own.shape[1]

    levels = buckets[:, 0].astype(F32).reshape(-1, HEAD_DIM)

    def shard(values, bit):
        return lax.dynamic_slice_in_dim(values, (t ^ bit) * share, share, 0)

    first = layout(lengths[0], tok_rows)[:, None]
    keep = (t < head_quarters).astype(F32)[:, None]
    w3 = jnp.transpose(w_qkv, (1, 0, 2))
    (
        logs,
        middle,
        cosine,
        sine,
        normed1,
        queries,
        keys,
        values,
        heads_low,
        n2,
        up_other,
        down_other,
        near_cotangent,
        near_levels,
    ) = front_call(
        tokens,
        (ln1_gain.reshape(1, -1), ln1_bias.reshape(1, -1)),
        w3,
        first,
        keep,
        w_out,
        (ln2_gain.reshape(1, -1), ln2_bias.reshape(1, -1)),
        up_own,
        down_own,
        cotangent.reshape(splits, share, model_width),
        levels,
    )
    level_all = jnp.concatenate([levels.reshape(-1), near_levels.reshape(-1)], 0)[:, None]
    (
        mixed_own,
        grad_middle,
        grad_attention_own,
        small,
        _,
        _,
        down_own,
        down_other,
        up_own,
        up_other,
        got_down,
        got_up,
    ) = middle_call(
        n2,
        cotangent,
        near_cotangent,
        (up_own, up_other),
        (down_own, down_other),
        w_router,
        level_all,
        middle,
        (ln2_gain.reshape(1, -1), ln2_bias.reshape(1, -1)),
    )
    sums, small, mixed, tokens_grad, down_far, up_far, down_twin, up_twin, _ = back_call(
        queries,
        keys,
        values,
        heads_low,
        logs,
        first,
        keep,
        (cosine, sine),
        w_out,
        w3,
        ln1_gain.reshape(1, -1),
        shard(tokens, 0),
        grad_middle,
        jnp.concatenate([small, jnp.zeros((2, model_width), F32)], 0),
        grad_attention_own,
        mixed_own,
        normed1,
        down_other,
        got_down,
        up_other,
        got_up,
        down_own,
        up_own,
    )
    size = model_width // copies

    def level_grad(own, twin, distant):
        mine = lax.dynamic_slice_in_dim(own, x * size, size, 0).astype(F32)
        return mine + jnp.sum(twin.astype(F32), 0) + distant.astype(F32)

    grad_down = level_grad(down_own, down_twin, down_far).T
    grad_up = level_grad(up_own, up_twin, up_far)
    width = model_width // (copies * owners)
    small = lax.dynamic_slice_in_dim(small, (x * owners + z) * width, width, 1)
    return (
        mixed.reshape(tok_rows, model_width),
        tokens_grad.reshape(tok_rows, model_width).astype(F32),
        small[2 + owners],
        small[3 + owners],
        jnp.transpose(sums[1:], (1, 0, 2)),
        sums[0].T,
        small[0],
        small[1],
        small[2 : 2 + owners].T,
        grad_up.reshape(-1, 1, hidden_width),
        grad_down.reshape(1, hidden_width, -1),
    )


def solution(mesh):
    placed = (
        P(("dp", "bucket"), None),
        P(("dp", "bucket"), None),
        P(("dp", "bucket"), None),
        P(("dp", "bucket")),
        P(("dp", "bucket"), None),
        P(),
        P(),
        P(None, None, "tensor"),
        P("tensor", None),
        P(),
        P(),
        P(),
        P(None, "bucket", "tensor"),
        P("bucket", "tensor", None),
    )
    return jax.shard_map(
        local,
        mesh=mesh,
        in_specs=placed,
        out_specs=(
            P(("dp", "bucket"), None),
            P(("dp", "bucket"), None),
            P(("dp", "bucket")),
            P(("dp", "bucket")),
            P(("dp", "bucket"), None, "tensor"),
            P("tensor", ("dp", "bucket")),
            P(("dp", "bucket")),
            P(("dp", "bucket")),
            P(("dp", "bucket"), None),
            P("dp", "bucket", "tensor"),
            P("bucket", "tensor", "dp"),
        ),
        check_vma=False,
    )
```

```python
import functools
import math

import jax
import jax.numpy as jnp
from jax import lax
from jax.experimental import pallas as pl
from jax.experimental.pallas import tpu as pltpu
from jax.sharding import PartitionSpec as P

HEAD_DIM = 128
QBLOCK = 256
EPS = 1e-05
HIGH = lax.Precision.HIGHEST
NEGATIVE = -1e30
F32 = jnp.float32
BF16 = jnp.bfloat16


def norm_parts(values):
    centred = values - jnp.mean(values, -1, keepdims=True)
    inverse = lax.rsqrt(jnp.mean(centred * centred, -1, keepdims=True) + EPS)
    return centred * inverse, inverse


def norm_backward(grad_in, normed, inverse, gain):
    scaled = grad_in * gain
    inner = (
        scaled
        - jnp.mean(scaled, -1, keepdims=True)
        - normed * jnp.mean(scaled * normed, -1, keepdims=True)
    )
    return inverse * inner, jnp.sum(grad_in * normed, 0), jnp.sum(grad_in, 0)


def layout(lengths_row, tok_rows):
    ends = jnp.cumsum(lengths_row)
    starts = ends - lengths_row
    tok_index = jnp.arange(tok_rows, dtype=jnp.int32)
    segments = jnp.sum((tok_index[:, None] >= ends[None, :]).astype(jnp.int32), 1)
    chosen = segments[:, None] == jnp.arange(lengths_row.shape[0], dtype=jnp.int32)[None, :]
    return jnp.sum(jnp.where(chosen, starts[None, :], 0), 1)


def dot(left, right, dims):
    return lax.dot_general(left, right, (dims, ((), ())), preferred_element_type=F32)


NN = ((1,), (0,))
NT = ((1,), (1,))
TN = ((0,), (0,))


def masked_scores(query, keys, first, block, length):
    scores = dot(query, keys, NT) * HEAD_DIM**-0.5
    key_at = lax.broadcasted_iota(jnp.int32, (QBLOCK, length), 1)
    row_at = lax.broadcasted_iota(jnp.int32, (QBLOCK, length), 0) + block * QBLOCK
    allowed = (key_at >= first) & (key_at <= row_at)
    return jnp.where(allowed, scores, NEGATIVE)


class Copies:
    def __init__(self, send_sems, recv_sems):
        self.send_sems, self.recv_sems, self.used = send_sems, recv_sems, 0

    def make(self, source, target, device):
        slot = self.used
        self.used += 1
        return pltpu.make_async_remote_copy(
            src_ref=source,
            dst_ref=target,
            send_sem=self.send_sems.at[slot],
            recv_sem=self.recv_sems.at[slot],
            device_id=device,
            device_id_type=pl.DeviceIdType.MESH,
        )

    def start(self, source, target, device):
        copy = self.make(source, target, device)
        copy.start()
        return copy


def meet(devices):
    barrier = pltpu.get_barrier_semaphore()
    for device in devices:
        pl.semaphore_signal(barrier, inc=1, device_id=device, device_id_type=pl.DeviceIdType.MESH)
    pl.semaphore_wait(barrier, len(devices))


def front_kernel(
    copies,
    gain1_ref,
    bias1_ref,
    first_ref,
    keep_ref,
    gain2_ref,
    bias2_ref,
    tokens_in,
    w_in,
    w_out_in,
    up_ref,
    down_ref,
    cot_ref,
    level_ref,
    log_ref,
    middle_ref,
    cos_ref,
    sin_ref,
    n1_out,
    q_out,
    k_out,
    v_out,
    heads_out,
    n2_ref,
    up_other_ref,
    down_other_ref,
    near_cot_ref,
    near_level_ref,
    tokens_ref,
    w_ref,
    w_out_ref,
    n1_ref,
    q_ref,
    k_ref,
    v_ref,
    heads_ref,
    away_ref,
    got_core_ref,
    pass_ref,
    got_y_ref,
    own_ref,
    send_sems,
    recv_sems,
    in_sems,
    out_sems,
):
    t, z, x = lax.axis_index("tensor"), lax.axis_index("bucket"), lax.axis_index("dp")
    rows, own = q_ref.shape
    share = own_ref.shape[0]
    heads = own // HEAD_DIM
    blocks = rows // QBLOCK
    core, y_side = {"tensor": t ^ 1}, {"tensor": t ^ 2}
    near, far = {"bucket": z ^ 1}, {"bucket": z ^ 2}
    twins = [{"dp": lax.rem(x + d, copies)} for d in range(1, copies)]

    def token_block(i):
        at = pl.ds(pl.multiple_of(i * QBLOCK, QBLOCK), QBLOCK)
        return pltpu.make_async_copy(tokens_in.at[at], tokens_ref.at[at], in_sems.at[i])

    w_copies = [
        pltpu.make_async_copy(w_in.at[part], w_ref.at[part], in_sems.at[blocks + part])
        for part in range(3)
    ]
    w_out_copy = pltpu.make_async_copy(w_out_in, w_out_ref, in_sems.at[blocks + 3])
    token_block(0).start()
    for copy in w_copies:
        copy.start()
    for i in range(1, blocks):
        token_block(i).start()
    w_out_copy.start()

    meet([core, y_side, near, far] + twins)
    links = Copies(send_sems, recv_sems)
    begun = []

    def send(source, target, device):
        copy = links.start(source, target, device)
        begun.append(copy)
        return copy

    def piece(ref, quarter):
        size = ref.shape[0] // copies // 4
        return ref.at[pl.ds(pl.multiple_of((x * 4 + quarter) * size, 16), size)]

    def fetch(ref, other_ref, quarter):
        copy = links.make(piece(ref, quarter), piece(other_ref, quarter), far)
        begun.append(copy)
        return copy

    outer = lax.rem(z, 2) == z // 2
    pieces = [fetch(up_ref, up_other_ref, quarter) for quarter in range(4)]
    pieces += [fetch(down_ref, down_other_ref, quarter) for quarter in range(4)]
    parity = lax.rem(t, 2)
    cots = [
        links.make(cot_ref.at[parity + i], near_cot_ref.at[parity + i], near) for i in (0, 2)
    ]
    begun.extend(cots)
    to_twins = [
        [links.make(ref, ref, device) for device in twins]
        for ref in [piece(up_other_ref, quarter) for quarter in range(4)]
        + [piece(down_other_ref, quarter) for quarter in range(4)]
    ]
    to_core_cots = [
        links.make(near_cot_ref.at[parity + i], near_cot_ref.at[parity + i], core) for i in (0, 2)
    ]

    def begin(copies_):
        for copy in copies_:
            copy.start()

    def pass_weights(indices):
        for index in indices:
            pieces[index].wait_recv()
            begin(to_twins[index])

    def pass_cots():
        for copy, onward_copy in zip(cots, to_core_cots):
            copy.wait_recv()
            onward_copy.start()

    @pl.when(outer)
    def _():
        begin(pieces)

    @pl.when(jnp.logical_not(outer))
    def _():
        begin(cots)

    near_level = send(level_ref, near_level_ref, near)

    half = HEAD_DIM // 2
    lane = lax.broadcasted_iota(jnp.int32, (1, HEAD_DIM), 1)
    freq = jnp.exp((lane % half).astype(F32) * (-math.log(10000.0) / half))
    side = jnp.where(lane < half, -1.0, 1.0)

    def project(i, carry):
        at = pl.ds(pl.multiple_of(i * QBLOCK, QBLOCK), QBLOCK)
        token_block(i).wait()
        normed, _ = norm_parts(tokens_ref[at, :].astype(F32))
        low = (normed * gain1_ref[...] + bias1_ref[...]).astype(BF16)
        n1_ref[at, :] = low
        token = lax.broadcasted_iota(jnp.int32, (QBLOCK, 1), 0) + i * QBLOCK
        angle = (token - first_ref[at, :]).astype(F32) * freq
        cosine, sine = jnp.cos(angle), jnp.sin(angle) * side
        cos_ref[at, :] = cosine
        sin_ref[at, :] = sine
        for part, out_ref in enumerate((q_ref, k_ref, v_ref)):

            @pl.when(i == 0)
            def _():
                w_copies[part].wait()

            projected = dot(low, w_ref[part], NN)
            if part == 2:
                out_ref[at, :] = projected.astype(BF16)
                continue
            for start in range(0, own, HEAD_DIM):
                head = projected[:, start : start + HEAD_DIM]
                turned = head * cosine + pltpu.roll(head, half, 1) * sine
                out_ref[at, start : start + HEAD_DIM] = turned.astype(BF16)
        return carry

    lax.fori_loop(0, blocks, project, 0)
    outs = [
        pltpu.make_async_copy(ref, out, out_sems.at[i])
        for i, (ref, out) in enumerate(
            ((n1_ref, n1_out), (q_ref, q_out), (k_ref, k_out), (v_ref, v_out), (heads_ref, heads_out))
        )
    ]
    for copy in outs[:4]:
        copy.start()

    for head in range(heads):
        lanes = slice(head * HEAD_DIM, (head + 1) * HEAD_DIM)
        for block in range(rows // QBLOCK):
            length = (block + 1) * QBLOCK
            at = slice(block * QBLOCK, length)
            scores = masked_scores(
                q_ref[at, lanes], k_ref[:length, lanes], first_ref[at], block, length
            )
            most = jnp.max(scores, -1, keepdims=True)
            expo = jnp.exp(scores - most)
            total = jnp.sum(expo, -1, keepdims=True)
            weights = (expo * (1.0 / total)).astype(BF16)
            out = dot(weights, v_ref[:length, lanes], NN)
            heads_ref[at, lanes] = (out * keep_ref[at]).astype(BF16)
            log_ref[at, head : head + 1] = most + jnp.log(total)

    outs[4].start()
    w_out_copy.wait()

    def attended(index):
        at = pl.ds(pl.multiple_of(index * share, share), share)
        return dot(heads_ref[at, :], w_out_ref[...], NN)

    away_ref[1] = attended(t ^ 3).astype(BF16)
    to_core1 = send(away_ref.at[1], got_core_ref.at[1], core)
    away_ref[0] = attended(t ^ 1).astype(BF16)
    to_core0 = send(away_ref.at[0], got_core_ref.at[0], core)
    passed = attended(t ^ 2)
    to_core1.wait_recv()
    pass_ref[...] = (passed + got_core_ref[1].astype(F32)).astype(BF16)
    to_y = send(pass_ref, got_y_ref, y_side)
    middle = attended(t)
    middle += tokens_ref[pl.ds(pl.multiple_of(t * share, share), share), :].astype(F32)
    to_core0.wait_recv()
    middle_ref[...] = middle + got_core_ref[0].astype(F32)

    @pl.when(jnp.logical_not(outer))
    def _():
        pass_weights(range(8))
        begin(pieces)

    @pl.when(outer)
    def _():
        begin(cots)
        pass_cots()

    to_y.wait_recv()
    total = middle_ref[...] + got_y_ref[...].astype(F32)
    middle_ref[...] = total
    normed, _ = norm_parts(total)
    own_ref[...] = (normed * gain2_ref[...] + bias2_ref[...]).astype(BF16)
    own_y = send(own_ref, n2_ref.at[t], y_side)
    own_core = send(own_ref, n2_ref.at[t], core)
    keep_own = pltpu.make_async_copy(own_ref, n2_ref.at[t], in_sems.at[0])
    keep_own.start()

    @pl.when(outer)
    def _():
        pass_weights(range(4))

    own_y.wait_recv()
    y_core = send(n2_ref.at[t ^ 2], n2_ref.at[t ^ 2], core)

    @pl.when(outer)
    def _():
        pass_weights(range(4, 8))

    @pl.when(jnp.logical_not(outer))
    def _():
        pass_cots()

    keep_own.wait()
    for copy in outs:
        copy.wait()
    for copy in (near_level, own_core, y_core, *to_core_cots, *sum(to_twins, [])):
        copy.wait_recv()
    for copy in (*begun, *to_core_cots, *sum(to_twins, [])):
        copy.wait_send()


def front_call(tokens, ln1, w3, first, keep, w_out, ln2, up, down, cotangent, levels):
    rows, width = tokens.shape
    own = w3.shape[2]
    splits, copies = lax.axis_size("tensor"), lax.axis_size("dp")
    share = rows // splits
    inside = pl.BlockSpec(memory_space=pltpu.VMEM)
    outside = pl.BlockSpec(memory_space=pl.ANY)
    shape = jax.ShapeDtypeStruct
    vmem = lambda dtype, *size: pltpu.VMEM(size, dtype)
    total = 19 + 8 * (copies - 1)
    narrow = shape((rows, own), BF16)
    return pl.pallas_call(
        functools.partial(front_kernel, copies),
        in_specs=[inside] * 6 + [outside] * 7,
        out_specs=[inside] * 4 + [outside] * 10,
        out_shape=[
            shape((rows, own // HEAD_DIM), F32),
            shape((share, width), F32),
            shape((rows, HEAD_DIM), F32),
            shape((rows, HEAD_DIM), F32),
            shape((rows, width), BF16),
            narrow,
            narrow,
            narrow,
            narrow,
            shape((splits, share, width), BF16),
            shape(up.shape, BF16),
            shape(down.shape, BF16),
            shape((splits, share, width), BF16),
            shape(levels.shape, F32),
        ],
        scratch_shapes=[
            vmem(BF16, rows, width),
            vmem(BF16, *w3.shape),
            vmem(BF16, *w_out.shape),
            vmem(BF16, rows, width),
            vmem(BF16, rows, own),
            vmem(BF16, rows, own),
            vmem(BF16, rows, own),
            vmem(BF16, rows, own),
            vmem(BF16, 2, share, width),
            vmem(BF16, 2, share, width),
            vmem(BF16, share, width),
            vmem(BF16, share, width),
            vmem(BF16, share, width),
            pltpu.SemaphoreType.DMA((total,)),
            pltpu.SemaphoreType.DMA((total,)),
            pltpu.SemaphoreType.DMA((rows // QBLOCK + 4,)),
            pltpu.SemaphoreType.DMA((5,)),
        ],
        compiler_params=pltpu.CompilerParams(
            vmem_limit_bytes=56 << 20, collective_id=0, has_side_effects=True
        ),
        cost_estimate=pl.CostEstimate(
            flops=8 * rows * width * own + 4 * rows * rows * own,
            bytes_accessed=60 << 20,
            transcendentals=rows * rows * own // HEAD_DIM,
        ),
        name="front",
    )(*ln1, first, keep, *ln2, tokens, w3, w_out, up, down, cotangent, levels)


def block_at(i, t):
    near, j = i // 4, i % 4
    own_bit = (1 - j // 2) * (3 - 2 * j) + (j // 2) * (6 - 2 * j)
    bit = (1 - near) * own_bit + near * (j + 1 - 2 * (j % 2))
    return near, t ^ bit


def router_gate(rows, w_router_ref, level):
    logits = dot(rows, w_router_ref[...], NN)
    expo = jnp.exp(logits - jnp.max(logits, -1, keepdims=True))
    probs = expo / jnp.sum(expo, -1, keepdims=True)
    number = lax.broadcasted_iota(jnp.int32, probs.shape, 1).astype(F32)
    onehot = (number == level).astype(F32)
    return jnp.sum(probs * onehot, -1, keepdims=True), probs, onehot


def middle_kernel(
    copies,
    n2_ref,
    cot_ref,
    near_cot_ref,
    up_own_ref,
    up_other_ref,
    down_own_ref,
    down_other_ref,
    router_ref,
    level_ref,
    gain2_ref,
    bias2_ref,
    x2_in,
    mixed_ref,
    gx2_ref,
    ga_ref,
    small_ref,
    near_n2_ref,
    gf_ref,
    down_own_grad,
    down_other_grad,
    up_own_grad,
    up_other_grad,
    got_down_ref,
    got_up_ref,
    n2_in,
    cot_in,
    gf_out,
    hid_ref,
    gu_ref,
    part_f,
    part_g,
    hold_f,
    send_ref,
    core_f,
    core_g,
    got_fz,
    got_fy,
    got_gy,
    got_gz,
    tile_in,
    tile_out,
    core_send_sems,
    core_recv_sems,
    send_sems,
    recv_sems,
    in_sems,
    out_sems,
    tile_sems,
    tile_out_sems,
    x2_sem,
):
    t, z, x = lax.axis_index("tensor"), lax.axis_index("bucket"), lax.axis_index("dp")
    share, width = gx2_ref.shape
    half = up_own_ref.shape[1]
    core, y_side, near = {"tensor": t ^ 1}, {"tensor": t ^ 2}, {"bucket": z ^ 1}
    twins = [{"dp": lax.rem(x + d, copies)} for d in range(1, copies)]
    splits = n2_ref.shape[0]

    def load(i, slot, act):
        at, s = block_at(i, t)
        for index, (rows_ref, grads_ref) in enumerate(
            ((n2_ref, cot_ref), (near_n2_ref, near_cot_ref))
        ):

            @pl.when(at == index)
            def _():
                act(pltpu.make_async_copy(rows_ref.at[s], n2_in.at[slot], in_sems.at[slot, 0]))
                act(pltpu.make_async_copy(grads_ref.at[s], cot_in.at[slot], in_sems.at[slot, 1]))

    def begin(copy):
        copy.start()

    def finish_load(copy):
        copy.wait()

    def store(i, slot):
        at, s = block_at(i, t)
        return pltpu.make_async_copy(gf_out.at[slot], gf_ref.at[at, s], out_sems.at[slot])

    def to_core(a):
        return [
            pltpu.make_async_remote_copy(
                src_ref=send_ref.at[kind * 2 + int(a == 1)],
                dst_ref=(core_f, core_g)[kind].at[a],
                send_sem=core_send_sems.at[kind, a],
                recv_sem=core_recv_sems.at[kind, a],
                device_id=core,
                device_id_type=pl.DeviceIdType.MESH,
            )
            for kind in (0, 1)
        ]

    load(0, 0, begin)
    meet([core, y_side, near] + twins)
    links = Copies(send_sems, recv_sems)
    few = share // 2
    late = pl.ds(few, few)
    early = pl.ds(0, few)
    to_near = [
        links.start(n2_ref.at[t, late], near_n2_ref.at[t, late], near),
        links.start(n2_ref.at[t, early], near_n2_ref.at[t, early], near),
        links.start(n2_ref.at[t ^ 2, early], near_n2_ref.at[t ^ 2, early], near),
    ]
    near_y = links.make(near_n2_ref.at[t, late], near_n2_ref.at[t, late], y_side)
    near_core = links.make(near_n2_ref.at[t], near_n2_ref.at[t], core)
    near_y_core = links.make(near_n2_ref.at[t ^ 2], near_n2_ref.at[t ^ 2], core)
    g_own_y = links.make(send_ref.at[4], got_gy.at[1], y_side)
    f_near = links.make(send_ref.at[1], got_fz.at[1], near)
    g_near_y = links.make(send_ref.at[0], got_gy.at[0], y_side)
    f_near_y = links.make(send_ref.at[2], got_fz.at[0], near)
    f_own_y = links.make(send_ref.at[3], got_fy, y_side)
    g_near = links.make(send_ref.at[4], got_gz, near)

    def work(i, carry):
        slot = i % 2
        at, s = block_at(i, t)
        load(i, slot, finish_load)

        @pl.when((i != 3) & (i != 5) & (i != 7))
        def _():
            load(i + 1, 1 - slot, begin)

        @pl.when(i >= 2)
        def _():
            store(i - 2, slot).wait()

        spot = pl.ds(pl.multiple_of((at * splits + s) * share, share), share)
        rows = n2_in[slot]
        level = level_ref[spot, :]
        gate, _, _ = router_gate(rows, router_ref, level)
        grad = (gate * cot_in[slot].astype(F32)).astype(BF16)
        gf_out[slot] = grad
        store(i, slot).start()
        for part, (up_ref, down_ref, unit_level) in enumerate(
            ((up_own_ref, down_own_ref, z), (up_other_ref, down_other_ref, z ^ 2))
        ):
            lanes = slice(part * half, (part + 1) * half)
            kept = level >= unit_level.astype(F32)
            act = jnp.where(kept, jnp.maximum(dot(rows, up_ref[...], NN), 0.0), 0.0)
            hid_ref[spot, lanes] = (act * act).astype(BF16)
            back = dot(grad, down_ref[...], NT)
            gu_ref[spot, lanes] = (back * 2.0 * act).astype(BF16)
        for lanes in (slice(0, width // 2), slice(width // 2, width)):
            part_f[:, lanes] = dot(hid_ref[spot, :half], down_own_ref[:, lanes], NN) + dot(
                hid_ref[spot, half:], down_other_ref[:, lanes], NN
            )
            part_g[:, lanes] = dot(gu_ref[spot, :half], up_own_ref[lanes, :], NT) + dot(
                gu_ref[spot, half:], up_other_ref[lanes, :], NT
            )

        def leave(a):
            for before in {2: (0,), 3: (2,)}.get(a, ()):
                for copy in to_core(before):
                    copy.wait_send()
            send_ref[int(a == 1)] = part_f[...].astype(BF16)
            send_ref[2 + int(a == 1)] = part_g[...].astype(BF16)
            for copy in to_core(a):
                copy.start()

        for a, index in enumerate((0, 1, 4, 6)):

            @pl.when(i == index)
            def _():
                leave(a)

        def with_core(kind, a):
            to_core(a)[kind].wait_recv()
            got = (core_f, core_g)[kind][a].astype(F32)
            return (part_f, part_g)[kind][...] + got

        @pl.when(i == 1)
        def _():
            to_near[0].wait_recv()
            near_y.start()

        @pl.when(i == 4)
        def _():
            to_near[2].wait_recv()
            near_y.wait_recv()
            near_y_core.start()

        @pl.when(i == 2)
        def _():
            send_ref[4] = with_core(1, 0).astype(BF16)
            g_own_y.start()
            hold_f[...] = with_core(0, 0)

        @pl.when(i == 3)
        def _():
            mixed_ref[...] = with_core(0, 1).astype(BF16)
            ga_ref[...] = with_core(1, 1).astype(BF16)
            to_near[1].wait_recv()
            near_core.start()
            near_core.wait_recv()
            load(i + 1, 1 - slot, begin)

        @pl.when(i == 5)
        def _():
            for copy in to_core(1):
                copy.wait_send()
            send_ref[1] = with_core(0, 2).astype(BF16)
            f_near.start()
            gx2_ref[...] = with_core(1, 2)
            near_y_core.wait_recv()
            load(i + 1, 1 - slot, begin)

        @pl.when(i == 7)
        def _():
            for copy in to_core(3):
                copy.wait_send()
            send_ref[0] = with_core(1, 3).astype(BF16)
            g_near_y.start()
            send_ref[2] = with_core(0, 3).astype(BF16)
            f_near_y.start()

        return carry

    lax.fori_loop(0, 8, work, 0)
    store(6, 0).wait()
    store(7, 1).wait()
    x2_ref = part_f
    x2_copy = pltpu.make_async_copy(x2_in, x2_ref, x2_sem)
    x2_copy.start()

    tile = tile_in.shape[-1]
    tiles = width // tile

    def weight_grads(sources, right_ref, results):
        def fetch(j, slot):
            lanes = pl.ds(pl.multiple_of(j * tile, tile), tile)
            return [
                pltpu.make_async_copy(
                    source.at[:, :, lanes], tile_in.at[slot, index], tile_sems.at[slot, index]
                )
                for index, source in enumerate(sources)
            ]

        def put(j, slot):
            rows = pl.ds(pl.multiple_of(j * tile, tile), tile)
            return [
                pltpu.make_async_copy(
                    tile_out.at[slot, index], result.at[rows, :], tile_out_sems.at[slot, index]
                )
                for index, result in enumerate(results)
            ]

        for copy in fetch(0, 0):
            copy.start()

        def step(j, carry):
            slot = j % 2
            for copy in fetch(j, slot):
                copy.wait()

            @pl.when(j < tiles - 1)
            def _():
                for copy in fetch(j + 1, 1 - slot):
                    copy.start()

            @pl.when(j >= 2)
            def _():
                for copy in put(j - 2, slot):
                    copy.wait()

            left = tile_in[slot].reshape(-1, tile)
            total = dot(left, right_ref[...], TN).astype(BF16)
            for index in (0, 1):
                tile_out[slot, index] = total[:, index * half : (index + 1) * half]
            for copy in put(j, slot):
                copy.start()
            return carry

        lax.fori_loop(0, tiles, step, 0)
        for j in (tiles - 2, tiles - 1):
            for copy in put(j, j % 2):
                copy.wait()

    size = width // copies

    def to_twins(grad_ref, got_ref):
        return [
            links.start(
                grad_ref.at[pl.ds(pl.multiple_of(lax.rem(x + d, copies) * size, size), size), :],
                got_ref.at[d - 1],
                twins[d - 1],
            )
            for d in range(1, copies)
        ]

    weight_grads((gf_ref.at[0], gf_ref.at[1]), hid_ref, (down_own_grad, down_other_grad))
    crossing = to_twins(down_other_grad, got_down_ref)

    weight_grads((n2_ref, near_n2_ref), gu_ref, (up_own_grad, up_other_grad))
    crossing += to_twins(up_other_grad, got_up_ref)

    f_near_y.wait_recv()
    send_ref[3] = (hold_f[...] + got_fz[0].astype(F32)).astype(BF16)
    f_own_y.start()
    g_near_y.wait_recv()
    g_own_y.wait_send()
    send_ref[4] = (gx2_ref[...] + got_gy[0].astype(F32)).astype(BF16)
    g_near.start()

    own = pltpu.make_async_copy(n2_ref.at[t], n2_in.at[0], in_sems.at[0, 0])
    own.start()
    own_cot = pltpu.make_async_copy(cot_ref.at[t], cot_in.at[0], in_sems.at[0, 1])
    own_cot.start()
    own.wait()
    own_cot.wait()
    for copy in (f_near, f_own_y, g_own_y, g_near):
        copy.wait_recv()
    x2_copy.wait()
    small_ref[...] = jnp.zeros_like(small_ref)
    few = 64

    def finish(j, carry):
        at = pl.ds(pl.multiple_of(j * few, few), few)
        level = level_ref[pl.ds(pl.multiple_of(t * share + j * few, few), few), :]
        rows = n2_in[0, at, :]
        gate, probs, onehot = router_gate(rows, router_ref, level)
        branch = mixed_ref[at, :].astype(F32) + got_fz[1, at, :].astype(F32) + got_fy[at, :].astype(F32)
        branch = branch.astype(BF16).astype(F32)
        x2 = x2_ref[at, :]
        mixed_ref[at, :] = (x2 + gate * branch).astype(BF16)
        grad_out = cot_in[0, at, :].astype(F32)
        grad_gate = jnp.sum(grad_out * branch, -1, keepdims=True)
        grad_logits = grad_gate * gate * (onehot - probs)
        returned = ga_ref[at, :].astype(F32) + got_gy[1, at, :].astype(F32) + got_gz[at, :].astype(F32)
        grad_n2 = returned.astype(BF16).astype(F32)
        grad_n2 += lax.dot_general(
            grad_logits,
            router_ref[...].astype(F32),
            (NT, ((), ())),
            precision=HIGH,
            preferred_element_type=F32,
        )
        hat, inverse = norm_parts(x2)
        back, gain_grad, bias_grad = norm_backward(grad_n2, hat, inverse, gain2_ref[...])
        gx2 = grad_out + back
        gx2_ref[at, :] = gx2
        ga_ref[at, :] = gx2.astype(BF16)
        small_ref[0:1, :] += gain_grad[None, :]
        small_ref[1:2, :] += bias_grad[None, :]
        small_ref[2 : 2 + probs.shape[1], :] += lax.dot_general(
            grad_logits, rows.astype(F32), (TN, ((), ())), precision=HIGH, preferred_element_type=F32
        )
        return carry

    lax.fori_loop(0, share // few, finish, 0)
    for copy in crossing:
        copy.wait_recv()
    for copy in (
        *to_near, near_y, near_core, near_y_core, f_near,
        g_near_y, f_near_y, f_own_y, g_near, *crossing,
    ):
        copy.wait_send()


def middle_call(n2, cotangent, near_cotangent, ups, downs, w_router, levels, middle, ln2):
    splits, share, width = n2.shape
    copies = lax.axis_size("dp")
    half = ups[0].shape[1]
    rows = 2 * splits * share
    inside = pl.BlockSpec(memory_space=pltpu.VMEM)
    outside = pl.BlockSpec(memory_space=pl.ANY)
    shape = jax.ShapeDtypeStruct
    block = lambda count, dtype=BF16: pltpu.VMEM((*count, share, width), dtype)
    dma = lambda *count: pltpu.SemaphoreType.DMA(count)
    return pl.pallas_call(
        functools.partial(middle_kernel, copies),
        in_specs=[outside] * 3 + [inside] * 8 + [outside],
        out_specs=[inside] * 4 + [outside] * 8,
        out_shape=[
            shape((share, width), BF16),
            shape((share, width), F32),
            shape((share, width), BF16),
            shape((2 + w_router.shape[1], width), F32),
            shape(n2.shape, BF16),
            shape((2, *n2.shape), BF16),
            *[shape((width, half), BF16)] * 4,
            *[shape((copies - 1, width // copies, half), BF16)] * 2,
        ],
        scratch_shapes=[
            block((2,)),
            block((2,)),
            block((2,)),
            pltpu.VMEM((rows, 2 * half), BF16),
            pltpu.VMEM((rows, 2 * half), BF16),
            block((), F32),
            block((), F32),
            block((), F32),
            block((5,)),
            block((4,)),
            block((4,)),
            block((2,)),
            block(()),
            block((2,)),
            block(()),
            pltpu.VMEM((2, 2, splits, share, 256), BF16),
            pltpu.VMEM((2, 2, 256, half), BF16),
            dma(2, 4),
            dma(2, 4),
            dma(12 + 2 * (copies - 1)),
            dma(12 + 2 * (copies - 1)),
            dma(2, 2),
            dma(2),
            dma(2, 2),
            dma(2, 2),
            pltpu.SemaphoreType.DMA,
        ],
        compiler_params=pltpu.CompilerParams(
            vmem_limit_bytes=62 << 20, collective_id=1, has_side_effects=True
        ),
        cost_estimate=pl.CostEstimate(
            flops=12 * rows * width * 2 * half, bytes_accessed=80 << 20, transcendentals=0
        ),
        name="middle",
    )(n2, cotangent.reshape(splits, share, width), near_cotangent, *ups, *downs, w_router, levels, *ln2, middle)


def back_kernel(
    copies,
    log_ref,
    first_ref,
    keep_ref,
    cos_ref,
    sin_ref,
    w_out_ref,
    gain1_ref,
    gx2_ref,
    small_in_ref,
    tokens_in,
    q_in,
    k_in,
    v_in,
    heads_in,
    w_in,
    ga_in_ref,
    mixed_in_ref,
    n1_ref,
    down_ref,
    got_down_ref,
    up_ref,
    got_up_ref,
    down_own_ref,
    up_own_ref,
    sums_ref,
    small_ref,
    mixed_ref,
    tg_ref,
    down_far_ref,
    up_far_ref,
    down_twin_ref,
    up_twin_ref,
    leave_ref,
    q_ref,
    k_ref,
    v_ref,
    heads_ref,
    w_ref,
    tokens_ref,
    ga_ref,
    go_ref,
    gp_ref,
    dk_ref,
    dv_ref,
    got_core_ref,
    got_y_ref,
    part_ref,
    tg_own_ref,
    tile_in,
    tile_out,
    fold_a,
    fold_b,
    fold_send,
    kept_ref,
    got_x_ref,
    z_send,
    z_kept,
    got_z1,
    got_z2,
    got_small,
    small_send,
    send_sems,
    recv_sems,
    local_sems,
    tile_sems,
    tile_out_sems,
    fold_sems,
    in_sems,
):
    t, z, x = lax.axis_index("tensor"), lax.axis_index("bucket"), lax.axis_index("dp")
    rows, own = q_ref.shape
    splits, share, width = ga_ref.shape
    heads, blocks = own // HEAD_DIM, rows // QBLOCK
    reach = width // copies
    part = got_z2.shape[1]
    core, y_side = {"tensor": t ^ 1}, {"tensor": t ^ 2}
    near, far = {"bucket": z ^ 1}, {"bucket": z ^ 2}
    twins = [{"dp": lax.rem(x + d, copies)} for d in range(1, copies)]
    meet([core, y_side, near, far] + twins)
    links = Copies(send_sems, recv_sems)
    begun = []

    def send(source, target, device):
        copy = links.start(source, target, device)
        begun.append(copy)
        return copy

    def span(start, size):
        return pl.ds(pl.multiple_of(start, size), size)

    ga_y = send(ga_in_ref, ga_ref.at[t], y_side)
    ga_core = send(ga_in_ref, ga_ref.at[t], core)
    ga_own = pltpu.make_async_copy(ga_in_ref, ga_ref.at[t], local_sems.at[0])
    ga_own.start()

    def to_twins(source_ref, target_ref):
        for d in range(1, copies):
            rows_there = span(lax.rem(x + d, copies) * reach, reach)
            twin_copies.append(send(source_ref.at[rows_there], target_ref.at[d - 1], twins[d - 1]))

    twin_copies = []
    to_twins(up_own_ref, up_twin_ref)
    mixed_y = send(mixed_in_ref, mixed_ref.at[t], y_side)
    mixed_core = send(mixed_in_ref, mixed_ref.at[t], core)
    mixed_take = pltpu.make_async_copy(mixed_in_ref, tg_own_ref, local_sems.at[1])
    mixed_take.start()
    mixed_own = pltpu.make_async_copy(tg_own_ref, mixed_ref.at[t], local_sems.at[3])

    loaded = [
        pltpu.make_async_copy(source, target, in_sems.at[index])
        for index, (source, target) in enumerate(
            (
                (heads_in, heads_ref),
                (q_in, q_ref),
                (k_in, k_ref),
                (v_in, v_ref),
                (w_in, w_ref),
                (tokens_in.at[t], tokens_ref),
            )
        )
    ]
    for copy in loaded:
        copy.start()

    few = fold_a.shape[1]

    def fold(which, source_ref, got_ref, target_ref):
        def loads(k, slot):
            mine = pltpu.make_async_copy(
                source_ref.at[span(x * reach + k * few, few)], fold_a.at[slot], fold_sems.at[0, slot]
            )
            theirs = [
                pltpu.make_async_copy(
                    got_ref.at[d, span(k * few, few)], fold_b.at[slot, d], fold_sems.at[1 + d, slot]
                )
                for d in range(copies - 1)
            ]
            return [mine] + theirs

        for copy in loads(0, 0):
            copy.start()
        steps = reach // few

        def step(k, carry):
            slot = k % 2
            for copy in loads(k, slot):
                copy.wait()

            @pl.when(k < steps - 1)
            def _():
                for copy in loads(k + 1, 1 - slot):
                    copy.start()

            total = fold_a[slot].astype(F32)
            for d in range(copies - 1):
                total += fold_b[slot, d].astype(F32)
            fold_send[which, span(k * few, few), :] = total.astype(BF16)
            return carry

        lax.fori_loop(0, steps, step, 0)
        return send(fold_send.at[which], target_ref, far)

    down_far = fold(0, down_ref, got_down_ref, down_far_ref)
    up_far = fold(1, up_ref, got_up_ref, up_far_ref)

    def grad_heads(s):
        at = span(s * share, share)
        grad = dot(ga_ref[s], w_out_ref[...], NT).astype(BF16).astype(F32)
        go_ref[at, :] = (grad * keep_ref[at, :]).astype(BF16)

    ga_own.wait()
    grad_heads(t)
    mixed_take.wait()
    mixed_own.start()
    ga_core.wait_recv()
    grad_heads(t ^ 1)
    ga_y.wait_recv()
    ga_y_core = send(ga_ref.at[t ^ 2], ga_ref.at[t ^ 2], core)
    grad_heads(t ^ 2)
    ga_y_core.wait_recv()
    grad_heads(t ^ 3)

    tile = tile_in.shape[-1]
    per = reach // tile

    def put_tile(slot, place, chunk, count):
        d, k = place
        return pltpu.make_async_copy(
            tile_out.at[slot, pl.ds(0, count)],
            leave_ref.at[d, pl.ds(chunk, count), span(k * tile, tile)],
            tile_out_sems.at[slot],
        )

    def store_tile(index, total, chunk, count):
        slot = index % 2
        d, k = index // per, index % per
        leaving = index < per * (copies - 1)

        @pl.when(leaving)
        def _():
            @pl.when(index >= 2)
            def _():
                put_tile(slot, ((index - 2) // per, (index - 2) % per), chunk, count).wait()

            for c in range(count):
                tile_out[slot, c] = total[:, c * own : (c + 1) * own].astype(BF16)
            put_tile(slot, (d, k), chunk, count).start()

        @pl.when(jnp.logical_not(leaving))
        def _():
            for c in range(count):
                kept_ref[chunk + c, span(k * tile, tile), :] = total[
                    :, c * own : (c + 1) * own
                ].astype(BF16)

    def tile_row(index):
        return lax.rem(x + 1 + index // per, copies) * per + index % per

    last = per * (copies - 1)

    def settle(chunk, count):
        for index in range(max(0, last - 2), last):
            put_tile(index % 2, (index // per, index % per), chunk, count).wait()
        return [
            [
                send(leave_ref.at[d - 1, chunk + c], got_x_ref.at[d - 1, chunk + c], twins[d - 1])
                for d in range(1, copies)
            ]
            for c in range(count)
        ]

    def out_tile(index, carry):
        lanes = span(tile_row(index) * tile, tile)
        left = ga_ref[:, :, lanes].reshape(rows, tile)
        store_tile(index, dot(left, heads_ref[...], TN), 0, 1)
        return carry

    loaded[0].wait()
    lax.fori_loop(0, last, out_tile, 0)
    crossing = settle(0, 1)
    lax.fori_loop(last, last + per, out_tile, 0)

    for copy in loaded[1:]:
        copy.wait()

    def turn_back(grad, at):
        grad = grad.astype(BF16).astype(F32)
        back = grad * cos_ref[at] - pltpu.roll(grad, HEAD_DIM // 2, 1) * sin_ref[at]
        return back.astype(BF16)

    for head in range(heads):
        lanes = slice(head * HEAD_DIM, (head + 1) * HEAD_DIM)
        for block in reversed(range(blocks)):
            length = (block + 1) * QBLOCK
            at = slice(block * QBLOCK, length)
            query, keys, grad = q_ref[at, lanes], k_ref[:length, lanes], go_ref[at, lanes]
            scores = masked_scores(query, keys, first_ref[at], block, length)
            probs = jnp.exp(scores - log_ref[at, head : head + 1])
            grad_probs = dot(grad, v_ref[:length, lanes], NT)
            inner = jnp.sum(probs * grad_probs, -1, keepdims=True)
            grad_scores = (probs * (grad_probs - inner)).astype(BF16)
            dq = dot(grad_scores, keys, NN) * HEAD_DIM**-0.5
            gp_ref[at, lanes] = turn_back(dq, at)
            dk = dot(grad_scores, query, TN)
            dv = dot(probs.astype(BF16), grad, TN)
            if block == blocks - 1:
                dk_ref[...] = dk
                dv_ref[...] = dv
            else:
                dk_ref[:length] += dk
                dv_ref[:length] += dv
        gp_ref[:, own + head * HEAD_DIM : own + (head + 1) * HEAD_DIM] = turn_back(
            dk_ref[...] * HEAD_DIM**-0.5, slice(None)
        )
        gp_ref[:, 2 * own + head * HEAD_DIM : 2 * own + (head + 1) * HEAD_DIM] = dv_ref[
            ...
        ].astype(BF16)

    ga_y.wait_send()
    ga_y_core.wait_send()

    def norm1_part(s):
        at = span(s * share, share)
        for lanes in (slice(0, width // 2), slice(width // 2, width)):
            total = dot(gp_ref[at, :own], w_ref[0, lanes, :], NT)
            total += dot(gp_ref[at, own : 2 * own], w_ref[1, lanes, :], NT)
            total += dot(gp_ref[at, 2 * own :], w_ref[2, lanes, :], NT)
            part_ref[:, lanes] = total

    norm1_part(t ^ 3)
    ga_ref[0] = part_ref[...].astype(BF16)
    core_pass = send(ga_ref.at[0], got_core_ref.at[0], core)
    norm1_part(t ^ 1)
    ga_ref[1] = part_ref[...].astype(BF16)
    core_own = send(ga_ref.at[1], got_core_ref.at[1], core)
    norm1_part(t ^ 2)
    core_pass.wait_recv()
    ga_ref[2] = (part_ref[...] + got_core_ref[0].astype(F32)).astype(BF16)
    y_own = send(ga_ref.at[2], got_y_ref, y_side)
    norm1_part(t)

    mixed_y.wait_recv()
    mixed_y_core = send(mixed_ref.at[t ^ 2], mixed_ref.at[t ^ 2], core)

    def fetch(index, slot):
        lanes = span(tile_row(index) * tile, tile)
        return pltpu.make_async_copy(n1_ref.at[:, lanes], tile_in.at[slot], tile_sems.at[slot])

    fetch(0, 0).start()

    def qkv_tile(index, carry):
        slot = index % 2
        fetch(index, slot).wait()

        @pl.when(index < last + per - 1)
        def _():
            fetch(index + 1, 1 - slot).start()

        store_tile(index, dot(tile_in[slot], gp_ref[...], TN), 1, 3)
        return carry

    lax.fori_loop(0, last, qkv_tile, 0)
    crossing += settle(1, 3)
    to_twins(down_own_ref, down_twin_ref)
    lax.fori_loop(last, last + per, qkv_tile, 0)

    def first_step(chunk):
        for copy in crossing[chunk]:
            copy.wait_recv()

        def total(index):
            at = span(index * part, part)
            value = kept_ref[chunk, at, :].astype(F32)
            for d in range(copies - 1):
                value += got_x_ref[d, chunk, at, :].astype(F32)
            return value

        z_send[chunk, 1] = total(z ^ 3).astype(BF16)
        one = send(z_send.at[chunk, 1], got_z1.at[chunk, 1], near)
        z_send[chunk, 0] = total(z ^ 1).astype(BF16)
        two = send(z_send.at[chunk, 0], got_z1.at[chunk, 0], near)
        z_kept[chunk] = total(z ^ 2)
        sums_ref[chunk] = total(z)
        return one, two

    def second_step(chunk, pair):
        one, two = pair
        one.wait_recv()
        one.wait_send()
        begun[:] = [copy for copy in begun if copy is not one]
        z_send[chunk, 1] = (z_kept[chunk] + got_z1[chunk, 1].astype(F32)).astype(BF16)
        gone = send(z_send.at[chunk, 1], got_z2.at[chunk], far)
        two.wait_recv()
        sums_ref[chunk] += got_z1[chunk, 0].astype(F32)
        return gone

    def third_step(chunk, gone):
        gone.wait_recv()
        sums_ref[chunk] += got_z2[chunk].astype(F32)

    mixed_own.wait()
    core_own.wait_recv()
    y_own.wait_recv()
    lines = 64
    count = small_in_ref.shape[0]
    small_ref[:count, :] = small_in_ref[...]
    small_ref[count:, :] = jnp.zeros((2, width), F32)

    def finish(j, carry):
        at = span(j * lines, lines)
        grad = part_ref[at, :] + got_core_ref[1, at, :].astype(F32) + got_y_ref[at, :].astype(F32)
        hat, inverse = norm_parts(tokens_ref[at, :].astype(F32))
        back, gain_grad, bias_grad = norm_backward(grad, hat, inverse, gain1_ref[...])
        tg_own_ref[at, :] = (gx2_ref[at, :] + back).astype(BF16)
        small_ref[count : count + 1, :] += gain_grad[None, :]
        small_ref[count + 1 : count + 2, :] += bias_grad[None, :]
        return carry

    lax.fori_loop(0, share // lines, finish, 0)
    tg_y = send(tg_own_ref, tg_ref.at[t], y_side)
    tg_core = send(tg_own_ref, tg_ref.at[t], core)
    tg_own = pltpu.make_async_copy(tg_own_ref, tg_ref.at[t], local_sems.at[2])
    tg_own.start()

    def small_step(step, devices):
        small_send[step] = small_ref[...]
        exchanged = [
            send(small_send.at[step], got_small.at[step + d], device)
            for d, device in enumerate(devices)
        ]
        for d, copy in enumerate(exchanged):
            copy.wait_recv()
            small_ref[...] += got_small[step + d]

    small_step(0, [core])
    pairs = {0: first_step(0)}
    gone = {0: second_step(0, pairs[0])}
    tg_y.wait_recv()
    tg_y_core = send(tg_ref.at[t ^ 2], tg_ref.at[t ^ 2], core)
    small_step(1, [y_side])
    for chunk in (1, 2, 3):
        pairs[chunk] = first_step(chunk)
        third_step(chunk - 1, gone[chunk - 1])
        if chunk == 3:
            small_step(4, twins)
        gone[chunk] = second_step(chunk, pairs[chunk])
    small_step(2, [near])
    third_step(3, gone[3])
    small_step(3, [far])
    for copy in (core_own, mixed_core, mixed_y_core, tg_core, tg_y_core, down_far, up_far, *twin_copies):
        if copy is not core_own:
            copy.wait_recv()
    tg_own.wait()
    for copy in begun:
        if copy is not ga_y and copy is not ga_y_core:
            copy.wait_send()


def back_call(
    queries, keys, values, heads, logs, first, keep, tables_, w_out, w3, gain1, tokens,
    grad_middle, small, grad_own, mixed_own, normed1, *level_grads,
):
    rows, own = queries.shape
    share, width = grad_own.shape
    copies, owners = lax.axis_size("dp"), lax.axis_size("bucket")
    splits = rows // share
    reach = width // copies
    part = reach // owners
    half = level_grads[0].shape[1]
    inside = pl.BlockSpec(memory_space=pltpu.VMEM)
    outside = pl.BlockSpec(memory_space=pl.ANY)
    shape = jax.ShapeDtypeStruct
    dma = lambda *count: pltpu.SemaphoreType.DMA(count)
    vmem = lambda dtype, *size: pltpu.VMEM(size, dtype)
    others = copies - 1
    totals = (small.shape[0] + 2, width)
    few = 256
    sends = 30 + 7 * others
    return pl.pallas_call(
        functools.partial(back_kernel, copies),
        in_specs=[inside] * 9 + [outside] * 15,
        out_specs=[inside] * 2 + [outside] * 7,
        out_shape=[
            shape((4, part, own), F32),
            shape(totals, F32),
            shape((splits, share, width), BF16),
            shape((splits, share, width), BF16),
            *[shape((reach, half), BF16)] * 2,
            *[shape((others, reach, half), BF16)] * 2,
            shape((others, 4, reach, own), BF16),
        ],
        scratch_shapes=[
            vmem(BF16, rows, own),
            vmem(BF16, rows, own),
            vmem(BF16, rows, own),
            vmem(BF16, rows, own),
            vmem(BF16, *w3.shape),
            vmem(BF16, share, width),
            vmem(BF16, splits, share, width),
            vmem(BF16, rows, own),
            vmem(BF16, rows, 3 * own),
            vmem(F32, rows, HEAD_DIM),
            vmem(F32, rows, HEAD_DIM),
            vmem(BF16, 2, share, width),
            vmem(BF16, share, width),
            vmem(F32, share, width),
            vmem(BF16, share, width),
            vmem(BF16, 2, rows, 256),
            vmem(BF16, 2, 3, 256, own),
            vmem(BF16, 2, few, half),
            vmem(BF16, 2, others, few, half),
            vmem(BF16, 2, reach, half),
            vmem(BF16, 4, reach, own),
            vmem(BF16, others, 4, reach, own),
            vmem(BF16, 4, 2, part, own),
            vmem(F32, 4, part, own),
            vmem(BF16, 4, 2, part, own),
            vmem(BF16, 4, part, own),
            vmem(F32, 4 + others, *totals),
            vmem(F32, 5, *totals),
            dma(sends),
            dma(sends),
            dma(4),
            dma(2),
            dma(2),
            dma(copies, 2),
            dma(6),
        ],
        compiler_params=pltpu.CompilerParams(
            vmem_limit_bytes=62 << 20, collective_id=2, has_side_effects=True
        ),
        cost_estimate=pl.CostEstimate(
            flops=16 * rows * width * own + 10 * rows * rows * own,
            bytes_accessed=80 << 20,
            transcendentals=rows * rows * own // HEAD_DIM,
        ),
        name="back",
    )(
        logs, first, keep, *tables_, w_out, gain1, grad_middle, small,
        tokens.reshape(splits, share, width), queries, keys, values, heads, w3, grad_own, mixed_own, normed1, *level_grads,
    )


def finish_kernel(tg_ref, mixed_ref, tg_out, mixed_out):
    tg_out[...] = tg_ref[...].astype(F32)
    mixed_out[...] = mixed_ref[...]


def finish_call(tokens_grad, mixed):
    rows, width = mixed.shape
    block = pl.BlockSpec((rows // 8, width), lambda i: (i, 0))
    return pl.pallas_call(
        finish_kernel,
        grid=(8,),
        in_specs=[block] * 2,
        out_specs=[block] * 2,
        out_shape=[
            jax.ShapeDtypeStruct((rows, width), F32),
            jax.ShapeDtypeStruct((rows, width), BF16),
        ],
        compiler_params=pltpu.CompilerParams(vmem_limit_bytes=24 << 20),
        cost_estimate=pl.CostEstimate(flops=0, bytes_accessed=10 * rows * width, transcendentals=0),
        name="finish",
    )(tokens_grad, mixed)


def local(
    tokens,
    cotangent,
    lengths,
    head_quarters,
    buckets,
    ln1_gain,
    ln1_bias,
    w_qkv,
    w_out,
    ln2_gain,
    ln2_bias,
    w_router,
    w_up,
    w_down,
):
    tok_rows, model_width = tokens.shape
    owners = lax.axis_size("bucket")
    splits = lax.axis_size("tensor")
    copies = lax.axis_size("dp")
    share = tok_rows // splits
    t, z, x = lax.axis_index("tensor"), lax.axis_index("bucket"), lax.axis_index("dp")
    up_own = w_up.reshape(model_width, -1)
    down_own = w_down.reshape(-1, model_width)
    hidden_width = up_own.shape[1]

    levels = buckets[:, 0].astype(F32).reshape(-1, HEAD_DIM)

    first = layout(lengths[0], tok_rows)[:, None]
    keep = (t < head_quarters).astype(F32)[:, None]
    w3 = jnp.transpose(w_qkv, (1, 0, 2))
    (
        logs,
        middle,
        cosine,
        sine,
        normed1,
        queries,
        keys,
        values,
        heads_low,
        n2,
        up_other,
        down_other,
        near_cotangent,
        near_levels,
    ) = front_call(
        tokens,
        (ln1_gain.reshape(1, -1), ln1_bias.reshape(1, -1)),
        w3,
        first,
        keep,
        w_out,
        (ln2_gain.reshape(1, -1), ln2_bias.reshape(1, -1)),
        up_own,
        down_own,
        cotangent.reshape(splits, share, model_width),
        levels,
    )
    level_all = jnp.concatenate([levels.reshape(-1), near_levels.reshape(-1)], 0)[:, None]
    (
        mixed_own,
        grad_middle,
        grad_attention_own,
        small,
        _,
        _,
        down_own,
        down_other,
        up_own,
        up_other,
        got_down,
        got_up,
    ) = middle_call(
        n2,
        cotangent,
        near_cotangent,
        (up_own, up_other),
        (down_own, down_other),
        w_router,
        level_all,
        middle,
        (ln2_gain.reshape(1, -1), ln2_bias.reshape(1, -1)),
    )
    sums, small, mixed, tokens_grad, down_far, up_far, down_twin, up_twin, _ = back_call(
        queries,
        keys,
        values,
        heads_low,
        logs,
        first,
        keep,
        (cosine, sine),
        w_out,
        w3,
        ln1_gain.reshape(1, -1),
        tokens,
        grad_middle,
        small,
        grad_attention_own,
        mixed_own,
        normed1,
        down_other,
        got_down,
        up_other,
        got_up,
        down_own,
        up_own,
    )
    size = model_width // copies

    def level_grad(own, twin, distant):
        mine = lax.dynamic_slice_in_dim(own, x * size, size, 0).astype(F32)
        return mine + jnp.sum(twin.astype(F32), 0) + distant.astype(F32)

    grad_down = level_grad(down_own, down_twin, down_far).T
    grad_up = level_grad(up_own, up_twin, up_far)
    tokens_grad, mixed = finish_call(
        tokens_grad.reshape(tok_rows, model_width), mixed.reshape(tok_rows, model_width)
    )
    width = model_width // (copies * owners)
    small = lax.dynamic_slice_in_dim(small, (x * owners + z) * width, width, 1)
    return (
        mixed,
        tokens_grad,
        small[2 + owners],
        small[3 + owners],
        jnp.transpose(sums[1:], (1, 0, 2)),
        sums[0].T,
        small[0],
        small[1],
        small[2 : 2 + owners].T,
        grad_up.reshape(-1, 1, hidden_width),
        grad_down.reshape(1, hidden_width, -1),
    )


def solution(mesh):
    placed = (
        P(("dp", "bucket"), None),
        P(("dp", "bucket"), None),
        P(("dp", "bucket"), None),
        P(("dp", "bucket")),
        P(("dp", "bucket"), None),
        P(),
        P(),
        P(None, None, "tensor"),
        P("tensor", None),
        P(),
        P(),
        P(),
        P(None, "bucket", "tensor"),
        P("bucket", "tensor", None),
    )
    return jax.shard_map(
        local,
        mesh=mesh,
        in_specs=placed,
        out_specs=(
            P(("dp", "bucket"), None),
            P(("dp", "bucket"), None),
            P(("dp", "bucket")),
            P(("dp", "bucket")),
            P(("dp", "bucket"), None, "tensor"),
            P("tensor", ("dp", "bucket")),
            P(("dp", "bucket")),
            P(("dp", "bucket")),
            P(("dp", "bucket"), None),
            P("dp", "bucket", "tensor"),
            P("bucket", "tensor", "dp"),
        ),
        check_vma=False,
    )
```

```python
import functools
import math

import jax
import jax.numpy as jnp
from jax import lax
from jax.experimental import pallas as pl
from jax.experimental.pallas import tpu as pltpu
from jax.sharding import PartitionSpec as P

HEAD_DIM = 128
QBLOCK = 256
EPS = 1e-05
HIGH = lax.Precision.HIGHEST
NEGATIVE = -1e30
F32 = jnp.float32
BF16 = jnp.bfloat16


def norm_parts(values):
    centred = values - jnp.mean(values, -1, keepdims=True)
    inverse = lax.rsqrt(jnp.mean(centred * centred, -1, keepdims=True) + EPS)
    return centred * inverse, inverse


def norm_backward(grad_in, normed, inverse, gain):
    scaled = grad_in * gain
    inner = (
        scaled
        - jnp.mean(scaled, -1, keepdims=True)
        - normed * jnp.mean(scaled * normed, -1, keepdims=True)
    )
    return inverse * inner, jnp.sum(grad_in * normed, 0), jnp.sum(grad_in, 0)


def layout(lengths_row, tok_rows):
    ends = jnp.cumsum(lengths_row)
    starts = ends - lengths_row
    tok_index = jnp.arange(tok_rows, dtype=jnp.int32)
    segments = jnp.sum((tok_index[:, None] >= ends[None, :]).astype(jnp.int32), 1)
    chosen = segments[:, None] == jnp.arange(lengths_row.shape[0], dtype=jnp.int32)[None, :]
    return jnp.sum(jnp.where(chosen, starts[None, :], 0), 1)


def dot(left, right, dims):
    return lax.dot_general(left, right, (dims, ((), ())), preferred_element_type=F32)


NN = ((1,), (0,))
NT = ((1,), (1,))
TN = ((0,), (0,))


def masked_scores(query, keys, first, block, length):
    scores = dot(query, keys, NT) * HEAD_DIM**-0.5
    key_at = lax.broadcasted_iota(jnp.int32, (QBLOCK, length), 1)
    row_at = lax.broadcasted_iota(jnp.int32, (QBLOCK, length), 0) + block * QBLOCK
    allowed = (key_at >= first) & (key_at <= row_at)
    return jnp.where(allowed, scores, NEGATIVE)


class Copies:
    def __init__(self, send_sems, recv_sems):
        self.send_sems, self.recv_sems, self.used = send_sems, recv_sems, 0

    def make(self, source, target, device):
        slot = self.used
        self.used += 1
        return pltpu.make_async_remote_copy(
            src_ref=source,
            dst_ref=target,
            send_sem=self.send_sems.at[slot],
            recv_sem=self.recv_sems.at[slot],
            device_id=device,
            device_id_type=pl.DeviceIdType.MESH,
        )

    def start(self, source, target, device):
        copy = self.make(source, target, device)
        copy.start()
        return copy


def meet(devices):
    barrier = pltpu.get_barrier_semaphore()
    for device in devices:
        pl.semaphore_signal(barrier, inc=1, device_id=device, device_id_type=pl.DeviceIdType.MESH)
    pl.semaphore_wait(barrier, len(devices))


def front_kernel(
    copies,
    gain1_ref,
    bias1_ref,
    first_ref,
    keep_ref,
    gain2_ref,
    bias2_ref,
    tokens_in,
    w_in,
    w_out_in,
    up_ref,
    down_ref,
    cot_ref,
    level_ref,
    log_ref,
    middle_ref,
    cos_ref,
    sin_ref,
    n1_out,
    q_out,
    k_out,
    v_out,
    heads_out,
    n2_ref,
    up_other_ref,
    down_other_ref,
    near_cot_ref,
    near_level_ref,
    tokens_ref,
    w_ref,
    w_out_ref,
    n1_ref,
    q_ref,
    k_ref,
    v_ref,
    heads_ref,
    away_ref,
    got_core_ref,
    pass_ref,
    got_y_ref,
    own_ref,
    send_sems,
    recv_sems,
    in_sems,
    out_sems,
):
    t, z, x = lax.axis_index("tensor"), lax.axis_index("bucket"), lax.axis_index("dp")
    rows, own = q_ref.shape
    share = own_ref.shape[0]
    heads = own // HEAD_DIM
    blocks = rows // QBLOCK
    core, y_side = {"tensor": t ^ 1}, {"tensor": t ^ 2}
    near, far = {"bucket": z ^ 1}, {"bucket": z ^ 2}
    twins = [{"dp": lax.rem(x + d, copies)} for d in range(1, copies)]

    def token_block(i):
        at = pl.ds(pl.multiple_of(i * QBLOCK, QBLOCK), QBLOCK)
        return pltpu.make_async_copy(tokens_in.at[at], tokens_ref.at[at], in_sems.at[i])

    w_copies = [
        pltpu.make_async_copy(w_in.at[part], w_ref.at[part], in_sems.at[blocks + part])
        for part in range(3)
    ]
    w_out_copy = pltpu.make_async_copy(w_out_in, w_out_ref, in_sems.at[blocks + 3])
    token_block(0).start()
    for copy in w_copies:
        copy.start()
    for i in range(1, blocks):
        token_block(i).start()
    w_out_copy.start()

    meet([core, y_side, near, far] + twins)
    links = Copies(send_sems, recv_sems)
    begun = []

    def send(source, target, device):
        copy = links.start(source, target, device)
        begun.append(copy)
        return copy

    def piece(ref, quarter):
        size = ref.shape[0] // copies // 4
        return ref.at[pl.ds(pl.multiple_of((x * 4 + quarter) * size, 16), size)]

    def fetch(ref, other_ref, quarter):
        copy = links.make(piece(ref, quarter), piece(other_ref, quarter), far)
        begun.append(copy)
        return copy

    outer = lax.rem(z, 2) == z // 2
    pieces = [fetch(up_ref, up_other_ref, quarter) for quarter in range(4)]
    pieces += [fetch(down_ref, down_other_ref, quarter) for quarter in range(4)]
    parity = lax.rem(t, 2)
    cots = [
        links.make(cot_ref.at[parity + i], near_cot_ref.at[parity + i], near) for i in (0, 2)
    ]
    begun.extend(cots)
    to_twins = [
        [links.make(ref, ref, device) for device in twins]
        for ref in [piece(up_other_ref, quarter) for quarter in range(4)]
        + [piece(down_other_ref, quarter) for quarter in range(4)]
    ]
    to_core_cots = [
        links.make(near_cot_ref.at[parity + i], near_cot_ref.at[parity + i], core) for i in (0, 2)
    ]

    def begin(copies_):
        for copy in copies_:
            copy.start()

    def pass_weights(indices):
        for index in indices:
            pieces[index].wait_recv()
            begin(to_twins[index])

    def pass_cots():
        for copy, onward_copy in zip(cots, to_core_cots):
            copy.wait_recv()
            onward_copy.start()

    @pl.when(outer)
    def _():
        begin(pieces)

    @pl.when(jnp.logical_not(outer))
    def _():
        begin(cots)

    near_level = send(level_ref, near_level_ref, near)

    half = HEAD_DIM // 2
    lane = lax.broadcasted_iota(jnp.int32, (1, HEAD_DIM), 1)
    freq = jnp.exp((lane % half).astype(F32) * (-math.log(10000.0) / half))
    side = jnp.where(lane < half, -1.0, 1.0)

    def project(i, carry):
        at = pl.ds(pl.multiple_of(i * QBLOCK, QBLOCK), QBLOCK)
        token_block(i).wait()
        normed, _ = norm_parts(tokens_ref[at, :].astype(F32))
        low = (normed * gain1_ref[...] + bias1_ref[...]).astype(BF16)
        n1_ref[at, :] = low
        token = lax.broadcasted_iota(jnp.int32, (QBLOCK, 1), 0) + i * QBLOCK
        angle = (token - first_ref[at, :]).astype(F32) * freq
        cosine, sine = jnp.cos(angle), jnp.sin(angle) * side
        cos_ref[at, :] = cosine
        sin_ref[at, :] = sine
        for part, out_ref in enumerate((q_ref, k_ref, v_ref)):

            @pl.when(i == 0)
            def _():
                w_copies[part].wait()

            projected = dot(low, w_ref[part], NN)
            if part == 2:
                out_ref[at, :] = projected.astype(BF16)
                continue
            for start in range(0, own, HEAD_DIM):
                head = projected[:, start : start + HEAD_DIM]
                turned = head * cosine + pltpu.roll(head, half, 1) * sine
                out_ref[at, start : start + HEAD_DIM] = turned.astype(BF16)
        return carry

    lax.fori_loop(0, blocks, project, 0)
    outs = [
        pltpu.make_async_copy(ref, out, out_sems.at[i])
        for i, (ref, out) in enumerate(
            ((n1_ref, n1_out), (q_ref, q_out), (k_ref, k_out), (v_ref, v_out), (heads_ref, heads_out))
        )
    ]
    for copy in outs[:4]:
        copy.start()

    for head in range(heads):
        lanes = slice(head * HEAD_DIM, (head + 1) * HEAD_DIM)
        for block in range(rows // QBLOCK):
            length = (block + 1) * QBLOCK
            at = slice(block * QBLOCK, length)
            scores = masked_scores(
                q_ref[at, lanes], k_ref[:length, lanes], first_ref[at], block, length
            )
            most = jnp.max(scores, -1, keepdims=True)
            expo = jnp.exp(scores - most)
            total = jnp.sum(expo, -1, keepdims=True)
            weights = (expo * (1.0 / total)).astype(BF16)
            out = dot(weights, v_ref[:length, lanes], NN)
            heads_ref[at, lanes] = (out * keep_ref[at]).astype(BF16)
            log_ref[at, head : head + 1] = most + jnp.log(total)

    outs[4].start()
    w_out_copy.wait()

    def attended(index):
        at = pl.ds(pl.multiple_of(index * share, share), share)
        return dot(heads_ref[at, :], w_out_ref[...], NN)

    away_ref[1] = attended(t ^ 3).astype(BF16)
    to_core1 = send(away_ref.at[1], got_core_ref.at[1], core)
    away_ref[0] = attended(t ^ 1).astype(BF16)
    to_core0 = send(away_ref.at[0], got_core_ref.at[0], core)
    passed = attended(t ^ 2)
    to_core1.wait_recv()
    pass_ref[...] = (passed + got_core_ref[1].astype(F32)).astype(BF16)
    to_y = send(pass_ref, got_y_ref, y_side)
    middle = attended(t)
    middle += tokens_ref[pl.ds(pl.multiple_of(t * share, share), share), :].astype(F32)
    to_core0.wait_recv()
    middle_ref[...] = middle + got_core_ref[0].astype(F32)

    @pl.when(jnp.logical_not(outer))
    def _():
        pass_weights(range(8))
        begin(pieces)

    @pl.when(outer)
    def _():
        begin(cots)
        pass_cots()

    to_y.wait_recv()
    total = middle_ref[...] + got_y_ref[...].astype(F32)
    middle_ref[...] = total
    normed, _ = norm_parts(total)
    own_ref[...] = (normed * gain2_ref[...] + bias2_ref[...]).astype(BF16)
    own_y = send(own_ref, n2_ref.at[t], y_side)
    own_core = send(own_ref, n2_ref.at[t], core)
    keep_own = pltpu.make_async_copy(own_ref, n2_ref.at[t], in_sems.at[0])
    keep_own.start()

    @pl.when(outer)
    def _():
        pass_weights(range(4))

    own_y.wait_recv()
    y_core = send(n2_ref.at[t ^ 2], n2_ref.at[t ^ 2], core)

    @pl.when(outer)
    def _():
        pass_weights(range(4, 8))

    @pl.when(jnp.logical_not(outer))
    def _():
        pass_cots()

    keep_own.wait()
    for copy in outs:
        copy.wait()
    for copy in (near_level, own_core, y_core, *to_core_cots, *sum(to_twins, [])):
        copy.wait_recv()
    for copy in (*begun, *to_core_cots, *sum(to_twins, [])):
        copy.wait_send()


def front_call(tokens, ln1, w3, first, keep, w_out, ln2, up, down, cotangent, levels):
    rows, width = tokens.shape
    own = w3.shape[2]
    splits, copies = lax.axis_size("tensor"), lax.axis_size("dp")
    share = rows // splits
    inside = pl.BlockSpec(memory_space=pltpu.VMEM)
    outside = pl.BlockSpec(memory_space=pl.ANY)
    shape = jax.ShapeDtypeStruct
    vmem = lambda dtype, *size: pltpu.VMEM(size, dtype)
    total = 19 + 8 * (copies - 1)
    narrow = shape((rows, own), BF16)
    return pl.pallas_call(
        functools.partial(front_kernel, copies),
        in_specs=[inside] * 6 + [outside] * 7,
        out_specs=[inside] * 4 + [outside] * 10,
        out_shape=[
            shape((rows, own // HEAD_DIM), F32),
            shape((share, width), F32),
            shape((rows, HEAD_DIM), F32),
            shape((rows, HEAD_DIM), F32),
            shape((rows, width), BF16),
            narrow,
            narrow,
            narrow,
            narrow,
            shape((splits, share, width), BF16),
            shape(up.shape, BF16),
            shape(down.shape, BF16),
            shape((splits, share, width), BF16),
            shape(levels.shape, F32),
        ],
        scratch_shapes=[
            vmem(BF16, rows, width),
            vmem(BF16, *w3.shape),
            vmem(BF16, *w_out.shape),
            vmem(BF16, rows, width),
            vmem(BF16, rows, own),
            vmem(BF16, rows, own),
            vmem(BF16, rows, own),
            vmem(BF16, rows, own),
            vmem(BF16, 2, share, width),
            vmem(BF16, 2, share, width),
            vmem(BF16, share, width),
            vmem(BF16, share, width),
            vmem(BF16, share, width),
            pltpu.SemaphoreType.DMA((total,)),
            pltpu.SemaphoreType.DMA((total,)),
            pltpu.SemaphoreType.DMA((rows // QBLOCK + 4,)),
            pltpu.SemaphoreType.DMA((5,)),
        ],
        compiler_params=pltpu.CompilerParams(
            vmem_limit_bytes=56 << 20, collective_id=0, has_side_effects=True
        ),
        cost_estimate=pl.CostEstimate(
            flops=8 * rows * width * own + 4 * rows * rows * own,
            bytes_accessed=60 << 20,
            transcendentals=rows * rows * own // HEAD_DIM,
        ),
        name="front",
    )(*ln1, first, keep, *ln2, tokens, w3, w_out, up, down, cotangent, levels)


def block_at(i, t):
    near, j = i // 4, i % 4
    own_bit = (1 - j // 2) * (3 - 2 * j) + (j // 2) * (6 - 2 * j)
    bit = (1 - near) * own_bit + near * (j + 1 - 2 * (j % 2))
    return near, t ^ bit


def router_gate(rows, w_router_ref, level):
    logits = dot(rows, w_router_ref[...], NN)
    expo = jnp.exp(logits - jnp.max(logits, -1, keepdims=True))
    probs = expo / jnp.sum(expo, -1, keepdims=True)
    number = lax.broadcasted_iota(jnp.int32, probs.shape, 1).astype(F32)
    onehot = (number == level).astype(F32)
    return jnp.sum(probs * onehot, -1, keepdims=True), probs, onehot


def middle_kernel(
    copies,
    n2_ref,
    cot_ref,
    near_cot_ref,
    up_own_ref,
    up_other_ref,
    down_own_ref,
    down_other_ref,
    router_ref,
    level_ref,
    gain2_ref,
    bias2_ref,
    x2_in,
    mixed_ref,
    gx2_ref,
    ga_ref,
    small_ref,
    near_n2_ref,
    gf_ref,
    down_own_grad,
    down_other_grad,
    up_own_grad,
    up_other_grad,
    got_down_ref,
    got_up_ref,
    n2_in,
    cot_in,
    gf_out,
    hid_ref,
    gu_ref,
    part_f,
    part_g,
    hold_f,
    send_ref,
    core_f,
    core_g,
    got_fz,
    got_fy,
    got_gy,
    got_gz,
    tile_in,
    tile_out,
    core_send_sems,
    core_recv_sems,
    send_sems,
    recv_sems,
    in_sems,
    out_sems,
    tile_sems,
    tile_out_sems,
    x2_sem,
):
    t, z, x = lax.axis_index("tensor"), lax.axis_index("bucket"), lax.axis_index("dp")
    share, width = gx2_ref.shape
    half = up_own_ref.shape[1]
    core, y_side, near = {"tensor": t ^ 1}, {"tensor": t ^ 2}, {"bucket": z ^ 1}
    twins = [{"dp": lax.rem(x + d, copies)} for d in range(1, copies)]
    splits = n2_ref.shape[0]

    def load(i, slot, act):
        at, s = block_at(i, t)
        for index, (rows_ref, grads_ref) in enumerate(
            ((n2_ref, cot_ref), (near_n2_ref, near_cot_ref))
        ):

            @pl.when(at == index)
            def _():
                act(pltpu.make_async_copy(rows_ref.at[s], n2_in.at[slot], in_sems.at[slot, 0]))
                act(pltpu.make_async_copy(grads_ref.at[s], cot_in.at[slot], in_sems.at[slot, 1]))

    def begin(copy):
        copy.start()

    def finish_load(copy):
        copy.wait()

    def store(i, slot):
        at, s = block_at(i, t)
        return pltpu.make_async_copy(gf_out.at[slot], gf_ref.at[at, s], out_sems.at[slot])

    def to_core(a):
        return [
            pltpu.make_async_remote_copy(
                src_ref=send_ref.at[kind * 2 + int(a == 1)],
                dst_ref=(core_f, core_g)[kind].at[a],
                send_sem=core_send_sems.at[kind, a],
                recv_sem=core_recv_sems.at[kind, a],
                device_id=core,
                device_id_type=pl.DeviceIdType.MESH,
            )
            for kind in (0, 1)
        ]

    load(0, 0, begin)
    meet([core, y_side, near] + twins)
    links = Copies(send_sems, recv_sems)
    few = share // 2
    late = pl.ds(few, few)
    early = pl.ds(0, few)
    to_near = [
        links.start(n2_ref.at[t, late], near_n2_ref.at[t, late], near),
        links.start(n2_ref.at[t, early], near_n2_ref.at[t, early], near),
        links.start(n2_ref.at[t ^ 2, early], near_n2_ref.at[t ^ 2, early], near),
    ]
    near_y = links.make(near_n2_ref.at[t, late], near_n2_ref.at[t, late], y_side)
    near_core = links.make(near_n2_ref.at[t], near_n2_ref.at[t], core)
    near_y_core = links.make(near_n2_ref.at[t ^ 2], near_n2_ref.at[t ^ 2], core)
    g_own_y = links.make(send_ref.at[4], got_gy.at[1], y_side)
    f_near = links.make(send_ref.at[1], got_fz.at[1], near)
    g_near_y = links.make(send_ref.at[0], got_gy.at[0], y_side)
    f_near_y = links.make(send_ref.at[2], got_fz.at[0], near)
    f_own_y = links.make(send_ref.at[3], got_fy, y_side)
    g_near = links.make(send_ref.at[4], got_gz, near)

    def work(i, carry):
        slot = i % 2
        at, s = block_at(i, t)
        load(i, slot, finish_load)

        @pl.when((i != 3) & (i != 5) & (i != 7))
        def _():
            load(i + 1, 1 - slot, begin)

        @pl.when(i >= 2)
        def _():
            store(i - 2, slot).wait()

        spot = pl.ds(pl.multiple_of((at * splits + s) * share, share), share)
        rows = n2_in[slot]
        level = level_ref[spot, :]
        gate, _, _ = router_gate(rows, router_ref, level)
        grad = (gate * cot_in[slot].astype(F32)).astype(BF16)
        gf_out[slot] = grad
        store(i, slot).start()
        for part, (up_ref, down_ref, unit_level) in enumerate(
            ((up_own_ref, down_own_ref, z), (up_other_ref, down_other_ref, z ^ 2))
        ):
            lanes = slice(part * half, (part + 1) * half)
            kept = level >= unit_level.astype(F32)
            act = jnp.where(kept, jnp.maximum(dot(rows, up_ref[...], NN), 0.0), 0.0)
            hid_ref[spot, lanes] = (act * act).astype(BF16)
            back = dot(grad, down_ref[...], NT)
            gu_ref[spot, lanes] = (back * 2.0 * act).astype(BF16)
        for lanes in (slice(0, width // 2), slice(width // 2, width)):
            part_f[:, lanes] = dot(hid_ref[spot, :half], down_own_ref[:, lanes], NN) + dot(
                hid_ref[spot, half:], down_other_ref[:, lanes], NN
            )
            part_g[:, lanes] = dot(gu_ref[spot, :half], up_own_ref[lanes, :], NT) + dot(
                gu_ref[spot, half:], up_other_ref[lanes, :], NT
            )

        def leave(a):
            for before in {2: (0,), 3: (2,)}.get(a, ()):
                for copy in to_core(before):
                    copy.wait_send()
            send_ref[int(a == 1)] = part_f[...].astype(BF16)
            send_ref[2 + int(a == 1)] = part_g[...].astype(BF16)
            for copy in to_core(a):
                copy.start()

        for a, index in enumerate((0, 1, 4, 6)):

            @pl.when(i == index)
            def _():
                leave(a)

        def with_core(kind, a):
            to_core(a)[kind].wait_recv()
            got = (core_f, core_g)[kind][a].astype(F32)
            return (part_f, part_g)[kind][...] + got

        @pl.when(i == 1)
        def _():
            to_near[0].wait_recv()
            near_y.start()

        @pl.when(i == 4)
        def _():
            to_near[2].wait_recv()
            near_y.wait_recv()
            near_y_core.start()

        @pl.when(i == 2)
        def _():
            send_ref[4] = with_core(1, 0).astype(BF16)
            g_own_y.start()
            hold_f[...] = with_core(0, 0)

        @pl.when(i == 3)
        def _():
            mixed_ref[...] = with_core(0, 1).astype(BF16)
            ga_ref[...] = with_core(1, 1).astype(BF16)
            to_near[1].wait_recv()
            near_core.start()
            near_core.wait_recv()
            load(i + 1, 1 - slot, begin)

        @pl.when(i == 5)
        def _():
            for copy in to_core(1):
                copy.wait_send()
            send_ref[1] = with_core(0, 2).astype(BF16)
            f_near.start()
            gx2_ref[...] = with_core(1, 2)
            near_y_core.wait_recv()
            load(i + 1, 1 - slot, begin)

        @pl.when(i == 7)
        def _():
            for copy in to_core(3):
                copy.wait_send()
            send_ref[0] = with_core(1, 3).astype(BF16)
            g_near_y.start()
            send_ref[2] = with_core(0, 3).astype(BF16)
            f_near_y.start()

        return carry

    lax.fori_loop(0, 8, work, 0)
    store(6, 0).wait()
    store(7, 1).wait()
    x2_ref = part_f
    x2_copy = pltpu.make_async_copy(x2_in, x2_ref, x2_sem)
    x2_copy.start()

    tile = tile_in.shape[-1]
    tiles = width // tile

    def weight_grads(sources, right_ref, results):
        def fetch(j, slot):
            lanes = pl.ds(pl.multiple_of(j * tile, tile), tile)
            return [
                pltpu.make_async_copy(
                    source.at[:, :, lanes], tile_in.at[slot, index], tile_sems.at[slot, index]
                )
                for index, source in enumerate(sources)
            ]

        def put(j, slot):
            rows = pl.ds(pl.multiple_of(j * tile, tile), tile)
            return [
                pltpu.make_async_copy(
                    tile_out.at[slot, index], result.at[rows, :], tile_out_sems.at[slot, index]
                )
                for index, result in enumerate(results)
            ]

        for copy in fetch(0, 0):
            copy.start()

        def step(j, carry):
            slot = j % 2
            for copy in fetch(j, slot):
                copy.wait()

            @pl.when(j < tiles - 1)
            def _():
                for copy in fetch(j + 1, 1 - slot):
                    copy.start()

            @pl.when(j >= 2)
            def _():
                for copy in put(j - 2, slot):
                    copy.wait()

            left = tile_in[slot].reshape(-1, tile)
            total = dot(left, right_ref[...], TN).astype(BF16)
            for index in (0, 1):
                tile_out[slot, index] = total[:, index * half : (index + 1) * half]
            for copy in put(j, slot):
                copy.start()
            return carry

        lax.fori_loop(0, tiles, step, 0)
        for j in (tiles - 2, tiles - 1):
            for copy in put(j, j % 2):
                copy.wait()

    size = width // copies

    def to_twins(grad_ref, got_ref):
        return [
            links.start(
                grad_ref.at[pl.ds(pl.multiple_of(lax.rem(x + d, copies) * size, size), size), :],
                got_ref.at[d - 1],
                twins[d - 1],
            )
            for d in range(1, copies)
        ]

    weight_grads((gf_ref.at[0], gf_ref.at[1]), hid_ref, (down_own_grad, down_other_grad))
    crossing = to_twins(down_other_grad, got_down_ref)

    weight_grads((n2_ref, near_n2_ref), gu_ref, (up_own_grad, up_other_grad))
    crossing += to_twins(up_other_grad, got_up_ref)

    f_near_y.wait_recv()
    send_ref[3] = (hold_f[...] + got_fz[0].astype(F32)).astype(BF16)
    f_own_y.start()
    g_near_y.wait_recv()
    g_own_y.wait_send()
    send_ref[4] = (gx2_ref[...] + got_gy[0].astype(F32)).astype(BF16)
    g_near.start()

    own = pltpu.make_async_copy(n2_ref.at[t], n2_in.at[0], in_sems.at[0, 0])
    own.start()
    own_cot = pltpu.make_async_copy(cot_ref.at[t], cot_in.at[0], in_sems.at[0, 1])
    own_cot.start()
    own.wait()
    own_cot.wait()
    for copy in (f_near, f_own_y, g_own_y, g_near):
        copy.wait_recv()
    x2_copy.wait()
    small_ref[...] = jnp.zeros_like(small_ref)
    few = 64

    def finish(j, carry):
        at = pl.ds(pl.multiple_of(j * few, few), few)
        level = level_ref[pl.ds(pl.multiple_of(t * share + j * few, few), few), :]
        rows = n2_in[0, at, :]
        gate, probs, onehot = router_gate(rows, router_ref, level)
        branch = mixed_ref[at, :].astype(F32) + got_fz[1, at, :].astype(F32) + got_fy[at, :].astype(F32)
        branch = branch.astype(BF16).astype(F32)
        x2 = x2_ref[at, :]
        mixed_ref[at, :] = (x2 + gate * branch).astype(BF16)
        grad_out = cot_in[0, at, :].astype(F32)
        grad_gate = jnp.sum(grad_out * branch, -1, keepdims=True)
        grad_logits = grad_gate * gate * (onehot - probs)
        returned = ga_ref[at, :].astype(F32) + got_gy[1, at, :].astype(F32) + got_gz[at, :].astype(F32)
        grad_n2 = returned.astype(BF16).astype(F32)
        grad_n2 += lax.dot_general(
            grad_logits,
            router_ref[...].astype(F32),
            (NT, ((), ())),
            precision=HIGH,
            preferred_element_type=F32,
        )
        hat, inverse = norm_parts(x2)
        back, gain_grad, bias_grad = norm_backward(grad_n2, hat, inverse, gain2_ref[...])
        gx2 = grad_out + back
        gx2_ref[at, :] = gx2
        ga_ref[at, :] = gx2.astype(BF16)
        small_ref[0:1, :] += gain_grad[None, :]
        small_ref[1:2, :] += bias_grad[None, :]
        small_ref[2 : 2 + probs.shape[1], :] += lax.dot_general(
            grad_logits, rows.astype(F32), (TN, ((), ())), precision=HIGH, preferred_element_type=F32
        )
        return carry

    lax.fori_loop(0, share // few, finish, 0)
    for copy in crossing:
        copy.wait_recv()
    for copy in (
        *to_near, near_y, near_core, near_y_core, f_near,
        g_near_y, f_near_y, f_own_y, g_near, *crossing,
    ):
        copy.wait_send()


def middle_call(n2, cotangent, near_cotangent, ups, downs, w_router, levels, middle, ln2):
    splits, share, width = n2.shape
    copies = lax.axis_size("dp")
    half = ups[0].shape[1]
    rows = 2 * splits * share
    inside = pl.BlockSpec(memory_space=pltpu.VMEM)
    outside = pl.BlockSpec(memory_space=pl.ANY)
    shape = jax.ShapeDtypeStruct
    block = lambda count, dtype=BF16: pltpu.VMEM((*count, share, width), dtype)
    dma = lambda *count: pltpu.SemaphoreType.DMA(count)
    return pl.pallas_call(
        functools.partial(middle_kernel, copies),
        in_specs=[outside] * 3 + [inside] * 8 + [outside],
        out_specs=[inside] * 4 + [outside] * 8,
        out_shape=[
            shape((share, width), BF16),
            shape((share, width), F32),
            shape((share, width), BF16),
            shape((2 + w_router.shape[1], width), F32),
            shape(n2.shape, BF16),
            shape((2, *n2.shape), BF16),
            *[shape((width, half), BF16)] * 4,
            *[shape((copies - 1, width // copies, half), BF16)] * 2,
        ],
        scratch_shapes=[
            block((2,)),
            block((2,)),
            block((2,)),
            pltpu.VMEM((rows, 2 * half), BF16),
            pltpu.VMEM((rows, 2 * half), BF16),
            block((), F32),
            block((), F32),
            block((), F32),
            block((5,)),
            block((4,)),
            block((4,)),
            block((2,)),
            block(()),
            block((2,)),
            block(()),
            pltpu.VMEM((2, 2, splits, share, 256), BF16),
            pltpu.VMEM((2, 2, 256, half), BF16),
            dma(2, 4),
            dma(2, 4),
            dma(12 + 2 * (copies - 1)),
            dma(12 + 2 * (copies - 1)),
            dma(2, 2),
            dma(2),
            dma(2, 2),
            dma(2, 2),
            pltpu.SemaphoreType.DMA,
        ],
        compiler_params=pltpu.CompilerParams(
            vmem_limit_bytes=62 << 20, collective_id=1, has_side_effects=True
        ),
        cost_estimate=pl.CostEstimate(
            flops=12 * rows * width * 2 * half, bytes_accessed=80 << 20, transcendentals=0
        ),
        name="middle",
    )(n2, cotangent.reshape(splits, share, width), near_cotangent, *ups, *downs, w_router, levels, *ln2, middle)


def back_kernel(
    copies,
    log_ref,
    first_ref,
    keep_ref,
    cos_ref,
    sin_ref,
    w_out_ref,
    gain1_ref,
    gx2_ref,
    small_in_ref,
    tokens_in,
    q_in,
    k_in,
    v_in,
    heads_in,
    w_in,
    ga_in_ref,
    mixed_in_ref,
    n1_ref,
    down_ref,
    got_down_ref,
    up_ref,
    got_up_ref,
    down_own_ref,
    up_own_ref,
    sums_ref,
    small_ref,
    mixed_ref,
    tg_ref,
    down_far_ref,
    up_far_ref,
    down_twin_ref,
    up_twin_ref,
    leave_ref,
    q_ref,
    k_ref,
    v_ref,
    heads_ref,
    w_ref,
    tokens_ref,
    ga_ref,
    go_ref,
    gp_ref,
    dk_ref,
    dv_ref,
    got_core_ref,
    got_y_ref,
    part_ref,
    tg_own_ref,
    tile_in,
    tile_out,
    fold_a,
    fold_b,
    fold_send,
    kept_ref,
    got_x_ref,
    z_send,
    z_kept,
    got_z1,
    got_z2,
    got_small,
    small_send,
    send_sems,
    recv_sems,
    local_sems,
    tile_sems,
    tile_out_sems,
    fold_sems,
    in_sems,
):
    t, z, x = lax.axis_index("tensor"), lax.axis_index("bucket"), lax.axis_index("dp")
    rows, own = q_ref.shape
    splits, share, width = ga_ref.shape
    heads, blocks = own // HEAD_DIM, rows // QBLOCK
    reach = width // copies
    part = got_z2.shape[1]
    core, y_side = {"tensor": t ^ 1}, {"tensor": t ^ 2}
    near, far = {"bucket": z ^ 1}, {"bucket": z ^ 2}
    twins = [{"dp": lax.rem(x + d, copies)} for d in range(1, copies)]
    meet([core, y_side, near, far] + twins)
    links = Copies(send_sems, recv_sems)
    begun = []

    def send(source, target, device):
        copy = links.start(source, target, device)
        begun.append(copy)
        return copy

    def span(start, size):
        return pl.ds(pl.multiple_of(start, size), size)

    ga_y = send(ga_in_ref, ga_ref.at[t], y_side)
    ga_core = send(ga_in_ref, ga_ref.at[t], core)
    ga_own = pltpu.make_async_copy(ga_in_ref, ga_ref.at[t], local_sems.at[0])
    ga_own.start()

    def to_twins(source_ref, target_ref):
        for d in range(1, copies):
            rows_there = span(lax.rem(x + d, copies) * reach, reach)
            twin_copies.append(send(source_ref.at[rows_there], target_ref.at[d - 1], twins[d - 1]))

    twin_copies = []
    to_twins(up_own_ref, up_twin_ref)
    mixed_y = send(mixed_in_ref, mixed_ref.at[t], y_side)
    mixed_core = send(mixed_in_ref, mixed_ref.at[t], core)
    mixed_take = pltpu.make_async_copy(mixed_in_ref, tg_own_ref, local_sems.at[1])
    mixed_take.start()
    mixed_own = pltpu.make_async_copy(tg_own_ref, mixed_ref.at[t], local_sems.at[3])

    loaded = [
        pltpu.make_async_copy(source, target, in_sems.at[index])
        for index, (source, target) in enumerate(
            (
                (heads_in, heads_ref),
                (q_in, q_ref),
                (k_in, k_ref),
                (v_in, v_ref),
                (w_in, w_ref),
                (tokens_in.at[t], tokens_ref),
            )
        )
    ]
    for copy in loaded:
        copy.start()

    few = fold_a.shape[1]

    def fold(which, source_ref, got_ref, target_ref):
        def loads(k, slot):
            mine = pltpu.make_async_copy(
                source_ref.at[span(x * reach + k * few, few)], fold_a.at[slot], fold_sems.at[0, slot]
            )
            theirs = [
                pltpu.make_async_copy(
                    got_ref.at[d, span(k * few, few)], fold_b.at[slot, d], fold_sems.at[1 + d, slot]
                )
                for d in range(copies - 1)
            ]
            return [mine] + theirs

        for copy in loads(0, 0):
            copy.start()
        steps = reach // few

        def step(k, carry):
            slot = k % 2
            for copy in loads(k, slot):
                copy.wait()

            @pl.when(k < steps - 1)
            def _():
                for copy in loads(k + 1, 1 - slot):
                    copy.start()

            total = fold_a[slot].astype(F32)
            for d in range(copies - 1):
                total += fold_b[slot, d].astype(F32)
            fold_send[which, span(k * few, few), :] = total.astype(BF16)
            return carry

        lax.fori_loop(0, steps, step, 0)
        return send(fold_send.at[which], target_ref, far)

    down_far = fold(0, down_ref, got_down_ref, down_far_ref)
    up_far = fold(1, up_ref, got_up_ref, up_far_ref)

    def grad_heads(s):
        at = span(s * share, share)
        grad = dot(ga_ref[s], w_out_ref[...], NT).astype(BF16).astype(F32)
        go_ref[at, :] = (grad * keep_ref[at, :]).astype(BF16)

    ga_own.wait()
    grad_heads(t)
    mixed_take.wait()
    mixed_own.start()
    ga_core.wait_recv()
    grad_heads(t ^ 1)
    ga_y.wait_recv()
    ga_y_core = send(ga_ref.at[t ^ 2], ga_ref.at[t ^ 2], core)
    grad_heads(t ^ 2)
    ga_y_core.wait_recv()
    grad_heads(t ^ 3)

    tile = tile_in.shape[-1]
    per = reach // tile

    def put_tile(slot, place, chunk, count):
        d, k = place
        return pltpu.make_async_copy(
            tile_out.at[slot, pl.ds(0, count)],
            leave_ref.at[d, pl.ds(chunk, count), span(k * tile, tile)],
            tile_out_sems.at[slot],
        )

    def store_tile(index, total, chunk, count):
        slot = index % 2
        d, k = index // per, index % per
        leaving = index < per * (copies - 1)

        @pl.when(leaving)
        def _():
            @pl.when(index >= 2)
            def _():
                put_tile(slot, ((index - 2) // per, (index - 2) % per), chunk, count).wait()

            for c in range(count):
                tile_out[slot, c] = total[:, c * own : (c + 1) * own].astype(BF16)
            put_tile(slot, (d, k), chunk, count).start()

        @pl.when(jnp.logical_not(leaving))
        def _():
            for c in range(count):
                kept_ref[chunk + c, span(k * tile, tile), :] = total[
                    :, c * own : (c + 1) * own
                ].astype(BF16)

    def tile_row(index):
        return lax.rem(x + 1 + index // per, copies) * per + index % per

    last = per * (copies - 1)

    def settle(chunk, count):
        for index in range(max(0, last - 2), last):
            put_tile(index % 2, (index // per, index % per), chunk, count).wait()
        return [
            [
                send(leave_ref.at[d - 1, chunk + c], got_x_ref.at[d - 1, chunk + c], twins[d - 1])
                for d in range(1, copies)
            ]
            for c in range(count)
        ]

    def out_tile(index, carry):
        lanes = span(tile_row(index) * tile, tile)
        left = ga_ref[:, :, lanes].reshape(rows, tile)
        store_tile(index, dot(left, heads_ref[...], TN), 0, 1)
        return carry

    loaded[0].wait()
    lax.fori_loop(0, last, out_tile, 0)
    crossing = settle(0, 1)
    lax.fori_loop(last, last + per, out_tile, 0)

    for copy in loaded[1:]:
        copy.wait()

    def turn_back(grad, at):
        grad = grad.astype(BF16).astype(F32)
        back = grad * cos_ref[at] - pltpu.roll(grad, HEAD_DIM // 2, 1) * sin_ref[at]
        return back.astype(BF16)

    for head in range(heads):
        lanes = slice(head * HEAD_DIM, (head + 1) * HEAD_DIM)
        for block in reversed(range(blocks)):
            length = (block + 1) * QBLOCK
            at = slice(block * QBLOCK, length)
            query, keys, grad = q_ref[at, lanes], k_ref[:length, lanes], go_ref[at, lanes]
            scores = masked_scores(query, keys, first_ref[at], block, length)
            probs = jnp.exp(scores - log_ref[at, head : head + 1])
            grad_probs = dot(grad, v_ref[:length, lanes], NT)
            inner = jnp.sum(probs * grad_probs, -1, keepdims=True)
            grad_scores = (probs * (grad_probs - inner)).astype(BF16)
            dq = dot(grad_scores, keys, NN) * HEAD_DIM**-0.5
            gp_ref[at, lanes] = turn_back(dq, at)
            dk = dot(grad_scores, query, TN)
            dv = dot(probs.astype(BF16), grad, TN)
            if block == blocks - 1:
                dk_ref[...] = dk
                dv_ref[...] = dv
            else:
                dk_ref[:length] += dk
                dv_ref[:length] += dv
        gp_ref[:, own + head * HEAD_DIM : own + (head + 1) * HEAD_DIM] = turn_back(
            dk_ref[...] * HEAD_DIM**-0.5, slice(None)
        )
        gp_ref[:, 2 * own + head * HEAD_DIM : 2 * own + (head + 1) * HEAD_DIM] = dv_ref[
            ...
        ].astype(BF16)

    ga_y.wait_send()
    ga_y_core.wait_send()

    def norm1_part(s):
        at = span(s * share, share)
        for lanes in (slice(0, width // 2), slice(width // 2, width)):
            total = dot(gp_ref[at, :own], w_ref[0, lanes, :], NT)
            total += dot(gp_ref[at, own : 2 * own], w_ref[1, lanes, :], NT)
            total += dot(gp_ref[at, 2 * own :], w_ref[2, lanes, :], NT)
            part_ref[:, lanes] = total

    norm1_part(t ^ 3)
    ga_ref[0] = part_ref[...].astype(BF16)
    core_pass = send(ga_ref.at[0], got_core_ref.at[0], core)
    norm1_part(t ^ 1)
    ga_ref[1] = part_ref[...].astype(BF16)
    core_own = send(ga_ref.at[1], got_core_ref.at[1], core)
    norm1_part(t ^ 2)
    core_pass.wait_recv()
    ga_ref[2] = (part_ref[...] + got_core_ref[0].astype(F32)).astype(BF16)
    y_own = send(ga_ref.at[2], got_y_ref, y_side)
    norm1_part(t)

    mixed_y.wait_recv()
    mixed_y_core = send(mixed_ref.at[t ^ 2], mixed_ref.at[t ^ 2], core)

    def fetch(index, slot):
        lanes = span(tile_row(index) * tile, tile)
        return pltpu.make_async_copy(n1_ref.at[:, lanes], tile_in.at[slot], tile_sems.at[slot])

    fetch(0, 0).start()

    def qkv_tile(index, carry):
        slot = index % 2
        fetch(index, slot).wait()

        @pl.when(index < last + per - 1)
        def _():
            fetch(index + 1, 1 - slot).start()

        store_tile(index, dot(tile_in[slot], gp_ref[...], TN), 1, 3)
        return carry

    lax.fori_loop(0, last, qkv_tile, 0)
    crossing += settle(1, 3)
    to_twins(down_own_ref, down_twin_ref)
    lax.fori_loop(last, last + per, qkv_tile, 0)

    def first_step(chunk):
        for copy in crossing[chunk]:
            copy.wait_recv()

        def total(index):
            at = span(index * part, part)
            value = kept_ref[chunk, at, :].astype(F32)
            for d in range(copies - 1):
                value += got_x_ref[d, chunk, at, :].astype(F32)
            return value

        z_send[chunk, 1] = total(z ^ 3).astype(BF16)
        one = send(z_send.at[chunk, 1], got_z1.at[chunk, 1], near)
        z_send[chunk, 0] = total(z ^ 1).astype(BF16)
        two = send(z_send.at[chunk, 0], got_z1.at[chunk, 0], near)
        z_kept[chunk] = total(z ^ 2)
        sums_ref[chunk] = total(z)
        return one, two

    def second_step(chunk, pair):
        one, two = pair
        one.wait_recv()
        one.wait_send()
        begun[:] = [copy for copy in begun if copy is not one]
        z_send[chunk, 1] = (z_kept[chunk] + got_z1[chunk, 1].astype(F32)).astype(BF16)
        gone = send(z_send.at[chunk, 1], got_z2.at[chunk], far)
        two.wait_recv()
        sums_ref[chunk] += got_z1[chunk, 0].astype(F32)
        return gone

    def third_step(chunk, gone):
        gone.wait_recv()
        sums_ref[chunk] += got_z2[chunk].astype(F32)

    mixed_own.wait()
    core_own.wait_recv()
    y_own.wait_recv()
    lines = 64
    count = small_in_ref.shape[0]
    small_ref[:count, :] = small_in_ref[...]
    small_ref[count:, :] = jnp.zeros((2, width), F32)

    def finish(j, carry):
        at = span(j * lines, lines)
        grad = part_ref[at, :] + got_core_ref[1, at, :].astype(F32) + got_y_ref[at, :].astype(F32)
        hat, inverse = norm_parts(tokens_ref[at, :].astype(F32))
        back, gain_grad, bias_grad = norm_backward(grad, hat, inverse, gain1_ref[...])
        tg_own_ref[at, :] = (gx2_ref[at, :] + back).astype(BF16)
        small_ref[count : count + 1, :] += gain_grad[None, :]
        small_ref[count + 1 : count + 2, :] += bias_grad[None, :]
        return carry

    lax.fori_loop(0, share // lines, finish, 0)
    tg_y = send(tg_own_ref, tg_ref.at[t], y_side)
    tg_core = send(tg_own_ref, tg_ref.at[t], core)
    tg_own = pltpu.make_async_copy(tg_own_ref, tg_ref.at[t], local_sems.at[2])
    tg_own.start()

    def small_step(step, devices):
        small_send[step] = small_ref[...]
        exchanged = [
            send(small_send.at[step], got_small.at[step + d], device)
            for d, device in enumerate(devices)
        ]
        for d, copy in enumerate(exchanged):
            copy.wait_recv()
            small_ref[...] += got_small[step + d]

    small_step(0, [core])
    pairs = {0: first_step(0)}
    gone = {0: second_step(0, pairs[0])}
    tg_y.wait_recv()
    tg_y_core = send(tg_ref.at[t ^ 2], tg_ref.at[t ^ 2], core)
    small_step(1, [y_side])
    for chunk in (1, 2, 3):
        pairs[chunk] = first_step(chunk)
        third_step(chunk - 1, gone[chunk - 1])
        if chunk == 3:
            small_step(4, twins)
        gone[chunk] = second_step(chunk, pairs[chunk])
    small_step(2, [near])
    third_step(3, gone[3])
    small_step(3, [far])
    for copy in (core_own, mixed_core, mixed_y_core, tg_core, tg_y_core, down_far, up_far, *twin_copies):
        if copy is not core_own:
            copy.wait_recv()
    tg_own.wait()
    for copy in begun:
        if copy is not ga_y and copy is not ga_y_core:
            copy.wait_send()


def back_call(
    queries, keys, values, heads, logs, first, keep, tables_, w_out, w3, gain1, tokens,
    grad_middle, small, grad_own, mixed_own, normed1, *level_grads,
):
    rows, own = queries.shape
    share, width = grad_own.shape
    copies, owners = lax.axis_size("dp"), lax.axis_size("bucket")
    splits = rows // share
    reach = width // copies
    part = reach // owners
    half = level_grads[0].shape[1]
    inside = pl.BlockSpec(memory_space=pltpu.VMEM)
    outside = pl.BlockSpec(memory_space=pl.ANY)
    shape = jax.ShapeDtypeStruct
    dma = lambda *count: pltpu.SemaphoreType.DMA(count)
    vmem = lambda dtype, *size: pltpu.VMEM(size, dtype)
    others = copies - 1
    totals = (small.shape[0] + 2, width)
    few = 256
    sends = 30 + 7 * others
    return pl.pallas_call(
        functools.partial(back_kernel, copies),
        in_specs=[inside] * 9 + [outside] * 15,
        out_specs=[inside] * 2 + [outside] * 7,
        out_shape=[
            shape((4, part, own), F32),
            shape(totals, F32),
            shape((splits, share, width), BF16),
            shape((splits, share, width), BF16),
            *[shape((reach, half), BF16)] * 2,
            *[shape((others, reach, half), BF16)] * 2,
            shape((others, 4, reach, own), BF16),
        ],
        scratch_shapes=[
            vmem(BF16, rows, own),
            vmem(BF16, rows, own),
            vmem(BF16, rows, own),
            vmem(BF16, rows, own),
            vmem(BF16, *w3.shape),
            vmem(BF16, share, width),
            vmem(BF16, splits, share, width),
            vmem(BF16, rows, own),
            vmem(BF16, rows, 3 * own),
            vmem(F32, rows, HEAD_DIM),
            vmem(F32, rows, HEAD_DIM),
            vmem(BF16, 2, share, width),
            vmem(BF16, share, width),
            vmem(F32, share, width),
            vmem(BF16, share, width),
            vmem(BF16, 2, rows, 256),
            vmem(BF16, 2, 3, 256, own),
            vmem(BF16, 2, few, half),
            vmem(BF16, 2, others, few, half),
            vmem(BF16, 2, reach, half),
            vmem(BF16, 4, reach, own),
            vmem(BF16, others, 4, reach, own),
            vmem(BF16, 4, 2, part, own),
            vmem(F32, 4, part, own),
            vmem(BF16, 4, 2, part, own),
            vmem(BF16, 4, part, own),
            vmem(F32, 4 + others, *totals),
            vmem(F32, 5, *totals),
            dma(sends),
            dma(sends),
            dma(4),
            dma(2),
            dma(2),
            dma(copies, 2),
            dma(6),
        ],
        compiler_params=pltpu.CompilerParams(
            vmem_limit_bytes=62 << 20, collective_id=2, has_side_effects=True
        ),
        cost_estimate=pl.CostEstimate(
            flops=16 * rows * width * own + 10 * rows * rows * own,
            bytes_accessed=80 << 20,
            transcendentals=rows * rows * own // HEAD_DIM,
        ),
        name="back",
    )(
        logs, first, keep, *tables_, w_out, gain1, grad_middle, small,
        tokens.reshape(splits, share, width), queries, keys, values, heads, w3, grad_own, mixed_own, normed1, *level_grads,
    )


def finish_kernel(tg_ref, mixed_ref, tg_out, mixed_out):
    tg_out[...] = tg_ref[...].astype(F32)
    mixed_out[...] = mixed_ref[...]


def finish_call(tokens_grad, mixed):
    rows, width = mixed.shape
    block = pl.BlockSpec((rows // 8, width), lambda i: (i, 0))
    return pl.pallas_call(
        finish_kernel,
        grid=(8,),
        in_specs=[block] * 2,
        out_specs=[block] * 2,
        out_shape=[
            jax.ShapeDtypeStruct((rows, width), F32),
            jax.ShapeDtypeStruct((rows, width), BF16),
        ],
        compiler_params=pltpu.CompilerParams(vmem_limit_bytes=62 << 20),
        cost_estimate=pl.CostEstimate(flops=0, bytes_accessed=10 * rows * width, transcendentals=0),
        name="finish",
    )(tokens_grad, mixed)


def local(
    tokens,
    cotangent,
    lengths,
    head_quarters,
    buckets,
    ln1_gain,
    ln1_bias,
    w_qkv,
    w_out,
    ln2_gain,
    ln2_bias,
    w_router,
    w_up,
    w_down,
):
    tok_rows, model_width = tokens.shape
    owners = lax.axis_size("bucket")
    splits = lax.axis_size("tensor")
    copies = lax.axis_size("dp")
    share = tok_rows // splits
    t, z, x = lax.axis_index("tensor"), lax.axis_index("bucket"), lax.axis_index("dp")
    up_own = w_up.reshape(model_width, -1)
    down_own = w_down.reshape(-1, model_width)
    hidden_width = up_own.shape[1]

    levels = buckets[:, 0].astype(F32).reshape(-1, HEAD_DIM)

    first = layout(lengths[0], tok_rows)[:, None]
    keep = (t < head_quarters).astype(F32)[:, None]
    w3 = jnp.transpose(w_qkv, (1, 0, 2))
    (
        logs,
        middle,
        cosine,
        sine,
        normed1,
        queries,
        keys,
        values,
        heads_low,
        n2,
        up_other,
        down_other,
        near_cotangent,
        near_levels,
    ) = front_call(
        tokens,
        (ln1_gain.reshape(1, -1), ln1_bias.reshape(1, -1)),
        w3,
        first,
        keep,
        w_out,
        (ln2_gain.reshape(1, -1), ln2_bias.reshape(1, -1)),
        up_own,
        down_own,
        cotangent.reshape(splits, share, model_width),
        levels,
    )
    level_all = jnp.concatenate([levels.reshape(-1), near_levels.reshape(-1)], 0)[:, None]
    (
        mixed_own,
        grad_middle,
        grad_attention_own,
        small,
        _,
        _,
        down_own,
        down_other,
        up_own,
        up_other,
        got_down,
        got_up,
    ) = middle_call(
        n2,
        cotangent,
        near_cotangent,
        (up_own, up_other),
        (down_own, down_other),
        w_router,
        level_all,
        middle,
        (ln2_gain.reshape(1, -1), ln2_bias.reshape(1, -1)),
    )
    sums, small, mixed, tokens_grad, down_far, up_far, down_twin, up_twin, _ = back_call(
        queries,
        keys,
        values,
        heads_low,
        logs,
        first,
        keep,
        (cosine, sine),
        w_out,
        w3,
        ln1_gain.reshape(1, -1),
        tokens,
        grad_middle,
        small,
        grad_attention_own,
        mixed_own,
        normed1,
        down_other,
        got_down,
        up_other,
        got_up,
        down_own,
        up_own,
    )
    size = model_width // copies

    def level_grad(own, twin, distant):
        mine = lax.dynamic_slice_in_dim(own, x * size, size, 0).astype(F32)
        return mine + jnp.sum(twin.astype(F32), 0) + distant.astype(F32)

    grad_down = level_grad(down_own, down_twin, down_far).T
    grad_up = level_grad(up_own, up_twin, up_far)
    tokens_grad, mixed = finish_call(
        tokens_grad.reshape(tok_rows, model_width), mixed.reshape(tok_rows, model_width)
    )
    width = model_width // (copies * owners)
    small = lax.dynamic_slice_in_dim(small, (x * owners + z) * width, width, 1)
    return (
        mixed,
        tokens_grad,
        small[2 + owners],
        small[3 + owners],
        jnp.transpose(sums[1:], (1, 0, 2)),
        sums[0].T,
        small[0],
        small[1],
        small[2 : 2 + owners].T,
        grad_up.reshape(-1, 1, hidden_width),
        grad_down.reshape(1, hidden_width, -1),
    )


def solution(mesh):
    placed = (
        P(("dp", "bucket"), None),
        P(("dp", "bucket"), None),
        P(("dp", "bucket"), None),
        P(("dp", "bucket")),
        P(("dp", "bucket"), None),
        P(),
        P(),
        P(None, None, "tensor"),
        P("tensor", None),
        P(),
        P(),
        P(),
        P(None, "bucket", "tensor"),
        P("bucket", "tensor", None),
    )
    return jax.shard_map(
        local,
        mesh=mesh,
        in_specs=placed,
        out_specs=(
            P(("dp", "bucket"), None),
            P(("dp", "bucket"), None),
            P(("dp", "bucket")),
            P(("dp", "bucket")),
            P(("dp", "bucket"), None, "tensor"),
            P("tensor", ("dp", "bucket")),
            P(("dp", "bucket")),
            P(("dp", "bucket")),
            P(("dp", "bucket"), None),
            P("dp", "bucket", "tensor"),
            P("bucket", "tensor", "dp"),
        ),
        check_vma=False,
    )
```
